32 devices in a mesh: replica: 4 (over x, core), shard: 8 (over z, y).
Axes of the slice: x: 2, y: 2, z: 4, core: 2. Of those that a mesh axis runs over, the one named last changes fastest.
Arguments:
- hidden_in: bfloat16 [8192, 2048], P(('replica', 'shard')), may hold values from -6 to 6
- out_grad: bfloat16 [8192, 2048], P(('replica', 'shard')), may hold values from -6 to 6
- routes: int32 [8192, 6], P(('replica', 'shard')), may hold values from 0 to 15, all different within a row; in each aligned block of 256 rows (0 to 255, 256 to 511, ...) at most 128 rows name the same one
- seq_adapter: int32 [4], P('replica'), may hold values from 0 to 7
- attn_gain: float32 [2048], replicated, may hold values from 0.5 to 1.5
- latent_gain: float32 [512], replicated, may hold values from 0.5 to 1.5
- ffn_gain: float32 [2048], replicated, may hold values from 0.5 to 1.5
- w_qa: bfloat16 [2048, 3648], P('shard'), may hold values from -0.125 to 0.125
- w_kvb: bfloat16 [512, 4096], P('shard'), may hold values from -0.25 to 0.25
- w_out: bfloat16 [2048, 2048], P('shard'), may hold values from -2 to 2
- w_router: bfloat16 [2048, 16], replicated, may hold values from -0.0625 to 0.0625
- w_shared_in: bfloat16 [2048, 5632], P('shard'), may hold values from -0.125 to 0.125
- w_shared_out: bfloat16 [2816, 2048], P('shard'), may hold values from -0.109375 to 0.109375
- w_expert_in: bfloat16 [16, 2048, 2816], P('shard'), may hold values from -0.125 to 0.125
- w_expert_out: bfloat16 [16, 1408, 2048], P('shard'), may hold values from -1 to 1
- qa_down: bfloat16 [8, 16, 2048], P('shard'), may hold values from -0.125 to 0.125
- qa_up: bfloat16 [8, 16, 3648], P('shard'), may hold values from -0.4375 to 0.4375
- kvb_down: bfloat16 [8, 16, 512], P('shard'), may hold values from -0.25 to 0.25
- kvb_up: bfloat16 [8, 16, 4096], P('shard'), may hold values from -0.4375 to 0.4375
- out_down: bfloat16 [8, 16, 2048], P('shard'), may hold values from -2 to 2
- out_up: bfloat16 [8, 16, 2048], P('shard'), may hold values from -0.75 to 0.75
- gu_down: bfloat16 [8, 16, 2048], P('shard'), may hold values from -0.125 to 0.125
- gu_up: bfloat16 [8, 16, 5632], P('shard'), may hold values from -0.4375 to 0.4375
- dn_down: bfloat16 [8, 16, 2816], P('shard'), may hold values from -0.109375 to 0.109375
- dn_up: bfloat16 [8, 16, 2048], P('shard'), may hold values from -0.4375 to 0.4375
Outputs:
- block_out: bfloat16 [8192, 2048], P(('replica', 'shard'))
- hidden_grad: float32 [8192, 2048], P(('replica', 'shard'))
- qa_down_grad: float32 [8, 16, 2048], P('shard')
- qa_up_grad: float32 [8, 16, 3648], P('shard')
- kvb_down_grad: float32 [8, 16, 512], P('shard')
- kvb_up_grad: float32 [8, 16, 4096], P('shard')
- out_down_grad: float32 [8, 16, 2048], P('shard')
- out_up_grad: float32 [8, 16, 2048], P('shard')
- gu_down_grad: float32 [8, 16, 2048], P('shard')
- gu_up_grad: float32 [8, 16, 5632], P('shard')
- dn_down_grad: float32 [8, 16, 2816], P('shard')
- dn_up_grad: float32 [8, 16, 2048], P('shard')
The draws below stay inside these ranges and needn't reach their ends.
Inputs may be any that keep to these rules, and one draw needn't show every extreme that they name: `routes`: each row names 6 different experts; in each aligned block of 256 rows (the rows of one device) no expert is named by more than 128 rows.
All inputs are finite; a program needn't handle non-finite values.
Results may differ from the reference program's by a relative error of at most 0.025.
Values may be sent and summed in bfloat16 or wider, within the bound.
No kernel may reach another device: no remote copies, remote signals or barrier semaphores. Data moves between devices by JAX's collectives and lax.ppermute only.
A program may use at most 384 MiB of HBM per device.

```python
import math
import jax
import jax.numpy as jnp
import numpy as np
from jax import lax

D = 2048
HEADS = 16
NOPE = 128
ROPE = 64
VDIM = 128
LATENT = 512
MOE_FF = 1408
SHARED_FF = 2816
TOPK = 6
RANK = 16
ADAPTERS = 8
BLOCK = 256
TOK_DEV = 256
SEQ = 2048
SEQS = 4
TOKENS = 8192
EXPERTS = 16
CAP = 128
QKVA = 3648
KVB = 4096


def set_ends(values, rng, low, high):
    dims = values.shape
    index_at = [jax.random.randint(jax.random.fold_in(rng, axis), (), 0, dims[axis]) for axis in range(len(dims))]
    values = values.at[tuple(index_at)].set(low)
    longest = dims.index(max(dims))
    index_at[longest] = (index_at[longest] + 1) % dims[longest]
    return values.at[tuple(index_at)].set(high)


def level_of(rng, extent, cuts, low, largest):
    def one(position, blocks):
        heights = jax.random.uniform(jax.random.fold_in(jax.random.fold_in(rng, 6), position), (blocks,), jnp.float32, low / len(cuts), largest / len(cuts))
        return jnp.repeat(jnp.exp(heights), extent[position] // blocks).reshape((-1,) + (1,) * (len(extent) - position - 1))

    loudness = one(*cuts[0])
    for cut in cuts[1:]:
        loudness = loudness * one(*cut)
    return loudness


def deal_out(own_key, own, number, rows, count, top, limit, slope):
    ranking = jax.random.permutation(own_key, count)
    heavy_load, common = shares(count, rows * top, limit, slope, True), shares(count, rows * top, limit, slope, False)
    places = jnp.arange(count)

    def named(lengths, offset_by):
        used = int((lengths > 0).sum())
        fixed = max(1, used // 4)
        moved = fixed + (places - fixed + offset_by * (used - fixed)) % max(1, count - fixed)
        return jnp.zeros((count,), jnp.int32).at[ranking[jnp.where(places < fixed, places, moved)]].set(jnp.asarray(lengths, jnp.int32))

    lengths = jnp.where(number % 4 == 0, named(heavy_load, number // 4), named(common, number - number // 4 - 1))
    mixed = jax.random.permutation(jax.random.fold_in(own, 3), count)
    donor, taker = mixed[0:count // 2 * 2:2], mixed[1:count // 2 * 2:2]
    slack = jnp.minimum(lengths[donor] - 1, limit - lengths[taker]) // 2
    slack = jnp.where((donor == ranking[0]) | (taker == ranking[0]) | (lengths[taker] == 0), 0, jnp.maximum(slack, 0))
    moved = jax.random.randint(jax.random.fold_in(own, 4), (count // 2,), 0, 1 << 20) % (slack + 1)
    lengths = lengths.at[donor].add(-moved).at[taker].add(moved)
    labels = jnp.searchsorted(jnp.cumsum(lengths), jnp.arange(rows * top), side="right").astype(jnp.int32)
    table = labels.reshape(top, rows).T
    table = table[jax.random.permutation(jax.random.fold_in(own, 1), rows)]
    offset_by = jax.random.randint(jax.random.fold_in(own, 2), (rows, 1), 0, top)
    return jnp.take_along_axis(table, (jnp.arange(top)[None, :] + offset_by) % top, axis=1)


def shares(number_of, total, reach, slope, full):
    weights = [(1 << 20) // math.isqrt(rank ** slope) + 1 for rank in range(1, number_of + 1)]
    largest = reach if full else min(reach, max(-(-total // number_of), total * weights[0] // sum(weights)))
    least = 1 if total - largest >= number_of - 1 else 0
    counts, surplus = [largest] + [least] * (number_of - 1), total - largest - least * (number_of - 1)
    while surplus > 0:
        movable = [i for i in range(1, number_of) if counts[i] < largest] or [i for i in range(1, number_of) if counts[i] < reach]
        pool, remaining = sum([weights[i] for i in movable]), surplus
        for i in movable:
            extra = min(reach - counts[i], max(1, remaining * weights[i] // pool), surplus)
            counts[i] = counts[i] + extra
            surplus = surplus - extra
    return np.array(counts)


def gaussian(rng, shape, width, reach, split=(), kind=jnp.bfloat16):
    values = width * jax.random.normal(rng, shape, jnp.float32)
    if split:
        values = values * level_of(rng, shape, split, -0.22, 0.18)
    return jnp.clip(values, -reach, reach).astype(kind)


def setup_inputs(seed: int = 0) -> dict:
    key_of = jax.random.split(jax.random.key(seed), 26)
    hidden_in = gaussian(key_of[0], (TOKENS, D), 1.0, 6.0, ((0, 32),))
    out_grad = gaussian(key_of[1], (TOKENS, D), 1.0, 6.0, ((0, 32),))
    routes_keys = jax.random.split(jax.random.fold_in(key_of[2], 1), TOKENS // TOK_DEV)
    routes_turns = jax.random.permutation(jax.random.fold_in(key_of[2], 3), TOKENS // TOK_DEV)
    routes = jax.vmap(lambda own, number: deal_out(jax.random.fold_in(key_of[2], 2), own, number, TOK_DEV, EXPERTS, TOPK, CAP, 0))(routes_keys, routes_turns).reshape((TOKENS, TOPK))
    seq_adapter = set_ends(jax.random.randint(key_of[3], (SEQS,), 0, ADAPTERS), jax.random.fold_in(key_of[3], 1), 0, ADAPTERS - 1).astype(jnp.int32)
    attn_gain = jnp.clip(1.0 + 0.1 * jax.random.normal(key_of[4], (D,), jnp.float32), 0.5, 1.5)
    latent_gain = jnp.clip(1.0 + 0.1 * jax.random.normal(key_of[5], (LATENT,), jnp.float32), 0.5, 1.5)
    ffn_gain = jnp.clip(1.0 + 0.1 * jax.random.normal(key_of[6], (D,), jnp.float32), 0.5, 1.5)
    w_qa = gaussian(key_of[7], (D, QKVA), D ** -0.5, 0.125, ((0, 8),))
    w_kvb = gaussian(key_of[8], (LATENT, KVB), LATENT ** -0.5, 0.25, ((0, 8),))
    w_out = gaussian(key_of[9], (HEADS * VDIM, D), (max(D // 256, 2)) ** -0.5, 2.0, ((0, 8),))
    w_router = gaussian(key_of[10], (D, EXPERTS), (4 * D) ** -0.5, 0.0625)
    w_shared_in = gaussian(key_of[11], (D, 2 * SHARED_FF), D ** -0.5, 0.125, ((0, 8),))
    w_shared_out = gaussian(key_of[12], (SHARED_FF, D), SHARED_FF ** -0.5, 0.109375, ((0, 8),))
    w_expert_in = gaussian(key_of[13], (EXPERTS, D, 2 * MOE_FF), D ** -0.5, 0.125, ((0, 8),))
    w_expert_out = gaussian(key_of[14], (EXPERTS, MOE_FF, D), (max(MOE_FF // 48, 1)) ** -0.5, 1.0, ((0, 8),))
    qa_down = gaussian(key_of[15], (ADAPTERS, RANK, D), D ** -0.5, 0.125, ((0, 8),))
    qa_up = gaussian(key_of[16], (ADAPTERS, RANK, QKVA), (RANK * 12) ** -0.5, 0.4375, ((0, 8),))
    kvb_down = gaussian(key_of[17], (ADAPTERS, RANK, LATENT), LATENT ** -0.5, 0.25, ((0, 8),))
    kvb_up = gaussian(key_of[18], (ADAPTERS, RANK, KVB), (RANK * 12) ** -0.5, 0.4375, ((0, 8),))
    out_down = gaussian(key_of[19], (ADAPTERS, RANK, HEADS * VDIM), (max(D // 256, 2)) ** -0.5, 2.0, ((0, 8),))
    out_up = gaussian(key_of[20], (ADAPTERS, RANK, D), (RANK * 4) ** -0.5, 0.75, ((0, 8),))
    gu_down = gaussian(key_of[21], (ADAPTERS, RANK, D), D ** -0.5, 0.125, ((0, 8),))
    gu_up = gaussian(key_of[22], (ADAPTERS, RANK, 2 * SHARED_FF), (RANK * 12) ** -0.5, 0.4375, ((0, 8),))
    dn_down = gaussian(key_of[23], (ADAPTERS, RANK, SHARED_FF), SHARED_FF ** -0.5, 0.109375, ((0, 8),))
    dn_up = gaussian(key_of[24], (ADAPTERS, RANK, D), (RANK * 12) ** -0.5, 0.4375, ((0, 8),))
    return dict(hidden_in=hidden_in, out_grad=out_grad, routes=routes, seq_adapter=seq_adapter, attn_gain=attn_gain, latent_gain=latent_gain, ffn_gain=ffn_gain, w_qa=w_qa, w_kvb=w_kvb, w_out=w_out, w_router=w_router, w_shared_in=w_shared_in, w_shared_out=w_shared_out, w_expert_in=w_expert_in, w_expert_out=w_expert_out, qa_down=qa_down, qa_up=qa_up, kvb_down=kvb_down, kvb_up=kvb_up, out_down=out_down, out_up=out_up, gu_down=gu_down, gu_up=gu_up, dn_down=dn_down, dn_up=dn_up)


@jax.custom_vjp
def low(v):
    return lax.optimization_barrier(v.astype(jnp.bfloat16)).astype(jnp.float32)

@jax.custom_vjp
def low_back(v):
    return v

def low_keep(v):
    return (low(v), None)

def low_pass(kept, grad):
    return (grad,)

def back_keep(v):
    return (v, None)

def back_low(kept, grad):
    return (low(grad),)
low.defvjp(low_keep, low_pass)
low_back.defvjp(back_keep, back_low)
epsilon = 1e-06
highest = lax.Precision.HIGHEST

def rounded(value):
    return low_back(low(value))

def matmul(left, right):
    return jnp.dot(left, right, precision=highest)

def rms_norm(value, gain):
    return value * lax.rsqrt(lax.optimization_barrier(jnp.mean(value * value, axis=-1, keepdims=True)) + epsilon) * gain

def rotary(value, positions):
    width_half = value.shape[-1] // 2
    ladder = jnp.arange(width_half).astype(jnp.float32)
    frequency = jnp.exp(ladder * (-2.0 * math.log(10000.0) / value.shape[-1]))
    angles = positions.astype(jnp.float32)[:, None] * frequency[None, :]
    cosine = jnp.cos(angles)
    sine_part = jnp.sin(angles)
    if value.ndim == 3:
        cosine = cosine[:, None, :]
        sine_part = sine_part[:, None, :]
    leading = value[..., :width_half]
    second = value[..., width_half:]
    return jnp.concatenate([leading * cosine - second * sine_part, second * cosine + leading * sine_part], axis=-1)

def adapted(source, weight, down, upward):
    narrow = rounded(matmul(source, down.T))
    return matmul(source, weight) + matmul(narrow, upward)

def attend(queries, query_pos, latent, key_rope, kvb_weight, kvb_down, kvb_up):
    length = latent.shape[0]
    joined = rounded(adapted(latent, kvb_weight, kvb_down, kvb_up)).reshape(length, HEADS, NOPE + VDIM)
    scaling = (NOPE + ROPE) ** (-0.5)
    scores = jnp.einsum('qhc,khc->hqk', queries[:, :, :NOPE], joined[:, :, :NOPE], precision=highest)
    scores = scores + jnp.einsum('qhr,kr->hqk', queries[:, :, NOPE:], key_rope, precision=highest)
    scores = low_back(scores * scaling)
    key_pos = jnp.arange(length)
    allowed = key_pos[None, :] // BLOCK <= query_pos[:, None] // BLOCK
    scores = jnp.where(allowed[None, :, :], scores, -1e+30)
    attention = rounded(jax.nn.softmax(scores, axis=-1))
    mixture = jnp.einsum('hqk,khv->qhv', attention, joined[:, :, NOPE:], precision=highest)
    return rounded(mixture.reshape(queries.shape[0], HEADS * VDIM))

def forward_sequence(inputs, adapter_id, adapters, weights, gain_set, route_rows):
    w_qa, w_kvb, w_out, w_router, w_shared_in, w_shared_out, w_expert_in, w_expert_out = weights
    picked = [lax.dynamic_index_in_dim(table, adapter_id, 0, keepdims=False) for table in adapters]
    length = inputs.shape[0]
    positions = jnp.arange(length)
    normed = rounded(rms_norm(inputs, gain_set[0]))
    projected = adapted(normed, w_qa, picked[0], picked[1])
    query_width = HEADS * (NOPE + ROPE)
    heads_raw = projected[:, :query_width].reshape(length, HEADS, NOPE + ROPE)
    queries = rounded(jnp.concatenate([heads_raw[:, :, :NOPE], rotary(heads_raw[:, :, NOPE:], positions)], axis=-1))
    latent = rounded(rms_norm(projected[:, query_width:query_width + LATENT], gain_set[1]))
    key_rope = rounded(rotary(projected[:, query_width + LATENT:], positions))
    groups = length // TOK_DEV

    def one_group(pieces):
        return attend(pieces[0], pieces[1], latent, key_rope, w_kvb, picked[2], picked[3])
    mixture = lax.map(jax.checkpoint(one_group), (queries.reshape(groups, TOK_DEV, HEADS, NOPE + ROPE), positions.reshape(groups, TOK_DEV)))
    mixture = mixture.reshape(length, HEADS * VDIM)
    after_attn = inputs + adapted(mixture, w_out, picked[4], picked[5])
    ffn_in = rms_norm(after_attn, gain_set[2])
    ffn_low = rounded(ffn_in)
    router = jax.nn.softmax(matmul(ffn_low, w_router), axis=-1)
    gate_up = low_back(adapted(ffn_low, w_shared_in, picked[6], picked[7]))
    inner_act = rounded(jax.nn.silu(gate_up[:, :SHARED_FF]) * gate_up[:, SHARED_FF:])
    partial_out = after_attn + adapted(inner_act, w_shared_out, picked[8], picked[9])

    def one_expert(running, element):
        expert, w_first, w_down = element
        chosen = lax.optimization_barrier(jnp.sum((route_rows == expert).astype(jnp.float32), axis=1)) * lax.dynamic_index_in_dim(router, expert, 1, keepdims=False)
        sent_rows = rounded(ffn_in)
        expert_act = low_back(matmul(sent_rows, w_first))
        hidden_act = rounded(jax.nn.silu(expert_act[:, :MOE_FF]) * expert_act[:, MOE_FF:])
        result = rounded(matmul(hidden_act, w_down))
        return (running + chosen[:, None] * result, None)
    routed, unused = lax.scan(jax.checkpoint(one_expert), jnp.zeros((length, D), jnp.float32), (jnp.arange(EXPERTS).astype(jnp.int32), w_expert_in, w_expert_out))
    return partial_out + routed

def reference(hidden_in, out_grad, routes, seq_adapter, attn_gain, latent_gain, ffn_gain, w_qa, w_kvb, w_out, w_router, w_shared_in, w_shared_out, w_expert_in, w_expert_out, qa_down, qa_up, kvb_down, kvb_up, out_down, out_up, gu_down, gu_up, dn_down, dn_up):
    weights = tuple((matrix.astype(jnp.float32) for matrix in (w_qa, w_kvb, w_out, w_router, w_shared_in, w_shared_out, w_expert_in, w_expert_out)))
    gain_set = (attn_gain.astype(jnp.float32), latent_gain.astype(jnp.float32), ffn_gain.astype(jnp.float32))
    adapters = tuple((matrix.astype(jnp.float32) for matrix in (qa_down, qa_up, kvb_down, kvb_up, out_down, out_up, gu_down, gu_up, dn_down, dn_up)))
    inputs = hidden_in.astype(jnp.float32).reshape(SEQS, SEQ, D)
    route_seq = routes.reshape(SEQS, SEQ, TOPK)

    def layer_all(inputs, adapters):

        def step_one(carry, element):
            return (carry, forward_sequence(element[0], element[1], adapters, weights, gain_set, element[2]))
        unused, outputs = lax.scan(step_one, jnp.zeros((), jnp.float32), (inputs, seq_adapter, route_seq))
        return outputs
    outputs, pullback = jax.vjp(layer_all, inputs, adapters)
    input_grad, adapter_grads = pullback(out_grad.astype(jnp.float32).reshape(SEQS, SEQ, D))
    return (outputs.reshape(TOKENS, D).astype(jnp.bfloat16), input_grad.reshape(TOKENS, D), adapter_grads[0], adapter_grads[1], adapter_grads[2], adapter_grads[3], adapter_grads[4], adapter_grads[5], adapter_grads[6], adapter_grads[7], adapter_grads[8], adapter_grads[9])
```

```python
import functools
import math

import jax
import jax.numpy as jnp
from jax import lax
from jax.experimental import pallas as pl
from jax.experimental.pallas import tpu as pltpu
from jax.sharding import PartitionSpec as P

D = 2048
HEADS = 16
NOPE = 128
ROPE = 64
VDIM = 128
LATENT = 512
TOPK = 6
RANK = 16
ADAPTERS = 8
BLOCK = 256
QW = HEADS * (NOPE + ROPE)
LW = LATENT + 2 * ROPE
LANES = 128
VMEM_LIMIT = 60 * 1024 * 1024
SCALE = (NOPE + ROPE) ** (-0.5)
EPS = 1e-06
f32 = jnp.float32
bf16 = jnp.bfloat16

NN = (((1,), (0,)), ((), ()))
NT = (((1,), (1,)), ((), ()))
TN = (((0,), (0,)), ((), ()))


def dot(a, b, dims=NN):
    return lax.dot_general(a, b, dims, preferred_element_type=f32)


def params(n):
    return pltpu.CompilerParams(
        dimension_semantics=("arbitrary",) * n, vmem_limit_bytes=VMEM_LIMIT
    )


def cost(flops, nbytes):
    return pl.CostEstimate(flops=int(flops), bytes_accessed=int(nbytes), transcendentals=0)


def ring_of(count):
    return list(range(0, count, 2)) + list(range(count - 1, 0, -2))


class Ring:
    def __init__(self, count):
        order = ring_of(count)
        place_of = [order.index(i) for i in range(count)]
        self.count = count
        self.order = jnp.asarray(order, jnp.int32)
        self.pos = jnp.asarray(place_of, jnp.int32)[lax.axis_index("shard")]
        self.right = [(order[i], order[(i + 1) % count]) for i in range(count)]
        self.left = [(order[i], order[(i - 1) % count]) for i in range(count)]

    def owner(self, off):
        return self.order[(self.pos + off) % self.count]

    def send_right(self, v):
        return lax.ppermute(v, "shard", self.right)

    def send_left(self, v):
        return lax.ppermute(v, "shard", self.left)

    def gather(self, v, halves=True):
        half = self.count // 2
        steps = [[(0, v)]]
        if halves:
            n = v.shape[0] // 2
            a, b = v[:n], v[n:]
            ra, rb, la, lb = a, b, a, b
            for h in range(1, half + 1):
                ra = self.send_right(ra)
                lb = self.send_left(lb)
                if h < half:
                    rb = self.send_right(rb)
                    la = self.send_left(la)
                    steps.append(
                        [(-h, jnp.concatenate([ra, rb], 0)), (h, jnp.concatenate([la, lb], 0))]
                    )
                else:
                    steps.append([(h, jnp.concatenate([ra, lb], 0))])
        else:
            r, l = v, v
            for h in range(1, half + 1):
                r = self.send_right(r)
                if h < half:
                    l = self.send_left(l)
                    steps.append([(-h, r), (h, l)])
                else:
                    steps.append([(h, r)])
        return steps

    def gather_rows(self, v, halves=True):
        n = v.shape[0]
        out = jnp.zeros((self.count * n,) + v.shape[1:], v.dtype)
        for step in self.gather(v, halves):
            for off, block in step:
                at = (self.owner(off) * n,) + (0,) * (v.ndim - 1)
                out = lax.dynamic_update_slice(out, block, at)
        return out

    def scatter_sum(self, piece):
        half = self.count // 2
        ra = rb = la = lb = None
        for h in range(half, 0, -1):
            up, down = piece(h), piece(-h)
            n = up.shape[0] // 2
            if h == half:
                sa, sb = up[:n], up[n:]
                sa, sb = sa.astype(bf16), sb.astype(bf16)
                ra = self.send_right(sa)
                lb = self.send_left(sb)
            else:
                sra = (up[:n].astype(f32) + ra.astype(f32)).astype(bf16)
                slb = (down[n:].astype(f32) + lb.astype(f32)).astype(bf16)
                srb, sla = up[n:], down[:n]
                if rb is not None:
                    srb = srb.astype(f32) + rb.astype(f32)
                    sla = sla.astype(f32) + la.astype(f32)
                ra = self.send_right(sra)
                lb = self.send_left(slb)
                rb = self.send_right(srb.astype(bf16))
                la = self.send_left(sla.astype(bf16))
        own = piece(0)
        n = own.shape[0] // 2
        top = own[:n].astype(f32) + ra.astype(f32) + la.astype(f32)
        low = own[n:].astype(f32) + rb.astype(f32) + lb.astype(f32)
        return jnp.concatenate([top, low], 0)


def pair_swap(v, replicas):
    return lax.ppermute(v, "replica", [(i, i ^ 1) for i in range(replicas)])


def shared_rows(ring, w, replicas):
    if replicas % 2:
        return ring.gather_rows(w, False)
    n = w.shape[0]
    half = n // 2
    core = lax.axis_index("replica") % 2
    mine = lax.dynamic_slice_in_dim(w, core * half, half, 0)
    blocks = ring.gather_rows(mine, False)
    other = pair_swap(blocks, replicas)
    blocks = blocks.reshape(ring.count, half, w.shape[1])
    other = other.reshape(ring.count, half, w.shape[1])
    first = jnp.where(core == 0, blocks, other)
    second = jnp.where(core == 0, other, blocks)
    return jnp.concatenate([first, second], 1).reshape(ring.count * n, w.shape[1])


def rotate_pair(lane, v):
    half = ROPE // 2
    return jnp.where(lane < half, -pltpu.roll(v, LANES - half, 1), pltpu.roll(v, half, 1))


def unrotate_pair(lane, v):
    half = ROPE // 2
    return jnp.where(lane < half, pltpu.roll(v, LANES - half, 1), -pltpu.roll(v, half, 1))


def query_kernel(hb_ref, r_ref, w_ref, up_ref, cos_ref, sin_ref, q_ref, qt_ref):
    acc = dot(hb_ref[...], w_ref[...]) + dot(r_ref[...], up_ref[...])
    lane = lax.broadcasted_iota(jnp.int32, (acc.shape[0], LANES), 1)
    for i in range(2):
        own = acc if i == 0 else pltpu.roll(acc, NOPE + ROPE, 1)
        rope = own[:, LANES : 2 * LANES]
        turned = rope * cos_ref[...] + rotate_pair(lane, rope) * sin_ref[...]
        head = jnp.concatenate([own[:, :LANES], turned], 1)
        q_ref[i] = head.astype(bf16)
        qt_ref[i] = head.T.astype(bf16)


def query_heads(hb, r, w_q, up, cos, sin):
    tokens = hb.shape[0]
    pairs = HEADS // 2
    width = 2 * (NOPE + ROPE)
    whole = lambda a: pl.BlockSpec(a.shape, lambda i: (0,) * a.ndim)
    shape = jax.ShapeDtypeStruct((HEADS, tokens, 2 * LANES), bf16)
    shape_t = jax.ShapeDtypeStruct((HEADS, 2 * LANES, tokens), bf16)
    return pl.pallas_call(
        query_kernel,
        grid=(pairs,),
        in_specs=[
            whole(hb),
            whole(r),
            pl.BlockSpec((D, width), lambda i: (0, i)),
            pl.BlockSpec((LANES, width), lambda i: (0, i)),
            whole(cos),
            whole(sin),
        ],
        out_specs=[
            pl.BlockSpec((2, tokens, 2 * LANES), lambda i: (i, 0, 0)),
            pl.BlockSpec((2, 2 * LANES, tokens), lambda i: (i, 0, 0)),
        ],
        out_shape=[shape, shape_t],
        compiler_params=params(1),
        cost_estimate=cost(2 * tokens * D * QW, D * QW * 2),
        name="query_heads",
    )(hb, r, w_q, up, cos, sin)


def query_back_kernel(dq_ref, w_ref, up_ref, rt_ref, dhb_ref, dr_ref, dup_ref, acc, racc):
    i = pl.program_id(0)
    tokens = dq_ref.shape[1]

    @pl.when(i == 0)
    def _():
        acc[...] = jnp.zeros_like(acc)
        racc[...] = jnp.zeros_like(racc)

    pad = jnp.zeros((tokens, LANES), f32)
    first = jnp.concatenate([dq_ref[0].astype(f32), pad], 1)
    second = jnp.concatenate([dq_ref[1].astype(f32), pad], 1)
    both = (first + pltpu.roll(second, NOPE + ROPE, 1)).astype(bf16)
    acc[...] += dot(both, w_ref[...], NT)
    racc[...] += dot(both, up_ref[...], NT)
    dup_ref[...] = dot(rt_ref[...], both)

    @pl.when(i == pl.num_programs(0) - 1)
    def _():
        dhb_ref[...] = acc[...]
        dr_ref[...] = racc[...]


def query_back(dq, w_q, up, rt):
    tokens = dq.shape[1]
    width = 2 * (NOPE + ROPE)
    return pl.pallas_call(
        query_back_kernel,
        grid=(HEADS // 2,),
        in_specs=[
            pl.BlockSpec((2, tokens, 2 * LANES), lambda i: (i, 0, 0)),
            pl.BlockSpec((D, width), lambda i: (0, i)),
            pl.BlockSpec((LANES, width), lambda i: (0, i)),
            pl.BlockSpec(rt.shape, lambda i: (0, 0)),
        ],
        out_specs=[
            pl.BlockSpec((tokens, D), lambda i: (0, 0)),
            pl.BlockSpec((tokens, LANES), lambda i: (0, 0)),
            pl.BlockSpec((LANES, width), lambda i: (0, i)),
        ],
        out_shape=[
            jax.ShapeDtypeStruct((tokens, D), f32),
            jax.ShapeDtypeStruct((tokens, LANES), f32),
            jax.ShapeDtypeStruct((LANES, QW), f32),
        ],
        scratch_shapes=[pltpu.VMEM((tokens, D), f32), pltpu.VMEM((tokens, LANES), f32)],
        compiler_params=params(1),
        cost_estimate=cost(2 * tokens * D * QW, D * QW * 2),
        name="query_back",
    )(dq, w_q, up, rt)


def keys_and_values(l_ref, w_ref, u_ref):
    kv = dot(l_ref[:, :LATENT], w_ref[...]) + dot(l_ref[:, LATENT:], u_ref[...])
    kv = kv.astype(bf16)
    keys = jnp.concatenate([kv[:, :NOPE], l_ref[:, LATENT:]], 1)
    return keys, kv[:, NOPE:]


def masked_scores(limit_ref, keys, qt):
    scores = dot(keys, qt) * SCALE
    row = lax.broadcasted_iota(jnp.int32, scores.shape, 0)
    return jnp.where(row < limit_ref[0], scores, -1e30)


def attend_kernel(limit_ref, l_ref, w_ref, u_ref, qt_ref, mix_ref, lse_ref):
    keys, values = keys_and_values(l_ref, w_ref, u_ref)
    scores = masked_scores(limit_ref, keys, qt_ref[0])
    top = jnp.max(scores, axis=0, keepdims=True)
    weights = jnp.exp(scores - top)
    total = jnp.sum(weights, axis=0, keepdims=True)
    probs = (weights * (1.0 / total)).astype(bf16)
    mix_ref[...] = dot(probs, values, TN).astype(bf16)
    lse_ref[0] = top + jnp.log(total)


def attend(limit, l_all, w_kvb, u_kvb, qt):
    length = l_all.shape[0]
    tokens = qt.shape[2]
    spec = pltpu.PrefetchScalarGridSpec(
        num_scalar_prefetch=1,
        grid=(HEADS,),
        in_specs=[
            pl.BlockSpec((length, LW), lambda h, s: (0, 0)),
            pl.BlockSpec((LATENT, NOPE + VDIM), lambda h, s: (0, h)),
            pl.BlockSpec((LANES, NOPE + VDIM), lambda h, s: (0, h)),
            pl.BlockSpec((1, 2 * LANES, tokens), lambda h, s: (h, 0, 0)),
        ],
        out_specs=[
            pl.BlockSpec((tokens, VDIM), lambda h, s: (0, h)),
            pl.BlockSpec((1, 1, tokens), lambda h, s: (h, 0, 0)),
        ],
    )
    return pl.pallas_call(
        attend_kernel,
        grid_spec=spec,
        out_shape=[
            jax.ShapeDtypeStruct((tokens, HEADS * VDIM), bf16),
            jax.ShapeDtypeStruct((HEADS, 1, tokens), f32),
        ],
        compiler_params=params(1),
        cost_estimate=cost(HEADS * 2 * length * (LW * 256 + tokens * 384), 8e6),
        name="attend",
    )(limit, l_all, w_kvb, u_kvb, qt)


def attend_back_kernel(
    limit_ref,
    l_ref,
    lt_ref,
    w_ref,
    u_ref,
    q_ref,
    qt_ref,
    lse_ref,
    dm_ref,
    dmt_ref,
    cos_ref,
    sin_ref,
    dq_ref,
    dl_ref,
    du_ref,
    acc,
):
    h = pl.program_id(0)

    @pl.when(h == 0)
    def _():
        acc[...] = jnp.zeros_like(acc)

    keys, values = keys_and_values(l_ref, w_ref, u_ref)
    scores = masked_scores(limit_ref, keys, qt_ref[0])
    probs = jnp.exp(scores - lse_ref[0])
    dvalues = dot(probs.astype(bf16), dm_ref[...])
    dprobs = dot(values, dmt_ref[...])
    delta = jnp.sum(probs * dprobs, axis=0, keepdims=True)
    dscores = (probs * (dprobs - delta)).astype(bf16)
    dq = dot(dscores, keys, TN) * SCALE
    lane = lax.broadcasted_iota(jnp.int32, (dq.shape[0], LANES), 1)
    rope = dq[:, LANES:]
    rope = rope * cos_ref[...] + unrotate_pair(lane, rope) * sin_ref[...]
    dq_ref[0] = jnp.concatenate([dq[:, :LANES], rope], 1).astype(bf16)
    dkeys = dot(dscores, q_ref[0]) * SCALE
    dkv = jnp.concatenate([dkeys[:, :NOPE], dvalues], 1).astype(bf16)
    acc[:, :LATENT] += dot(dkv, w_ref[...], NT)
    acc[:, LATENT:] += dot(dkv, u_ref[...], NT) + dkeys[:, NOPE:]
    du_ref[...] = dot(lt_ref[...], dkv)

    @pl.when(h == pl.num_programs(0) - 1)
    def _():
        dl_ref[...] = acc[...].astype(bf16)


def attend_back(limit, l_all, lt, w_kvb, u_kvb, q, qt, lse, dmix, dmix_t, cos, sin):
    length = l_all.shape[0]
    tokens = qt.shape[2]
    spec = pltpu.PrefetchScalarGridSpec(
        num_scalar_prefetch=1,
        grid=(HEADS,),
        in_specs=[
            pl.BlockSpec((length, LW), lambda h, s: (0, 0)),
            pl.BlockSpec((LANES, length), lambda h, s: (0, 0)),
            pl.BlockSpec((LATENT, NOPE + VDIM), lambda h, s: (0, h)),
            pl.BlockSpec((LANES, NOPE + VDIM), lambda h, s: (0, h)),
            pl.BlockSpec((1, tokens, 2 * LANES), lambda h, s: (h, 0, 0)),
            pl.BlockSpec((1, 2 * LANES, tokens), lambda h, s: (h, 0, 0)),
            pl.BlockSpec((1, 1, tokens), lambda h, s: (h, 0, 0)),
            pl.BlockSpec((tokens, VDIM), lambda h, s: (0, h)),
            pl.BlockSpec((VDIM, tokens), lambda h, s: (h, 0)),
            pl.BlockSpec((tokens, LANES), lambda h, s: (0, 0)),
            pl.BlockSpec((tokens, LANES), lambda h, s: (0, 0)),
        ],
        out_specs=[
            pl.BlockSpec((1, tokens, 2 * LANES), lambda h, s: (h, 0, 0)),
            pl.BlockSpec((length, LW), lambda h, s: (0, 0)),
            pl.BlockSpec((LANES, NOPE + VDIM), lambda h, s: (0, h)),
        ],
        scratch_shapes=[pltpu.VMEM((length, LW), f32)],
    )
    return pl.pallas_call(
        attend_back_kernel,
        grid_spec=spec,
        out_shape=[
            jax.ShapeDtypeStruct((HEADS, tokens, 2 * LANES), bf16),
            jax.ShapeDtypeStruct((length, LW), bf16),
            jax.ShapeDtypeStruct((LANES, HEADS * (NOPE + VDIM)), f32),
        ],
        compiler_params=params(1),
        cost_estimate=cost(HEADS * 2 * length * (2 * LW * 256 + tokens * 1024), 16e6),
        name="attend_back",
    )(limit, l_all, lt, w_kvb, u_kvb, q, qt, lse, dmix, dmix_t, cos, sin)


def picks(slot_row, slots):
    row = lax.broadcasted_iota(jnp.int32, (slots, slot_row.shape[1]), 0)
    return jnp.where(row == slot_row, 1.0, 0.0).astype(bf16)


def routed_kernel(
    first_ref,
    x_ref,
    g_ref,
    slot_ref,
    prob_ref,
    wg0,
    wg1,
    wu0,
    wu1,
    wo0,
    wo1,
    y_ref,
    dx_ref,
    rows,
    grads,
    yacc,
    xacc,
    *,
    slots,
):
    e, j = pl.program_id(0), pl.program_id(1)
    last = pl.num_programs(1) - 1
    chunks = x_ref.shape[0]

    @pl.when(j == 0)
    def _():
        for c in range(chunks):
            pick = picks(slot_ref[c, pl.ds(e, 1), :], slots)
            at = pl.ds(c * slots, slots)
            rows[at, :] = dot(pick, x_ref[c]).astype(bf16)
            weight = dot(pick, prob_ref[c].astype(bf16))
            lane = lax.broadcasted_iota(jnp.int32, weight.shape, 1)
            weight = jnp.sum(
                jnp.where(lane == first_ref[0] + e, weight, 0.0), axis=1, keepdims=True
            )
            grads[at, :] = (dot(pick, g_ref[c]) * weight).astype(bf16)
        yacc[...] = jnp.zeros_like(yacc)
        xacc[...] = jnp.zeros_like(xacc)

    w_in = jnp.concatenate([wg0[0], wg1[0], wu0[0], wu1[0]], 1)
    w_out = jnp.concatenate([wo0[0], wo1[0]], 0)
    acts = dot(rows[...], w_in)
    width = 2 * LANES
    gate, up = acts[:, :width], acts[:, width:]
    sig = 1.0 / (1.0 + jnp.exp(-gate))
    lane = lax.broadcasted_iota(jnp.int32, gate.shape, 1)
    keep = jnp.logical_or(lane < LANES, j < last)
    silu = jnp.where(keep, gate * sig, 0.0)
    yacc[...] += dot((silu * up).astype(bf16), w_out)
    dhid = dot(grads[...], w_out, NT)
    dhid = jnp.where(keep, dhid, 0.0)
    dgate = dhid * up * (sig * (1.0 + gate * (1.0 - sig)))
    dboth = jnp.concatenate([dgate, dhid * silu], 1).astype(bf16)
    xacc[...] += dot(dboth, w_in, NT)

    @pl.when(j == last)
    def _():
        y_ref[0] = yacc[...].astype(bf16)
        dx_ref[0] = xacc[...].astype(bf16)


def routed(first, x, g, slot, prob, w_in, w_out):
    chunks, tokens, _ = x.shape
    local = w_in.shape[0]
    ff = w_out.shape[1]
    slots = tokens // 2
    tiles = ff // LANES
    steps = (tiles + 1) // 2
    rows = chunks * slots
    whole = lambda a: pl.BlockSpec(a.shape, lambda e, j, s: (0,) * a.ndim)
    odd = lambda j: jnp.minimum(2 * j + 1, tiles - 1)
    in_block = (1, D, LANES)
    out_block = (1, LANES, D)
    spec = pltpu.PrefetchScalarGridSpec(
        num_scalar_prefetch=1,
        grid=(local, steps),
        in_specs=[
            whole(x),
            whole(g),
            whole(slot),
            whole(prob),
            pl.BlockSpec(in_block, lambda e, j, s: (e, 0, 2 * j)),
            pl.BlockSpec(in_block, lambda e, j, s: (e, 0, odd(j))),
            pl.BlockSpec(in_block, lambda e, j, s: (e, 0, tiles + 2 * j)),
            pl.BlockSpec(in_block, lambda e, j, s: (e, 0, tiles + odd(j))),
            pl.BlockSpec(out_block, lambda e, j, s: (e, 2 * j, 0)),
            pl.BlockSpec(out_block, lambda e, j, s: (e, odd(j), 0)),
        ],
        out_specs=[
            pl.BlockSpec((1, rows, D), lambda e, j, s: (e, 0, 0)),
            pl.BlockSpec((1, rows, D), lambda e, j, s: (e, 0, 0)),
        ],
        scratch_shapes=[
            pltpu.VMEM((rows, D), bf16),
            pltpu.VMEM((rows, D), bf16),
            pltpu.VMEM((rows, D), f32),
            pltpu.VMEM((rows, D), f32),
        ],
    )
    shape = jax.ShapeDtypeStruct((local, rows, D), bf16)
    return pl.pallas_call(
        functools.partial(routed_kernel, slots=slots),
        grid_spec=spec,
        out_shape=[shape, shape],
        compiler_params=params(2),
        cost_estimate=cost(local * rows * D * ff * 12, local * D * ff * 6),
        name="routed",
    )(first, x, g, slot, prob, w_in, w_in, w_in, w_in, w_out, w_out)


def shared_kernel(
    first_ref,
    x_ref,
    g_ref,
    slot_ref,
    prob_ref,
    y_ref,
    dx_ref,
    wi_ref,
    wo_ref,
    u_ref,
    dn_ref,
    out_ref,
    dout_ref,
    gu_up_ref,
    gu_down_ref,
    dn_up_ref,
    dn_down_ref,
    *,
    slots,
):
    c = pl.program_id(0)
    local = y_ref.shape[0]
    half = dn_ref.shape[0]
    x, g = x_ref[0], g_ref[0]
    proj = dot(x, wi_ref[...])
    r = proj[:, 2 * half :].astype(bf16)
    acts = proj[:, : 2 * half] + dot(r, u_ref[...])
    gate, up = acts[:, :half], acts[:, half:]
    sig = 1.0 / (1.0 + jnp.exp(-gate))
    silu = gate * sig
    inner = (silu * up).astype(bf16)
    rdn = dot(inner, dn_ref[...]).astype(bf16)
    out = dot(jnp.concatenate([inner, rdn], 1), wo_ref[...])
    back = dot(g, wo_ref[...], NT)
    drdn = back[:, half:].astype(bf16)
    dinner = back[:, :half] + dot(drdn, dn_ref[...], NT)
    dgate = dinner * up * (sig * (1.0 + gate * (1.0 - sig)))
    dboth = jnp.concatenate([dgate, dinner * silu], 1).astype(bf16)
    dr = dot(dboth, u_ref[...], NT)

    prob = prob_ref[0]
    lane = lax.broadcasted_iota(jnp.int32, prob.shape, 1)
    gf = g.astype(f32)
    pulls = jnp.zeros_like(prob)
    picked = []
    for e in range(local):
        pick = picks(slot_ref[0, e : e + 1, :], slots)
        picked.append(pick)
        mine = lane == first_ref[0] + e
        weight = jnp.sum(jnp.where(mine, prob, 0.0), axis=1, keepdims=True)
        result = dot(pick, y_ref[e], TN)
        out += weight * result
        pull = weight * jnp.sum(result * gf, axis=1, keepdims=True)
        pulls += jnp.where(mine, pull, 0.0)
    dlogit = pulls - prob * jnp.sum(pulls, axis=1, keepdims=True)
    out_ref[0] = out.astype(bf16)
    dsmall = (dr + dlogit).astype(bf16)
    dx = dot(jnp.concatenate([dboth, dsmall], 1), wi_ref[...], NT)
    for e in range(local):
        dx += dot(picked[e], dx_ref[e], TN)
    dout_ref[0] = dx.astype(bf16)

    @pl.when(c == 0)
    def _():
        gu_up_ref[...] = jnp.zeros_like(gu_up_ref)
        gu_down_ref[...] = jnp.zeros_like(gu_down_ref)
        dn_up_ref[...] = jnp.zeros_like(dn_up_ref)
        dn_down_ref[...] = jnp.zeros_like(dn_down_ref)

    gu_up_ref[...] += dot(r, dboth, TN)
    gu_down_ref[...] += dot(dr.astype(bf16), x, TN)
    dn_up_ref[...] += dot(rdn, g, TN)
    dn_down_ref[...] += dot(drdn, inner, TN)


def shared(first, x, g, slot, prob, y, dx, wi, wo, u, dn):
    chunks, tokens, _ = x.shape
    local = y.shape[0]
    slots = tokens // 2
    half = dn.shape[0]
    whole = lambda a: pl.BlockSpec(a.shape, lambda c, s: (0,) * a.ndim)
    one = lambda a: pl.BlockSpec((1,) + a.shape[1:], lambda c, s: (c,) + (0,) * (a.ndim - 1))
    rows = pl.BlockSpec((local, slots, D), lambda c, s: (0, c, 0))
    still = lambda *shape: pl.BlockSpec(shape, lambda c, s: (0, 0))
    spec = pltpu.PrefetchScalarGridSpec(
        num_scalar_prefetch=1,
        grid=(chunks,),
        in_specs=[one(x), one(g), one(slot), one(prob), rows, rows]
        + [whole(wi), whole(wo), whole(u), whole(dn)],
        out_specs=[
            one(x),
            one(x),
            still(LANES, 2 * half),
            still(LANES, D),
            still(LANES, D),
            still(LANES, half),
        ],
    )
    shape = jax.ShapeDtypeStruct(x.shape, bf16)
    return pl.pallas_call(
        functools.partial(shared_kernel, slots=slots),
        grid_spec=spec,
        out_shape=[
            shape,
            shape,
            jax.ShapeDtypeStruct((LANES, 2 * half), f32),
            jax.ShapeDtypeStruct((LANES, D), f32),
            jax.ShapeDtypeStruct((LANES, D), f32),
            jax.ShapeDtypeStruct((LANES, half), f32),
        ],
        compiler_params=params(1),
        cost_estimate=cost(chunks * 4e9, chunks * 8e6),
        name="shared",
    )(first, x, g, slot, prob, y, dx, wi, wo, u, dn)


def rms_scale(v):
    return lax.rsqrt(jnp.mean(v * v, axis=-1, keepdims=True) + EPS)


def rms_back(v, scale, gain, dy):
    unit = v * scale
    gdy = gain * dy
    return (gdy - unit * jnp.mean(unit * gdy, axis=-1, keepdims=True)) * scale


def angles(positions):
    half = ROPE // 2
    ladder = jnp.arange(half).astype(f32)
    frequency = jnp.exp(ladder * (-2.0 * math.log(10000.0) / ROPE))
    turn = positions.astype(f32)[:, None] * frequency[None, :]
    return jnp.cos(turn), jnp.sin(turn)


def pad_lanes(v, width, before=0):
    return jnp.pad(v, ((0, 0), (before, width - before - v.shape[1])))


def pad_rows(v, height, before=0):
    return jnp.pad(v, ((before, height - before - v.shape[0]), (0, 0)))


def round_up(n, m):
    return -(-n // m) * m


def pack(parts, unit=LANES):
    return jnp.concatenate([pad_lanes(v, round_up(v.shape[1], unit)) for v in parts], 1)


def unpack(v, widths, unit=LANES):
    out, at = [], 0
    for w in widths:
        out.append(v[:, at : at + w])
        at += round_up(w, unit)
    return out


def total_adapters(parts, ids, shards):
    widths = [v.shape[1] for v in parts]
    packed = pack(parts)
    columns = round_up(packed.shape[1], shards * LANES)
    packed = pad_lanes(packed, columns).astype(bf16)
    cut = columns // shards
    mine = packed.reshape(RANK, shards, cut).transpose(1, 0, 2)
    mine = lax.all_to_all(mine, "shard", split_axis=0, concat_axis=0, tiled=True)
    mine = jnp.sum(mine.astype(f32), axis=0).astype(bf16)
    seqs = lax.all_gather(mine, "replica", axis=0)
    chosen = (ids[None, :] == jnp.arange(ADAPTERS)[:, None]).astype(f32)
    sums = jnp.sum(chosen[:, :, None, None] * seqs.astype(f32)[None], axis=1).astype(bf16)
    sums = sums.reshape(shards, ADAPTERS // shards, RANK, cut)
    full = lax.all_to_all(sums, "shard", split_axis=0, concat_axis=0, tiled=True)
    full = full.transpose(1, 2, 0, 3).reshape(ADAPTERS // shards, RANK, columns)
    out, at = [], 0
    for w in widths:
        out.append(full[:, :, at : at + w].astype(f32))
        at += round_up(w, LANES)
    return out


def body(
    hidden_in,
    out_grad,
    routes,
    seq_adapter,
    attn_gain,
    latent_gain,
    ffn_gain,
    w_qa,
    w_kvb,
    w_out,
    w_router,
    w_shared_in,
    w_shared_out,
    w_expert_in,
    w_expert_out,
    qa_down,
    qa_up,
    kvb_down,
    kvb_up,
    out_down,
    out_up,
    gu_down,
    gu_up,
    dn_down,
    dn_up,
):
    shards = lax.axis_size("shard")
    replicas = lax.axis_size("replica")
    place = lax.axis_index("shard")
    tokens = hidden_in.shape[0]
    local = w_expert_in.shape[0]
    experts = local * shards
    ring = Ring(shards)
    adapter_id = seq_adapter[0]
    first = (place * local).astype(jnp.int32).reshape(1)
    limit = ((place + 1) * tokens).astype(jnp.int32).reshape(1)

    early = pack([qa_down[0], qa_up[0], kvb_down[0]])
    early = ring.gather_rows(early, False).reshape(shards, RANK, early.shape[1])
    early = lax.dynamic_index_in_dim(early, adapter_id, 0, keepdims=False)
    a_qd, a_qu, a_kd = unpack(early, [D, qa_up.shape[2], LATENT])
    rest = [kvb_up[0], out_down[0], out_up[0], gu_down[0], gu_up[0], dn_down[0], dn_up[0]]
    late = pack(rest) * (adapter_id == place).astype(bf16)
    late = lax.psum(late, "shard")
    a_ku, a_od, a_ou, a_gd, a_gu, a_nd, a_nu = unpack(late, [v.shape[1] for v in rest])
    ids = lax.all_gather(seq_adapter, "replica", axis=0, tiled=True)

    routes_all = lax.all_gather(routes, "shard", axis=0)
    wanted = first[0] + jnp.arange(local)
    mask = jnp.any(routes_all[:, None, :, :] == wanted[None, :, None, None], axis=-1)
    before = jnp.triu(jnp.ones((tokens, tokens), bf16), 1)
    rank = lax.dot_general(
        mask.astype(bf16), before, (((2,), (0,)), ((), ())), preferred_element_type=f32
    )
    slot_all = jnp.where(mask, rank.astype(jnp.int32), -1)

    width = w_shared_out.shape[0]
    half = round_up(width, LANES)
    rows_in = w_shared_in.shape[0]
    if replicas % 2 == 0:
        core = lax.axis_index("replica") % 2
        mine = lax.dynamic_slice_in_dim(w_shared_in, core * (rows_in // 2), rows_in // 2, 0)
    else:
        mine = w_shared_in
    mine = mine.reshape(mine.shape[0], 2, shards, width).transpose(2, 0, 1, 3)
    mine = jnp.pad(mine, ((0, 0), (0, 0), (0, 0), (0, half - width)))
    mine = mine.reshape(shards, mine.shape[1], 2 * half)
    mine = lax.all_to_all(mine, "shard", split_axis=0, concat_axis=0, tiled=True)
    if replicas % 2 == 0:
        other = pair_swap(mine, replicas)
        w_si = jnp.concatenate(
            [jnp.where(core == 0, mine, other), jnp.where(core == 0, other, mine)], 1
        )
    else:
        w_si = mine
    w_si = w_si.reshape(shards * rows_in, 2 * half)

    inputs = hidden_in.astype(f32)
    in_scale = rms_scale(inputs)
    hb = (inputs * in_scale * attn_gain).astype(bf16)
    w_lat = shared_rows(ring, w_qa[:, QW:], replicas)
    w_q = shared_rows(ring, w_qa[:, :QW], replicas)
    r_qa = dot(hb, a_qd, NT).astype(bf16)
    lat_raw = dot(hb, w_lat) + dot(r_qa, a_qu[:, QW:])
    latent_raw, rope_raw = lat_raw[:, :LATENT], lat_raw[:, LATENT:]
    lat_scale = rms_scale(latent_raw)
    latent = (latent_raw * lat_scale * latent_gain).astype(bf16)
    positions = place * tokens + jnp.arange(tokens)
    cos_half, sin_half = angles(positions)
    rh = ROPE // 2
    rope_a, rope_b = rope_raw[:, :rh], rope_raw[:, rh:]
    rope = jnp.concatenate(
        [rope_a * cos_half - rope_b * sin_half, rope_b * cos_half + rope_a * sin_half], 1
    ).astype(bf16)
    r_kv = dot(latent, a_kd, NT).astype(bf16)
    l_own = pad_lanes(jnp.concatenate([latent, rope, r_kv], 1), LW)
    l_all = ring.gather_rows(l_own, False)
    cos = pad_lanes(jnp.concatenate([cos_half, cos_half], 1), LANES)
    sin = pad_lanes(jnp.concatenate([sin_half, sin_half], 1), LANES)
    u_qa = pad_rows(a_qu, LANES)
    q, qt = query_heads(hb, pad_lanes(r_qa, LANES), w_q, u_qa[:, :QW], cos, sin)

    full_kvb = shared_rows(ring, w_kvb, replicas)
    u_kvb = pad_rows(a_ku, LANES, ROPE)
    mixture, lse = attend(limit, l_all, full_kvb, u_kvb, qt)
    full_out = shared_rows(ring, w_out, replicas)
    r_out = dot(mixture, a_od, NT).astype(bf16)
    after_attn = inputs + dot(mixture, full_out) + dot(r_out, a_ou)
    ffn_scale = rms_scale(after_attn)
    ffn_low = (after_attn * ffn_scale * ffn_gain).astype(bf16)

    w_i = jnp.concatenate([w_si, pad_lanes(jnp.concatenate([w_router, a_gd.T], 1), LANES)], 1)
    w_o = jnp.concatenate([pad_rows(w_shared_out, half), pad_rows(a_nu, LANES)], 0)
    gu_g = lax.dynamic_slice_in_dim(a_gu, place * width, width, 1)
    gu_u = lax.dynamic_slice_in_dim(a_gu, shards * width + place * width, width, 1)
    u_gu = jnp.concatenate([pad_lanes(gu_g, half), pad_lanes(gu_u, half)], 1)
    u_gu = pad_rows(u_gu, LANES, experts)
    nd_own = lax.dynamic_slice_in_dim(a_nd, place * width, width, 1)
    dn_own = pad_rows(pad_lanes(nd_own.T, LANES), half)
    g_steps = ring.gather(out_grad, False)
    x_steps = ring.gather(ffn_low, True)
    groups = [x_steps[0] + x_steps[1], x_steps[2], x_steps[3] + x_steps[4]]
    g_groups = [g_steps[0] + g_steps[1], g_steps[2], g_steps[3] + g_steps[4]]
    out_piece, dx_piece, small = {}, {}, None
    for members, g_members in zip(groups, g_groups):
        offs = [off for off, _ in members]
        g_by = dict(g_members)
        x = jnp.stack([block for _, block in members])
        g = jnp.stack([g_by[off] for off in offs])
        slot = jnp.stack(
            [lax.dynamic_index_in_dim(slot_all, ring.owner(off), 0, False) for off in offs]
        )
        logit = lax.dot_general(
            x, w_router, (((2,), (0,)), ((), ())), preferred_element_type=f32
        )
        prob = jnp.pad(
            jax.nn.softmax(logit, axis=-1), ((0, 0), (0, 0), (0, LANES - experts))
        )
        y, dxr = routed(first, x, g, slot, prob, w_expert_in, w_expert_out)
        o, dx, *grads = shared(first, x, g, slot, prob, y, dxr, w_i, w_o, u_gu, dn_own)
        small = grads if small is None else [a + b for a, b in zip(small, grads)]
        for i, off in enumerate(offs):
            out_piece[off], dx_piece[off] = o[i], dx[i]
    far = shards // 2
    out_piece[-far], dx_piece[-far] = out_piece[far], dx_piece[far]
    ffn_grad = ring.scatter_sum(lambda off: dx_piece[off])
    block_out = (after_attn + ring.scatter_sum(lambda off: out_piece[off])).astype(bf16)

    def spread(v, cols):
        return jnp.concatenate(
            [
                lax.dynamic_update_slice_in_dim(
                    jnp.zeros((RANK, cols), f32), part, place * width, 1
                )
                for part in v
            ],
            1,
        )

    g_gu_up = small[0][experts : experts + RANK]
    g_gu_up = spread([g_gu_up[:, :width], g_gu_up[:, half : half + width]], shards * width)
    g_gu_down = small[1][experts : experts + RANK]
    g_dn_up = small[2][:RANK]
    g_dn_down = spread([small[3][:RANK, :width]], shards * width)

    d_after = out_grad.astype(f32) + rms_back(after_attn, ffn_scale, ffn_gain, ffn_grad)
    d_after_low = d_after.astype(bf16)
    dr_out = dot(d_after_low, a_ou, NT).astype(bf16)
    dmix = (dot(d_after_low, full_out, NT) + dot(dr_out, a_od)).astype(bf16)
    g_out_up = dot(r_out, d_after_low, TN)
    g_out_down = dot(dr_out, mixture, TN)
    dq, dl, g_ku = attend_back(
        limit,
        l_all,
        l_all[:, LATENT:].T,
        full_kvb,
        u_kvb,
        q,
        qt,
        lse,
        dmix,
        dmix.T,
        cos,
        sin,
    )
    g_kvb_up = g_ku[ROPE : ROPE + RANK]
    dl_own = ring.scatter_sum(
        lambda off: lax.dynamic_slice_in_dim(dl, ring.owner(off) * tokens, tokens, 0)
    )
    dr_kv = dl_own[:, LATENT + ROPE : LATENT + ROPE + RANK].astype(bf16)
    d_latent = dl_own[:, :LATENT] + dot(dr_kv, a_kd)
    g_kvb_down = dot(dr_kv, latent, TN)
    d_latent = rms_back(latent_raw, lat_scale, latent_gain, d_latent)
    drope = dl_own[:, LATENT : LATENT + ROPE]
    drope_a, drope_b = drope[:, :rh], drope[:, rh:]
    drope = jnp.concatenate(
        [drope_a * cos_half + drope_b * sin_half, drope_b * cos_half - drope_a * sin_half], 1
    )
    d_lat = jnp.concatenate([d_latent, drope], 1).astype(bf16)
    dhb_q, dr_q, g_qu = query_back(dq, w_q, u_qa[:, :QW], pad_lanes(r_qa, LANES).T)
    dr_qa = (dr_q[:, :RANK] + dot(d_lat, a_qu[:, QW:], NT)).astype(bf16)
    dhb = dhb_q + dot(d_lat, w_lat, NT) + dot(dr_qa, a_qd)
    g_qa_up = jnp.concatenate([g_qu[:RANK], dot(r_qa, d_lat, TN)], 1)
    g_qa_down = dot(dr_qa, hb, TN)
    hidden_grad = d_after + rms_back(inputs, in_scale, attn_gain, dhb)

    t_rest = total_adapters(
        [g_kvb_down, g_kvb_up, g_out_down, g_out_up, g_gu_down, g_gu_up, g_dn_down, g_dn_up],
        ids,
        shards,
    )
    t_qa = total_adapters([g_qa_down, g_qa_up], ids, shards)
    return (block_out, hidden_grad, *t_qa, *t_rest)


def solution(mesh):
    rows = P(("replica", "shard"), None)
    cut2 = P("shard", None)
    cut3 = P("shard", None, None)
    in_specs = (
        (rows, rows, rows, P("replica"), P(), P(), P())
        + (cut2, cut2, cut2, P(), cut2, cut2, cut3, cut3)
        + (cut3,) * 10
    )
    out_specs = (rows, rows) + (cut3,) * 10
    return jax.shard_map(body, mesh=mesh, in_specs=in_specs, out_specs=out_specs, check_vma=False)
```

```python
import functools
import math

import jax
import jax.numpy as jnp
from jax import lax
from jax.experimental import pallas as pl
from jax.experimental.pallas import tpu as pltpu
from jax.sharding import PartitionSpec as P

D = 2048
HEADS = 16
NOPE = 128
ROPE = 64
VDIM = 128
LATENT = 512
TOPK = 6
RANK = 16
ADAPTERS = 8
BLOCK = 256
QW = HEADS * (NOPE + ROPE)
LW = LATENT + 2 * ROPE
LANES = 128
VMEM_LIMIT = 60 * 1024 * 1024
SCALE = (NOPE + ROPE) ** (-0.5)
EPS = 1e-06
f32 = jnp.float32
bf16 = jnp.bfloat16

NN = (((1,), (0,)), ((), ()))
NT = (((1,), (1,)), ((), ()))
TN = (((0,), (0,)), ((), ()))


def dot(a, b, dims=NN):
    return lax.dot_general(a, b, dims, preferred_element_type=f32)


def params(n):
    return pltpu.CompilerParams(
        dimension_semantics=("arbitrary",) * n, vmem_limit_bytes=VMEM_LIMIT
    )


def cost(flops, nbytes):
    return pl.CostEstimate(flops=int(flops), bytes_accessed=int(nbytes), transcendentals=0)


def gate_kernel(*refs):
    del refs


def gate(values, marks):
    anywhere = pl.BlockSpec(memory_space=pl.ANY)
    values, marks = tuple(values), tuple(marks)
    return pl.pallas_call(
        gate_kernel,
        in_specs=[anywhere] * len(values + marks),
        out_specs=[anywhere] * len(values),
        out_shape=[jax.ShapeDtypeStruct(v.shape, v.dtype) for v in values],
        input_output_aliases={i: i for i in range(len(values))},
        cost_estimate=cost(0, 0),
        name="gate",
    )(*values, *marks)


def zero_kernel(*refs):
    refs[-1][0] = 0


def zero_after(*marks):
    anywhere = pl.BlockSpec(memory_space=pl.ANY)
    return pl.pallas_call(
        zero_kernel,
        in_specs=[anywhere] * len(marks),
        out_specs=pl.BlockSpec(memory_space=pltpu.SMEM),
        out_shape=jax.ShapeDtypeStruct((1,), jnp.int32),
        cost_estimate=cost(0, 0),
        name="zero_after",
    )(*marks)[0]


def ring_of(count):
    return list(range(0, count, 2)) + list(range(count - 1, 0, -2))


class Ring:
    def __init__(self, count):
        order = ring_of(count)
        place_of = [order.index(i) for i in range(count)]
        self.count = count
        pos = jnp.asarray(place_of, jnp.int32)[lax.axis_index("shard")]
        self.owners = jnp.asarray(order, jnp.int32)[(pos + jnp.arange(count)) % count]
        self.right = [(order[i], order[(i + 1) % count]) for i in range(count)]
        self.left = [(order[i], order[(i - 1) % count]) for i in range(count)]

    def owner(self, off):
        return self.owners[off % self.count]

    def send_right(self, v):
        return lax.ppermute(v, "shard", self.right)

    def send_left(self, v):
        return lax.ppermute(v, "shard", self.left)

    def scatter_sum(self, piece, holds):
        half = self.count // 2
        far = piece(half)
        n = far.shape[0] // 2
        r, l = far[:n], far[n:]
        if half in holds:
            r, l = gate((r, l), holds[half]())
        r, l = self.send_right(r), self.send_left(l)
        for h in range(half - 1, 0, -1):
            up, down = piece(h), piece(-h)
            if h in holds:
                r, l = gate((r, l), holds[h](r, l))
            if r.shape[0] == n:
                up = jnp.concatenate([up[:n].astype(f32) + r.astype(f32), up[n:].astype(f32)], 0)
                down = jnp.concatenate([down[:n].astype(f32), down[n:].astype(f32) + l.astype(f32)], 0)
            else:
                up = up.astype(f32) + r.astype(f32)
                down = down.astype(f32) + l.astype(f32)
            r, l = self.send_right(up.astype(bf16)), self.send_left(down.astype(bf16))
        return piece(0).astype(f32) + r.astype(f32) + l.astype(f32)


class Walk:
    def __init__(self, ring, *arrays):
        self.ring, self.own, self.pairs, self.halves = ring, list(arrays), [], None

    def hop(self, *marks):
        half, k = self.ring.count // 2, len(self.own)
        if self.pairs:
            held = gate(self.pairs[-1], marks)
            self.pairs[-1] = held
            r, l = held[:k], held[k:]
        else:
            if marks:
                self.own = gate(self.own, marks)
            r = l = self.own
        if len(self.pairs) < half - 1:
            right = [self.ring.send_right(v) for v in r]
            left = [self.ring.send_left(v) for v in l]
            self.pairs.append(right + left)
            return self.pairs[-1]
        right = [self.ring.send_right(v[: v.shape[0] // 2]) for v in r]
        left = [self.ring.send_left(v[v.shape[0] // 2 :]) for v in l]
        self.halves = right + left
        return self.halves

    def blocks(self, i=0):
        k = len(self.own)
        out = [(0, 0, self.own[i])]
        for h, pair in enumerate(self.pairs):
            out += [(-h - 1, 0, pair[i]), (h + 1, 0, pair[k + i])]
        far = self.ring.count // 2
        n = self.own[i].shape[0] // 2
        return out + [(far, 0, self.halves[i]), (far, n, self.halves[k + i])]


def pair_swap(v, replicas):
    return lax.ppermute(v, "replica", [(i, i ^ 1) for i in range(replicas)])


def fill_rows(info, places, blocks, out):
    count = info.shape[0] - 1
    for (off, n, row, half, other), block in zip(places, blocks):
        core = info[count]
        at = info[off % count] * n + row + half * (1 - core if other else core)
        out[pl.ds(pl.multiple_of(at, 16), block.shape[0]), :] = block[...]


def place_kernel(info, *refs, places):
    fill_rows(info, places, refs[:-1], refs[-1])


def place_rows(info, places, blocks, height, first=0, width=None, cut=None):
    width = width or blocks[0].shape[1]
    cut = cut or next((c for c in (2048, 1024) if width % c == 0 and height * c <= 1 << 21), width)
    at = first // cut
    spec = pltpu.PrefetchScalarGridSpec(
        num_scalar_prefetch=1,
        grid=(width // cut,),
        in_specs=[pl.BlockSpec((b.shape[0], cut), lambda i, s: (0, at + i)) for b in blocks],
        out_specs=pl.BlockSpec((height, cut), lambda i, s: (0, i)),
    )
    return pl.pallas_call(
        functools.partial(place_kernel, places=places),
        grid_spec=spec,
        out_shape=jax.ShapeDtypeStruct((height, width), blocks[0].dtype),
        compiler_params=params(1),
        cost_estimate=cost(0, height * width * 4),
        name="place_rows",
    )(info, *blocks)


def whole_rows(info, blocks, n):
    places = [(off, n, row, 0, False) for off, row, _ in blocks]
    return place_rows(info, places, [v for _, _, v in blocks], (info.shape[0] - 1) * n)


def pack_kernel(core, qa_ref, kvb_ref, out_ref, all_ref, *, fold):
    del core
    rows, wide = kvb_ref.shape[0], kvb_ref.shape[1] // fold
    all_ref[:, :QW] = qa_ref[:, :QW]
    for i in range(fold):
        all_ref[i * rows : (i + 1) * rows, QW : QW + wide] = kvb_ref[:, i * wide : (i + 1) * wide]
    all_ref[:, QW + wide : QW + wide + D] = out_ref[...]
    rest = jnp.zeros((all_ref.shape[0], LW - LATENT - ROPE), all_ref.dtype)
    all_ref[:, QW + wide + D :] = jnp.concatenate([qa_ref[:, QW:], rest], 1)


def pack_weights(core, w_qa, w_kvb, w_out, replicas):
    parts = 2 if replicas % 2 == 0 else 1
    height, kvb_rows = w_out.shape[0] // parts, w_kvb.shape[0] // parts
    fold = height // kvb_rows
    wide = w_kvb.shape[1] // fold
    width = QW + wide + D + LW
    mine = (core % parts).reshape(1)
    share = lambda n, w: pl.BlockSpec((n, w.shape[1]), lambda i, s: (s[0], 0))
    spec = pltpu.PrefetchScalarGridSpec(
        num_scalar_prefetch=1,
        grid=(1,),
        in_specs=[share(height, w_qa), share(kvb_rows, w_kvb), share(height, w_out)],
        out_specs=pl.BlockSpec((height, width), lambda i, s: (0, 0)),
    )
    packed = pl.pallas_call(
        functools.partial(pack_kernel, fold=fold),
        grid_spec=spec,
        out_shape=jax.ShapeDtypeStruct((height, width), bf16),
        compiler_params=params(1),
        cost_estimate=cost(0, height * width * 4),
        name="pack_weights",
    )(mine, w_qa, w_kvb, w_out)
    return kvb_rows, fold, wide, packed


def own_share(w, replicas, zero=0):
    if replicas % 2:
        return w
    half = w.shape[0] // 2
    return lax.dynamic_slice_in_dim(w, lax.axis_index("replica") % 2 * half + zero, half, 0)


class Swaps:
    def __init__(self, ring, walk, replicas):
        self.ring, self.walk, self.replicas = ring, walk, replicas
        self.pairs = []

    def swap(self, blocks):
        got = [pair_swap(v, self.replicas) for v in blocks] if self.replicas % 2 == 0 else []
        self.pairs.append(got)
        return got

    def rows(self, i, n):
        walk, k = self.walk, len(self.walk.own)
        paired = self.replicas % 2 == 0
        far = self.ring.count // 2
        half = walk.own[i].shape[0] // 2
        got = [(0, 0, walk.own, i)]
        for h, pair in enumerate(walk.pairs):
            got += [(-h - 1, 0, pair, i), (h + 1, 0, pair, k + i)]
        got += [(far, 0, walk.halves, i), (far, half, walk.halves, k + i)]
        sets = [walk.own] + list(walk.pairs) + [walk.halves]
        places, out = [], []
        for off, row, blocks, j in got:
            where = next(m for m, v in enumerate(sets) if v is blocks)
            step = n // 2 if paired else 0
            places.append((off, n, row, step, False))
            out.append(blocks[j])
            if paired:
                places.append((off, n, row, step, True))
                out.append(self.pairs[where][j])
        return places, out


def rotate_pair(lane, v):
    half = ROPE // 2
    return jnp.where(lane < half, -pltpu.roll(v, LANES - half, 1), pltpu.roll(v, half, 1))


def unrotate_pair(lane, v):
    half = ROPE // 2
    return jnp.where(lane < half, pltpu.roll(v, LANES - half, 1), -pltpu.roll(v, half, 1))


def query_kernel(info, hb_ref, r_ref, up_ref, cos_ref, sin_ref, *rest, places):
    blocks, q_ref, w_ref = rest[:-2], rest[-2], rest[-1]
    fill_rows(info, places, blocks, w_ref)
    acc = dot(hb_ref[...], w_ref[...]) + dot(r_ref[...], up_ref[...])
    lane = lax.broadcasted_iota(jnp.int32, (acc.shape[0], LANES), 1)
    for i in range(2):
        own = acc if i == 0 else pltpu.roll(acc, NOPE + ROPE, 1)
        rope = own[:, LANES : 2 * LANES]
        turned = rope * cos_ref[...] + rotate_pair(lane, rope) * sin_ref[...]
        turned = jnp.where(lane == LANES - 1, 1.0, turned)
        q_ref[i] = jnp.concatenate([own[:, :LANES], turned], 1).astype(bf16)


def query_heads(info, hb, r, places, blocks, up, cos, sin):
    tokens = hb.shape[0]
    width = 2 * (NOPE + ROPE)
    whole = lambda a: pl.BlockSpec(a.shape, lambda i, s: (0,) * a.ndim)
    column = lambda a: pl.BlockSpec((a.shape[0], width), lambda i, s: (0, i))
    spec = pltpu.PrefetchScalarGridSpec(
        num_scalar_prefetch=1,
        grid=(HEADS // 2,),
        in_specs=[whole(hb), whole(r), column(up), whole(cos), whole(sin)]
        + [column(block) for block in blocks],
        out_specs=pl.BlockSpec((2, tokens, 2 * LANES), lambda i, s: (i, 0, 0)),
        scratch_shapes=[pltpu.VMEM((D, width), bf16)],
    )
    return pl.pallas_call(
        functools.partial(query_kernel, places=places),
        grid_spec=spec,
        out_shape=jax.ShapeDtypeStruct((HEADS, tokens, 2 * LANES), bf16),
        compiler_params=params(1),
        cost_estimate=cost(2 * tokens * D * QW, D * QW * 2),
        name="query_heads",
    )(info, hb, r, up, cos, sin, *blocks)


def query_back_kernel(info, dq_ref, up_ref, rt_ref, *rest, places):
    blocks = rest[:-6]
    dhb_ref, dr_ref, dup_ref, acc, racc, w_ref = rest[-6:]
    i = pl.program_id(0)
    tokens = dq_ref.shape[1]

    @pl.when(i == 0)
    def _():
        acc[...] = jnp.zeros_like(acc)
        racc[...] = jnp.zeros_like(racc)

    fill_rows(info, places, blocks, w_ref)
    pad = jnp.zeros((tokens, LANES), f32)
    first = jnp.concatenate([dq_ref[0].astype(f32), pad], 1)
    second = jnp.concatenate([dq_ref[1].astype(f32), pad], 1)
    both = (first + pltpu.roll(second, NOPE + ROPE, 1)).astype(bf16)
    acc[...] += dot(both, w_ref[...], NT)
    racc[...] += dot(both, up_ref[...], NT)
    dup_ref[...] = dot(rt_ref[...], both)

    @pl.when(i == pl.num_programs(0) - 1)
    def _():
        dhb_ref[...] = acc[...]
        dr_ref[...] = racc[...]


def query_back(info, dq, places, blocks, up, rt):
    tokens = dq.shape[1]
    width = 2 * (NOPE + ROPE)
    column = lambda a: pl.BlockSpec((a.shape[0], width), lambda i, s: (0, i))
    still = lambda *shape: pl.BlockSpec(shape, lambda i, s: (0, 0))
    spec = pltpu.PrefetchScalarGridSpec(
        num_scalar_prefetch=1,
        grid=(HEADS // 2,),
        in_specs=[
            pl.BlockSpec((2, tokens, 2 * LANES), lambda i, s: (i, 0, 0)),
            column(up),
            still(*rt.shape),
        ]
        + [column(block) for block in blocks],
        out_specs=[still(tokens, D), still(tokens, LANES), column(up)],
        scratch_shapes=[
            pltpu.VMEM((tokens, D), f32),
            pltpu.VMEM((tokens, LANES), f32),
            pltpu.VMEM((D, width), bf16),
        ],
    )
    return pl.pallas_call(
        functools.partial(query_back_kernel, places=places),
        grid_spec=spec,
        out_shape=[
            jax.ShapeDtypeStruct((tokens, D), f32),
            jax.ShapeDtypeStruct((tokens, LANES), f32),
            jax.ShapeDtypeStruct((LANES, QW), f32),
        ],
        compiler_params=params(1),
        cost_estimate=cost(2 * tokens * D * QW, D * QW * 2),
        name="query_back",
    )(info, dq, up, rt, *blocks)


LOG2E = math.log2(math.e)


def attend_kernel(l_ref, w_ref, u_ref, q_ref, mix_ref, lse_ref, kv_ref):
    w = w_ref[...].reshape(LATENT, NOPE + VDIM)
    kv = dot(l_ref[:, :LATENT], w) + dot(l_ref[:, LATENT:], u_ref[...])
    kv = kv.astype(bf16)
    kv_ref[...] = kv
    keys = jnp.concatenate([kv[:, :NOPE], l_ref[:, LATENT:]], 1)
    values = jnp.concatenate([kv[:, NOPE:], jnp.ones((kv.shape[0], LANES), bf16)], 1)
    scores = dot(q_ref[0], keys, NT)
    top = jnp.max(scores, axis=1, keepdims=True)
    weights = jnp.exp2((scores - top) * (SCALE * LOG2E)).astype(bf16)
    both = dot(weights, values)
    total = both[:, VDIM:]
    mix_ref[...] = (both[:, :VDIM] / total).astype(bf16)
    lse = top * (SCALE * LOG2E) + jnp.log2(total)
    lse_ref[0] = lse.T[:8]


def folded(w_kvb, at):
    pieces, _, rows, width = w_kvb.shape
    wide = NOPE + VDIM
    per = width // wide
    return pl.BlockSpec(
        (pieces, 1, rows, wide), lambda h: (0, (at + h) // per, 0, (at + h) % per)
    )


def attend(l_all, w_kvb, u_kvb, q):
    length = l_all.shape[0]
    tokens = q.shape[1]
    wide = NOPE + VDIM
    return pl.pallas_call(
        attend_kernel,
        grid=(HEADS,),
        in_specs=[
            pl.BlockSpec((length, LW), lambda h: (0, 0)),
            folded(w_kvb, 0),
            pl.BlockSpec((LANES, wide), lambda h: (0, h)),
            pl.BlockSpec((1, tokens, 2 * LANES), lambda h: (h, 0, 0)),
        ],
        out_specs=[
            pl.BlockSpec((tokens, VDIM), lambda h: (0, h)),
            pl.BlockSpec((1, 8, tokens), lambda h: (h, 0, 0)),
            pl.BlockSpec((length, wide), lambda h: (0, h)),
        ],
        out_shape=[
            jax.ShapeDtypeStruct((tokens, HEADS * VDIM), bf16),
            jax.ShapeDtypeStruct((HEADS, 8, tokens), f32),
            jax.ShapeDtypeStruct((length, HEADS * wide), bf16),
        ],
        compiler_params=params(1),
        cost_estimate=cost(HEADS * 2 * length * (LW * 256 + tokens * 512), 8e6),
        name="attend",
    )(l_all, w_kvb, u_kvb, q)


def attend_back_kernel(
    l_ref,
    lt_ref,
    w_ref,
    u_ref,
    kv_ref,
    q_ref,
    lse_ref,
    delta_ref,
    dm_ref,
    cos_ref,
    sin_ref,
    was_ref,
    dq_ref,
    dl_ref,
    du_ref,
    acc,
):
    h = pl.program_id(0)

    @pl.when(h == 0)
    def _():
        if was_ref.shape == acc.shape:
            acc[...] = was_ref[...].astype(f32)
        else:
            acc[...] = jnp.zeros_like(acc)

    keys = jnp.concatenate([kv_ref[:, :NOPE], l_ref[:, LATENT:]], 1)
    values = kv_ref[:, NOPE:]
    scores = dot(keys, q_ref[0], NT)
    probs = jnp.exp2(scores * (SCALE * LOG2E) - lse_ref[0, :1])
    dvalues = dot(probs.astype(bf16), dm_ref[...])
    dprobs = dot(values, dm_ref[...], NT)
    dscores = (probs * (dprobs - delta_ref[0, :1])).astype(bf16)
    dq = dot(dscores, keys, TN) * SCALE
    lane = lax.broadcasted_iota(jnp.int32, (dq.shape[0], LANES), 1)
    rope = dq[:, LANES:]
    rope = rope * cos_ref[...] + unrotate_pair(lane, rope) * sin_ref[...]
    dq_ref[0] = jnp.concatenate([dq[:, :LANES], rope], 1).astype(bf16)
    dkeys = dot(dscores, q_ref[0]) * SCALE
    dkv = jnp.concatenate([dkeys[:, :NOPE], dvalues], 1).astype(bf16)
    acc[:, :LATENT] += dot(dkv, w_ref[...].reshape(LATENT, NOPE + VDIM), NT)
    acc[:, LATENT:] += dot(dkv, u_ref[...], NT) + dkeys[:, NOPE:]
    du_ref[...] = dot(lt_ref[...], dkv)

    @pl.when(h == pl.num_programs(0) - 1)
    def _():
        dl_ref[...] = acc[...].astype(bf16)


def attend_back(part, l_all, lt, w_kvb, u_kvb, kv, q, lse, delta, dmix, cos, sin, was):
    length = l_all.shape[0]
    tokens = q.shape[1]
    wide = NOPE + VDIM
    heads = HEADS // 2
    at = part * heads
    still = lambda a: pl.BlockSpec(a.shape, lambda h: (0, 0))
    column = lambda n, w: pl.BlockSpec((n, w), lambda h: (0, at + h))
    head = lambda *shape: pl.BlockSpec((1,) + shape, lambda h: (at + h, 0, 0))
    return pl.pallas_call(
        attend_back_kernel,
        grid=(heads,),
        in_specs=[
            still(l_all),
            still(lt),
            folded(w_kvb, at),
            column(LANES, wide),
            column(length, wide),
            head(tokens, 2 * LANES),
            head(8, tokens),
            head(8, tokens),
            column(tokens, VDIM),
            still(cos),
            still(sin),
            still(was),
        ],
        out_specs=[
            pl.BlockSpec((1, tokens, 2 * LANES), lambda h: (h, 0, 0)),
            pl.BlockSpec((length, LW), lambda h: (0, 0)),
            pl.BlockSpec((LANES, wide), lambda h: (0, h)),
        ],
        out_shape=[
            jax.ShapeDtypeStruct((heads, tokens, 2 * LANES), bf16),
            jax.ShapeDtypeStruct((length, LW), bf16),
            jax.ShapeDtypeStruct((LANES, heads * wide), f32),
        ],
        scratch_shapes=[pltpu.VMEM((length, LW), f32)],
        compiler_params=params(1),
        cost_estimate=cost(heads * 2 * length * (LW * 256 + tokens * 1024), 30e6),
        name="attend_back",
    )(l_all, lt, w_kvb, u_kvb, kv, q, lse, delta, dmix, cos, sin, was)


def picks(slot_row, slots):
    row = lax.broadcasted_iota(jnp.int32, (slots, slot_row.shape[1]), 0)
    return jnp.where(row == slot_row, 1.0, 0.0).astype(bf16)


def silu_parts(gate):
    sig = 1.0 / (1.0 + jnp.exp(-gate))
    return gate * sig, sig * (1.0 + gate * (1.0 - sig))


def router_probs(logits, experts):
    lane = lax.broadcasted_iota(jnp.int32, logits.shape, 1)
    logits = jnp.where(lane < experts, logits, -1e30)
    odds = jnp.exp(logits - jnp.max(logits, axis=1, keepdims=True))
    return odds / jnp.sum(odds, axis=1, keepdims=True)


def routed_kernel(info, slot_ref, wr_ref, w_in, w_out, *rest, offs, slots, wide, experts):
    chunks, count = len(offs), info.shape[0] - 1
    x_refs, g_refs = rest[:chunks], rest[chunks : 2 * chunks]
    y_ref, dx_ref, pull_ref, rows, grads, hidden, dacts = rest[2 * chunks :]
    e = pl.program_id(0)
    ff = w_out.shape[1]
    weights = []
    for c in range(chunks):
        pick = picks(slot_ref[info[1 + offs[c] % count], pl.ds(e, 1), :], slots)
        at = pl.ds(c * slots, slots)
        x = dot(pick, x_refs[c][...]).astype(bf16)
        rows[at, :] = x
        weight = router_probs(dot(x, wr_ref[...]), experts)
        lane = lax.broadcasted_iota(jnp.int32, weight.shape, 1)
        weight = jnp.sum(jnp.where(lane == info[0] + e, weight, 0.0), axis=1, keepdims=True)
        weights.append(weight)
        grads[at, :] = (dot(pick, g_refs[c][...]) * weight).astype(bf16)
    weight = jnp.concatenate(weights, 0)
    for a in range(0, ff, wide):
        b = min(a + wide, ff)
        gate = dot(rows[...], w_in[0, :, a:b])
        up = dot(rows[...], w_in[0, :, ff + a : ff + b])
        dhid = dot(grads[...], w_out[0, a:b, :], NT)
        silu, slope = silu_parts(gate)
        hidden[:, a:b] = (silu * up).astype(bf16)
        dacts[:, a:b] = (dhid * up * slope).astype(bf16)
        dacts[:, ff + a : ff + b] = (dhid * silu).astype(bf16)
    pull = jnp.zeros((rows.shape[0], 1), f32)
    step = 2 * wide
    for a in range(0, D, step):
        y = dot(hidden[...], w_out[0, :, a : a + step])
        pull += jnp.sum(y * grads[:, a : a + step].astype(f32), axis=1, keepdims=True)
        y_ref[0, :, a : a + step] = (y * weight).astype(bf16)
        dx_ref[0, :, a : a + step] = dot(dacts[...], w_in[0, a : a + step, :], NT).astype(bf16)
    lane = lax.broadcasted_iota(jnp.int32, (rows.shape[0], LANES), 1)
    pull_ref[0] = jnp.where(lane == info[0] + e, pull, 0.0).astype(bf16)


def routed(info, offs, xs, gs, slot_all, w_router, experts, w_in, w_out):
    chunks, tokens = len(xs), xs[0].shape[0]
    local = w_in.shape[0]
    ff = w_out.shape[1]
    slots = tokens // 2
    rows = chunks * slots
    once = pl.Buffered(1)
    whole = lambda a: pl.BlockSpec(a.shape, lambda e, s: (0,) * a.ndim, pipeline_mode=once)
    out = pl.BlockSpec((1, rows, D), lambda e, s: (e, 0, 0))
    spec = pltpu.PrefetchScalarGridSpec(
        num_scalar_prefetch=1,
        grid=(local,),
        in_specs=[
            whole(slot_all),
            whole(w_router),
            pl.BlockSpec((1, D, 2 * ff), lambda e, s: (e, 0, 0)),
            pl.BlockSpec((1, ff, D), lambda e, s: (e, 0, 0)),
        ]
        + [whole(v) for v in (*xs, *gs)],
        out_specs=[out, out, pl.BlockSpec((1, rows, LANES), lambda e, s: (e, 0, 0))],
        scratch_shapes=[
            pltpu.VMEM((rows, D), bf16),
            pltpu.VMEM((rows, D), bf16),
            pltpu.VMEM((rows, ff), bf16),
            pltpu.VMEM((rows, 2 * ff), bf16),
        ],
    )
    shape = jax.ShapeDtypeStruct((local, rows, D), bf16)
    return pl.pallas_call(
        functools.partial(
            routed_kernel, offs=offs, slots=slots, wide=2 * LANES, experts=experts
        ),
        grid_spec=spec,
        out_shape=[shape, shape, jax.ShapeDtypeStruct((local, rows, LANES), bf16)],
        compiler_params=params(1),
        cost_estimate=cost(local * rows * D * ff * 12, local * D * ff * 6),
        name="routed",
    )(info, slot_all, w_router, w_in, w_out, *xs, *gs)


def shared_kernel(
    info,
    slot_ref,
    y_ref,
    dx_ref,
    pull_ref,
    wi_ref,
    wo_ref,
    u_ref,
    dn_ref,
    *rest,
    offs,
    slots,
    experts,
):
    blocks = rest[:-8]
    out_ref, dout_ref, gu_up_ref, gu_down_ref, dn_up_ref, dn_down_ref, x_ref, g_ref = rest[-8:]
    c = pl.program_id(0)
    chunks, count = len(offs), info.shape[0] - 1
    spot = sum(jnp.where(c == i, off % count, 0) for i, off in enumerate(offs))
    owner = info[1 + spot]
    for i in range(chunks):

        @pl.when(c == i)
        def _(i=i):
            x_ref[...] = blocks[i][...]
            g_ref[...] = blocks[chunks + i][...]

    local = y_ref.shape[0]
    half = dn_ref.shape[0]
    x, g = x_ref[...], g_ref[...]
    proj = dot(x, wi_ref[...])
    r = proj[:, 2 * half :].astype(bf16)
    prob = router_probs(proj[:, 2 * half :], experts)
    acts = proj[:, : 2 * half] + dot(r, u_ref[...])
    gate, up = acts[:, :half], acts[:, half:]
    silu, slope = silu_parts(gate)
    inner = (silu * up).astype(bf16)
    rdn = dot(inner, dn_ref[...]).astype(bf16)
    back = dot(g, wo_ref[...], NT)
    drdn = back[:, half:].astype(bf16)
    dinner = back[:, :half] + dot(drdn, dn_ref[...], NT)
    dboth = jnp.concatenate([dinner * up * slope, dinner * silu], 1).astype(bf16)
    dr = dot(dboth, u_ref[...], NT)

    pick = jnp.concatenate([picks(slot_ref[owner, e : e + 1, :], slots) for e in range(local)], 0)
    rows = lambda ref: jnp.concatenate([ref[e] for e in range(local)], 0)
    out = dot(jnp.concatenate([inner, rdn], 1), wo_ref[...]) + dot(pick, rows(y_ref), TN)
    out_ref[0] = out.astype(bf16)
    pulls = dot(pick, rows(pull_ref), TN)
    dlogit = pulls - prob * jnp.sum(pulls, axis=1, keepdims=True)
    dsmall = (dr + dlogit).astype(bf16)
    dx = dot(jnp.concatenate([dboth, dsmall], 1), wi_ref[...], NT)
    dout_ref[0] = (dx + dot(pick, rows(dx_ref), TN)).astype(bf16)

    @pl.when(c == 0)
    def _():
        gu_up_ref[...] = jnp.zeros_like(gu_up_ref)
        gu_down_ref[...] = jnp.zeros_like(gu_down_ref)
        dn_up_ref[...] = jnp.zeros_like(dn_up_ref)
        dn_down_ref[...] = jnp.zeros_like(dn_down_ref)

    gu_up_ref[...] += dot(r, dboth, TN)
    gu_down_ref[...] += dot(dr.astype(bf16), x, TN)
    dn_up_ref[...] += dot(rdn, g, TN)
    dn_down_ref[...] += dot(drdn, inner, TN)


def shared(info, offs, xs, gs, slot_all, experts, y, dx, pull, wi, wo, u, dn):
    chunks, tokens = len(xs), xs[0].shape[0]
    local = y.shape[0]
    slots = tokens // 2
    half = dn.shape[0]
    whole = lambda a: pl.BlockSpec(a.shape, lambda c, s: (0,) * a.ndim)
    one = pl.BlockSpec((1, tokens, D), lambda c, s: (c, 0, 0))
    rows = lambda a: pl.BlockSpec((local, slots, a.shape[2]), lambda c, s: (0, c, 0))
    still = lambda *shape: pl.BlockSpec(shape, lambda c, s: (0, 0))
    operands = [slot_all, y, dx, pull, wi, wo, u, dn, *xs, *gs]
    specs = [whole(slot_all), rows(y), rows(dx), rows(pull)]
    specs += [whole(a) for a in operands[4:]]
    spec = pltpu.PrefetchScalarGridSpec(
        num_scalar_prefetch=1,
        grid=(chunks,),
        in_specs=specs,
        out_specs=[
            one,
            one,
            still(LANES, 2 * half),
            still(LANES, D),
            still(LANES, D),
            still(LANES, half),
        ],
        scratch_shapes=[pltpu.VMEM((tokens, D), bf16)] * 2,
    )
    return pl.pallas_call(
        functools.partial(shared_kernel, offs=offs, slots=slots, experts=experts),
        grid_spec=spec,
        out_shape=[
            jax.ShapeDtypeStruct((chunks, tokens, D), bf16),
            jax.ShapeDtypeStruct((chunks, tokens, D), bf16),
            jax.ShapeDtypeStruct((LANES, 2 * half), f32),
            jax.ShapeDtypeStruct((LANES, D), f32),
            jax.ShapeDtypeStruct((LANES, D), f32),
            jax.ShapeDtypeStruct((LANES, half), f32),
        ],
        compiler_params=params(1),
        cost_estimate=cost(chunks * 4e9, chunks * 8e6),
        name="shared",
    )(info, *operands)


def rms_scale(v):
    return lax.rsqrt(jnp.mean(v * v, axis=-1, keepdims=True) + EPS)


def rms_back(v, scale, gain, dy):
    unit = v * scale
    gdy = gain * dy
    return (gdy - unit * jnp.mean(unit * gdy, axis=-1, keepdims=True)) * scale


def angles(positions):
    half = ROPE // 2
    ladder = jnp.arange(half).astype(f32)
    frequency = jnp.exp(ladder * (-2.0 * math.log(10000.0) / ROPE))
    turn = positions.astype(f32)[:, None] * frequency[None, :]
    return jnp.cos(turn), jnp.sin(turn)


def pad_lanes(v, width, before=0):
    return jnp.pad(v, ((0, 0), (before, width - before - v.shape[1])))


def pad_rows(v, height, before=0):
    return jnp.pad(v, ((before, height - before - v.shape[0]), (0, 0)))


def round_up(n, m):
    return -(-n // m) * m


def pack(parts, unit=LANES):
    return jnp.concatenate([pad_lanes(v, round_up(v.shape[1], unit)) for v in parts], 1)


def unpack(v, widths, unit=LANES):
    out, at = [], 0
    for w in widths:
        out.append(v[:, at : at + w])
        at += round_up(w, unit)
    return out


class Totals:
    def __init__(self, parts, shards):
        self.shards = shards
        self.widths = [v.shape[1] for v in parts]
        packed = pack(parts)
        self.columns = round_up(packed.shape[1], shards * LANES)
        packed = pad_lanes(packed, self.columns).astype(bf16)
        self.cut = self.columns // shards
        self.packed = packed.reshape(RANK, shards, self.cut).transpose(1, 0, 2)

    def deal(self):
        mine = lax.all_to_all(self.packed, "shard", split_axis=0, concat_axis=0, tiled=True)
        self.mine = jnp.sum(mine.astype(f32), axis=0).astype(bf16)
        return self.mine

    def gather(self, ids):
        seqs = lax.all_gather(self.mine, "replica", axis=0)
        chosen = (ids[None, :] == jnp.arange(ADAPTERS)[:, None]).astype(f32)
        sums = jnp.sum(chosen[:, :, None, None] * seqs.astype(f32)[None], axis=1).astype(bf16)
        self.sums = sums.reshape(self.shards, ADAPTERS // self.shards, RANK, self.cut)
        return self.sums

    def home(self):
        full = lax.all_to_all(self.sums, "shard", split_axis=0, concat_axis=0, tiled=True)
        full = full.transpose(1, 2, 0, 3).reshape(ADAPTERS // self.shards, RANK, self.columns)
        out, at = [], 0
        for w in self.widths:
            out.append(full[:, :, at : at + w].astype(f32))
            at += round_up(w, LANES)
        return out


def body(
    hidden_in,
    out_grad,
    routes,
    seq_adapter,
    attn_gain,
    latent_gain,
    ffn_gain,
    w_qa,
    w_kvb,
    w_out,
    w_router,
    w_shared_in,
    w_shared_out,
    w_expert_in,
    w_expert_out,
    qa_down,
    qa_up,
    kvb_down,
    kvb_up,
    out_down,
    out_up,
    gu_down,
    gu_up,
    dn_down,
    dn_up,
):
    shards = lax.axis_size("shard")
    replicas = lax.axis_size("replica")
    place = lax.axis_index("shard")
    tokens = hidden_in.shape[0]
    local = w_expert_in.shape[0]
    experts = local * shards
    ring = Ring(shards)
    adapter_id = seq_adapter[0]
    core = (lax.axis_index("replica") % 2).astype(jnp.int32)
    spots = jnp.concatenate([ring.owners, core.reshape(1)])
    ids = lax.all_gather(seq_adapter, "replica", axis=0, tiled=True)
    first = (place * local).astype(jnp.int32).reshape(1)

    tables = [qa_down, qa_up[:, :, :QW], qa_up[:, :, QW:], kvb_down, kvb_up, out_down, out_up]
    tables = [t[0] for t in tables + [gu_down, gu_up, dn_down, dn_up]]
    dealt = pack(tables)
    cut = round_up(dealt.shape[1], shards * LANES) // shards
    dealt = pad_lanes(dealt, cut * shards).reshape(RANK, shards, cut).transpose(1, 0, 2)
    dealt = lax.all_to_all(dealt, "shard", split_axis=0, concat_axis=0, tiled=True)
    dealt = lax.dynamic_index_in_dim(dealt, adapter_id, 0, keepdims=True)
    dealt = jnp.broadcast_to(dealt, (shards, RANK, cut))
    dealt = lax.all_to_all(dealt, "shard", split_axis=0, concat_axis=0, tiled=True)
    dealt = dealt.transpose(1, 0, 2).reshape(RANK, shards * cut)
    a_qd, a_quq, a_qul, a_kd, a_ku, a_od, a_ou, a_gd, a_gu, a_nd, a_nu = unpack(
        dealt, [t.shape[1] for t in tables]
    )

    kvb_rows, fold, kvb_wide, own_weights = pack_weights(core, w_qa, w_kvb, w_out, replicas)
    w_walk = Walk(ring, own_weights)
    w_swaps = Swaps(ring, w_walk, replicas)
    w1 = w_walk.hop()
    own_swap = w_swaps.swap(w_walk.own)
    w2 = w_walk.hop(*own_swap)
    u_q = pad_rows(a_quq, LANES)
    u_kvb = pad_rows(a_ku, LANES, ROPE)
    wr = pad_lanes(w_router, LANES)
    width = w_shared_out.shape[0]
    half = round_up(width, LANES)
    rows_in = w_shared_in.shape[0]
    if replicas % 2 == 0:
        core = lax.axis_index("replica") % 2
    mine = own_share(w_shared_in, replicas, zero_after(*w1))
    mine = mine.reshape(mine.shape[0], 2, shards, width).transpose(2, 0, 1, 3)
    mine = jnp.pad(mine, ((0, 0), (0, 0), (0, 0), (0, half - width)))
    mine = mine.reshape(shards, mine.shape[1], 2 * half)
    ready = mine
    mine = lax.all_to_all(mine, "shard", split_axis=0, concat_axis=0, tiled=True)
    if replicas % 2 == 0:
        other = pair_swap(mine, replicas)
        w_si = jnp.concatenate(
            [jnp.where(core == 0, mine, other), jnp.where(core == 0, other, mine)], 1
        )
    else:
        w_si = mine
    w_si = w_si.reshape(shards * rows_in, 2 * half)

    w_i = jnp.concatenate([w_si, pad_lanes(jnp.concatenate([w_router, a_gd.T], 1), LANES)], 1)
    w_o = jnp.concatenate([pad_rows(w_shared_out, half), pad_rows(a_nu, LANES)], 0)
    gu_g = lax.dynamic_slice_in_dim(a_gu, place * width, width, 1)
    gu_u = lax.dynamic_slice_in_dim(a_gu, shards * width + place * width, width, 1)
    u_gu = jnp.concatenate([pad_lanes(gu_g, half), pad_lanes(gu_u, half)], 1)
    u_gu = pad_rows(u_gu, LANES, experts)
    nd_own = lax.dynamic_slice_in_dim(a_nd, place * width, width, 1)
    dn_own = pad_rows(pad_lanes(nd_own.T, LANES), half)

    inputs = hidden_in.astype(f32)
    in_scale = rms_scale(inputs)
    hb = (inputs * in_scale * attn_gain).astype(bf16)
    r_qa = dot(hb, a_qd, NT).astype(bf16)
    swap1 = w_swaps.swap(w_walk.pairs[0])
    w3 = w_walk.hop(*swap1, ready)
    swap2 = w_swaps.swap(w_walk.pairs[1])
    w4 = w_walk.hop(*swap2, wr, w_o, u_gu, dn_own, r_qa, u_q, u_kvb, ids)
    w_swaps.swap(w_walk.pairs[2])
    w_swaps.swap(w_walk.halves)
    w_at, w_blocks = w_swaps.rows(0, w_out.shape[0])
    kvb_at, out_at, lat_at = QW, QW + kvb_wide, QW + kvb_wide + D
    w_lat = place_rows(spots, w_at, w_blocks, D, lat_at, LW, LANES)[:, : LATENT + ROPE]
    full_kvb = place_rows(spots, w_at, w_blocks, D, kvb_at, kvb_wide, kvb_wide)
    full_kvb = full_kvb.reshape(LATENT // kvb_rows, fold, kvb_rows, kvb_wide)
    full_out = place_rows(spots, w_at, w_blocks, D, out_at, D, D // 2)

    lat_raw = dot(hb, w_lat) + dot(r_qa, a_qul)
    latent_raw, rope_raw = lat_raw[:, :LATENT], lat_raw[:, LATENT:]
    lat_scale = rms_scale(latent_raw)
    latent = (latent_raw * lat_scale * latent_gain).astype(bf16)
    positions = place * tokens + jnp.arange(tokens)
    cos_half, sin_half = angles(positions)
    rh = ROPE // 2
    rope_a, rope_b = rope_raw[:, :rh], rope_raw[:, rh:]
    rope = jnp.concatenate(
        [rope_a * cos_half - rope_b * sin_half, rope_b * cos_half + rope_a * sin_half], 1
    ).astype(bf16)
    r_kv = dot(latent, a_kd, NT).astype(bf16)
    l_own = jnp.concatenate([latent, rope, r_kv, routes.astype(bf16)], 1)
    l_own = pad_lanes(l_own, LW)
    l_walk = Walk(ring, l_own)
    l_walk.hop()
    l_walk.hop()
    l_walk.hop()
    l4 = l_walk.hop()
    g_walk = Walk(ring, out_grad)
    g_walk.hop(*l4)
    last_lane = jnp.arange(LW) == LW - 1
    l_blocks = []
    for off, row, block in l_walk.blocks():
        hide = jnp.where(ring.owner(off) > place, -1e30, 0.0).astype(bf16)
        l_blocks.append((off, row, jnp.where(last_lane, hide, block)))
    l_all = whole_rows(spots, l_blocks, tokens)
    cos = pad_lanes(jnp.concatenate([cos_half, cos_half], 1), LANES)
    sin = pad_lanes(jnp.concatenate([sin_half, sin_half], 1), LANES)
    q = query_heads(
        spots, hb, pad_lanes(r_qa, LANES), w_at, w_blocks, u_q, cos, sin
    )

    mixture, lse, kv = attend(l_all, full_kvb, u_kvb, q)
    r_out = dot(mixture, a_od, NT).astype(bf16)
    after_attn = inputs + dot(mixture, full_out) + dot(r_out, a_ou)
    ffn_scale = rms_scale(after_attn)
    ffn_low = (after_attn * ffn_scale * ffn_gain).astype(bf16)

    at = LATENT + ROPE + RANK
    routes_all = l_all[:, at : at + TOPK].astype(jnp.int32).reshape(shards, tokens, TOPK)
    wanted = first[0] + jnp.arange(local)
    mask = jnp.any(routes_all[:, None, :, :] == wanted[None, :, None, None], axis=-1)
    before = jnp.triu(jnp.ones((tokens, tokens), bf16), 1)
    rank = lax.dot_general(
        mask.astype(bf16), before, (((2,), (0,)), ((), ())), preferred_element_type=f32
    )
    slot_all = jnp.where(mask, rank.astype(jnp.int32), -1)

    out_piece, dx_piece, small = {}, {}, []


    info = jnp.concatenate([first, ring.owners])

    def run_routed(members, *after):
        offs, xs, gs = ([m[i] for m in members] for i in range(3))
        if after:
            xs = gate(xs, after)
        return offs, xs, gs, *routed(
            info, offs, xs, gs, slot_all, wr, experts, w_expert_in, w_expert_out
        )

    def run_shared(offs, xs, gs, y, dxr, pull):
        out, dx, *grads = shared(
            info, offs, xs, gs, slot_all, experts, y, dxr, pull, w_i, w_o, u_gu, dn_own
        )
        small.append(grads)
        for i, off in enumerate(offs):
            out_piece[off], dx_piece[off] = out[i], dx[i]
        return grads[-1]

    far = shards // 2
    walk = Walk(ring, ffn_low)
    members = lambda h: [
        (off, x, g) for off, x, g in zip((-h, h), walk.pairs[h - 1], g_walk.pairs[h - 1])
    ]
    g_walk.hop(mixture)
    x1 = walk.hop()
    done = run_routed([(0, ffn_low, out_grad)])
    walk.hop(done[3])
    g_walk.hop(*x1)
    mark = run_shared(*done)
    done = run_routed(members(1), mark)
    x3 = walk.hop(done[3])
    g_walk.hop(*walk.pairs[1])
    mark = run_shared(*done)
    done = run_routed(members(2), mark)
    walk.hop(done[3])
    mark = run_shared(*done)
    opposite = (far, jnp.concatenate(walk.halves, 0), jnp.concatenate(g_walk.halves, 0))
    run_shared(*run_routed(members(3) + [opposite], mark))
    out_piece[-far], dx_piece[-far] = out_piece[far], dx_piece[far]
    small = [sum(parts[1:], parts[0]) for parts in zip(*small)]

    def spread(v, cols):
        return jnp.concatenate(
            [
                lax.dynamic_update_slice_in_dim(
                    jnp.zeros((RANK, cols), f32), part, place * width, 1
                )
                for part in v
            ],
            1,
        )

    g_gu_up = small[0][experts : experts + RANK]
    g_gu_up = spread([g_gu_up[:, :width], g_gu_up[:, half : half + width]], shards * width)
    g_gu_down = small[1][experts : experts + RANK]
    g_dn_up = small[2][:RANK]
    g_dn_down = spread([small[3][:RANK, :width]], shards * width)

    t_ffn, seen = Totals([g_gu_down, g_gu_up, g_dn_down, g_dn_up], shards), {}

    def late_hold(r, l):
        seen["near"] = (r, l)
        return (t_ffn.gather(ids),)

    ffn_grad = ring.scatter_sum(
        lambda off: dx_piece[off],
        {
            far - 1: lambda r, l: (t_ffn.packed,),
            far - 2: lambda r, l: (t_ffn.deal(),),
            far - 3: late_hold,
        },
    )

    d_after = out_grad.astype(f32) + rms_back(after_attn, ffn_scale, ffn_gain, ffn_grad)
    d_after_low = d_after.astype(bf16)
    dr_out = dot(d_after_low, a_ou, NT).astype(bf16)
    dmix = (dot(d_after_low, full_out, NT) + dot(dr_out, a_od)).astype(bf16)
    g_out_up = dot(r_out, d_after_low, TN)
    g_out_down = dot(dr_out, mixture, TN)
    delta = (dmix.astype(f32) * mixture.astype(f32)).reshape(tokens, HEADS, VDIM).sum(-1).T
    delta = jnp.broadcast_to(delta[:, None, :], (HEADS, 8, tokens))
    lt = l_all[:, LATENT:].T
    parts = []

    def back(*marks):
        was = parts[-1][1] if parts else jnp.zeros((8, LANES), bf16)
        (marked,) = gate((lse,), marks) if not parts else gate((lse + 0.0,), marks)
        parts.append(
            attend_back(
                len(parts), l_all, lt, full_kvb, u_kvb, kv, q, marked, delta, dmix, cos, sin, was
            )
        )
        return (parts[-1][2],)

    def first_arrived(r, l):
        seen["far"] = (r[:16], l[:16])
        return ()

    def next_arrived(r, l):
        seen["next"] = (r[:16], l[:16])
        return back(*seen["far"])

    out_sum = ring.scatter_sum(
        lambda off: out_piece[off],
        {
            far: lambda: (ffn_grad,),
            far - 1: first_arrived,
            far - 2: next_arrived,
            far - 3: lambda r, l: back(*seen["next"]),
        },
    )
    block_out = (after_attn + out_sum).astype(bf16)
    dq = jnp.concatenate([part[0] for part in parts], 0)
    dl = parts[-1][1]
    g_ku = jnp.concatenate([part[2] for part in parts], 1)
    g_kvb_up = g_ku[ROPE : ROPE + RANK]
    dhb_q, dr_q, g_qu = query_back(spots, dq, w_at, w_blocks, u_q, pad_lanes(r_qa, LANES).T)
    dl_own = ring.scatter_sum(
        lambda off: lax.dynamic_slice_in_dim(dl, ring.owner(off) * tokens, tokens, 0),
        {far - 2: lambda r, l: (dr_q,)},
    )
    dr_kv = dl_own[:, LATENT + ROPE : LATENT + ROPE + RANK].astype(bf16)
    d_latent = dl_own[:, :LATENT] + dot(dr_kv, a_kd)
    g_kvb_down = dot(dr_kv, latent, TN)
    d_latent = rms_back(latent_raw, lat_scale, latent_gain, d_latent)
    drope = dl_own[:, LATENT : LATENT + ROPE]
    drope_a, drope_b = drope[:, :rh], drope[:, rh:]
    drope = jnp.concatenate(
        [drope_a * cos_half + drope_b * sin_half, drope_b * cos_half - drope_a * sin_half], 1
    )
    d_lat = jnp.concatenate([d_latent, drope], 1).astype(bf16)
    dr_qa = (dr_q[:, :RANK] + dot(d_lat, a_qul, NT)).astype(bf16)
    dhb = dhb_q + dot(d_lat, w_lat, NT) + dot(dr_qa, a_qd)
    g_qa_up = jnp.concatenate([g_qu[:RANK], dot(r_qa, d_lat, TN)], 1)
    g_qa_down = dot(dr_qa, hb, TN)
    hidden_grad = d_after + rms_back(inputs, in_scale, attn_gain, dhb)

    t_attn = Totals(
        [g_qa_down, g_qa_up, g_kvb_down, g_kvb_up, g_out_down, g_out_up], shards
    )
    t_attn.deal()
    t_attn.gather(ids)
    return (block_out, hidden_grad, *t_attn.home(), *t_ffn.home())


def solution(mesh):
    rows = P(("replica", "shard"), None)
    cut2 = P("shard", None)
    cut3 = P("shard", None, None)
    in_specs = (
        (rows, rows, rows, P("replica"), P(), P(), P())
        + (cut2, cut2, cut2, P(), cut2, cut2, cut3, cut3)
        + (cut3,) * 10
    )
    out_specs = (rows, rows) + (cut3,) * 10
    return jax.shard_map(body, mesh=mesh, in_specs=in_specs, out_specs=out_specs, check_vma=False)
```

```python
import functools
import math

import jax
import jax.numpy as jnp
from jax import lax
from jax.experimental import pallas as pl
from jax.experimental.pallas import tpu as pltpu
from jax.sharding import PartitionSpec as P

D = 2048
HEADS = 16
NOPE = 128
ROPE = 64
VDIM = 128
LATENT = 512
TOPK = 6
RANK = 16
ADAPTERS = 8
BLOCK = 256
QW = HEADS * (NOPE + ROPE)
LW = LATENT + 2 * ROPE
LANES = 128
VMEM_LIMIT = 60 * 1024 * 1024
SCALE = (NOPE + ROPE) ** (-0.5)
EPS = 1e-06
f32 = jnp.float32
bf16 = jnp.bfloat16

NN = (((1,), (0,)), ((), ()))
NT = (((1,), (1,)), ((), ()))
TN = (((0,), (0,)), ((), ()))


def dot(a, b, dims=NN):
    return lax.dot_general(a, b, dims, preferred_element_type=f32)


def params(n):
    return pltpu.CompilerParams(
        dimension_semantics=("arbitrary",) * n, vmem_limit_bytes=VMEM_LIMIT
    )


def cost(flops, nbytes):
    return pl.CostEstimate(flops=int(flops), bytes_accessed=int(nbytes), transcendentals=0)


def gate_kernel(*refs):
    del refs


def gate(values, marks):
    anywhere = pl.BlockSpec(memory_space=pl.ANY)
    values, marks = tuple(values), tuple(marks)
    return pl.pallas_call(
        gate_kernel,
        in_specs=[anywhere] * len(values + marks),
        out_specs=[anywhere] * len(values),
        out_shape=[jax.ShapeDtypeStruct(v.shape, v.dtype) for v in values],
        input_output_aliases={i: i for i in range(len(values))},
        cost_estimate=cost(0, 0),
        name="gate",
    )(*values, *marks)


def zero_kernel(*refs):
    refs[-1][0] = 0


def zero_after(*marks):
    anywhere = pl.BlockSpec(memory_space=pl.ANY)
    return pl.pallas_call(
        zero_kernel,
        in_specs=[anywhere] * len(marks),
        out_specs=pl.BlockSpec(memory_space=pltpu.SMEM),
        out_shape=jax.ShapeDtypeStruct((1,), jnp.int32),
        cost_estimate=cost(0, 0),
        name="zero_after",
    )(*marks)[0]


def ring_of(count):
    return list(range(0, count, 2)) + list(range(count - 1, 0, -2))


class Ring:
    def __init__(self, count):
        order = ring_of(count)
        place_of = [order.index(i) for i in range(count)]
        self.count = count
        pos = jnp.asarray(place_of, jnp.int32)[lax.axis_index("shard")]
        self.owners = jnp.asarray(order, jnp.int32)[(pos + jnp.arange(count)) % count]
        self.right = [(order[i], order[(i + 1) % count]) for i in range(count)]
        self.left = [(order[i], order[(i - 1) % count]) for i in range(count)]

    def owner(self, off):
        return self.owners[off % self.count]

    def send_right(self, v):
        return lax.ppermute(v, "shard", self.right)

    def send_left(self, v):
        return lax.ppermute(v, "shard", self.left)

    def scatter_sum(self, piece, holds):
        half = self.count // 2
        far = piece(half)
        n = far.shape[0] // 2
        r, l = far[:n], far[n:]
        if half in holds:
            r, l = gate((r, l), holds[half]())
        r, l = self.send_right(r), self.send_left(l)
        for h in range(half - 1, 0, -1):
            up, down = piece(h), piece(-h)
            if h in holds:
                r, l = gate((r, l), holds[h](r, l))
            if r.shape[0] == n:
                up = jnp.concatenate([up[:n].astype(f32) + r.astype(f32), up[n:].astype(f32)], 0)
                down = jnp.concatenate([down[:n].astype(f32), down[n:].astype(f32) + l.astype(f32)], 0)
            else:
                up = up.astype(f32) + r.astype(f32)
                down = down.astype(f32) + l.astype(f32)
            r, l = self.send_right(up.astype(bf16)), self.send_left(down.astype(bf16))
        return piece(0).astype(f32) + r.astype(f32) + l.astype(f32)


class Walk:
    def __init__(self, ring, *arrays):
        self.ring, self.own, self.pairs, self.halves = ring, list(arrays), [], None

    def hop(self, *marks):
        half, k = self.ring.count // 2, len(self.own)
        if self.pairs:
            held = gate(self.pairs[-1], marks)
            self.pairs[-1] = held
            r, l = held[:k], held[k:]
        else:
            if marks:
                self.own = gate(self.own, marks)
            r = l = self.own
        if len(self.pairs) < half - 1:
            right = [self.ring.send_right(v) for v in r]
            left = [self.ring.send_left(v) for v in l]
            self.pairs.append(right + left)
            return self.pairs[-1]
        right = [self.ring.send_right(v[: v.shape[0] // 2]) for v in r]
        left = [self.ring.send_left(v[v.shape[0] // 2 :]) for v in l]
        self.halves = right + left
        return self.halves

    def blocks(self, i=0):
        k = len(self.own)
        out = [(0, 0, self.own[i])]
        for h, pair in enumerate(self.pairs):
            out += [(-h - 1, 0, pair[i]), (h + 1, 0, pair[k + i])]
        far = self.ring.count // 2
        n = self.own[i].shape[0] // 2
        return out + [(far, 0, self.halves[i]), (far, n, self.halves[k + i])]


def pair_swap(v, replicas):
    return lax.ppermute(v, "replica", [(i, i ^ 1) for i in range(replicas)])


def fill_rows(info, places, blocks, out):
    count = info.shape[0] - 1
    for (off, n, row, half, other), block in zip(places, blocks):
        core = info[count]
        at = info[off % count] * n + row + half * (1 - core if other else core)
        out[pl.ds(pl.multiple_of(at, 16), block.shape[0]), :] = block[...]


def place_kernel(info, *refs, places):
    fill_rows(info, places, refs[:-1], refs[-1])


def place_rows(info, places, blocks, height, first=0, width=None, cut=None):
    width = width or blocks[0].shape[1]
    cut = cut or next((c for c in (2048, 1024) if width % c == 0 and height * c <= 1 << 21), width)
    at = first // cut
    spec = pltpu.PrefetchScalarGridSpec(
        num_scalar_prefetch=1,
        grid=(width // cut,),
        in_specs=[pl.BlockSpec((b.shape[0], cut), lambda i, s: (0, at + i)) for b in blocks],
        out_specs=pl.BlockSpec((height, cut), lambda i, s: (0, i)),
    )
    return pl.pallas_call(
        functools.partial(place_kernel, places=places),
        grid_spec=spec,
        out_shape=jax.ShapeDtypeStruct((height, width), blocks[0].dtype),
        compiler_params=params(1),
        cost_estimate=cost(0, height * width * 4),
        name="place_rows",
    )(info, *blocks)


def latents_kernel(info, *refs, places):
    blocks, out = refs[:-1], refs[-1]
    count = info.shape[0] - 1
    for (off, n, row, _, _), block in zip(places, blocks):
        rows = block.shape[0]
        at = pl.ds(pl.multiple_of(info[off % count] * n + row, 16), rows)
        hide = jnp.where(info[off % count] > info[0], -1e30, 0.0)
        lane = lax.broadcasted_iota(jnp.int32, (rows, LANES), 1)
        tail = jnp.where(lane == LANES - 1, hide, block[:, LATENT:].astype(f32))
        out[at, :LATENT] = block[:, :LATENT]
        out[at, LATENT:] = tail.astype(bf16)


def all_latents(info, blocks, n):
    places = [(off, n, row, 0, False) for off, row, _ in blocks]
    blocks = [v for _, _, v in blocks]
    height = (info.shape[0] - 1) * n
    spec = pltpu.PrefetchScalarGridSpec(
        num_scalar_prefetch=1,
        grid=(1,),
        in_specs=[pl.BlockSpec(b.shape, lambda i, s: (0, 0)) for b in blocks],
        out_specs=pl.BlockSpec((height, LW), lambda i, s: (0, 0)),
    )
    return pl.pallas_call(
        functools.partial(latents_kernel, places=places),
        grid_spec=spec,
        out_shape=jax.ShapeDtypeStruct((height, LW), bf16),
        compiler_params=params(1),
        cost_estimate=cost(0, height * LW * 4),
        name="all_latents",
    )(info, *blocks)


def whole_rows(info, blocks, n):
    places = [(off, n, row, 0, False) for off, row, _ in blocks]
    return place_rows(info, places, [v for _, _, v in blocks], (info.shape[0] - 1) * n)


def pack_kernel(core, qa_ref, kvb_ref, out_ref, all_ref, *, fold):
    del core
    rows, wide = kvb_ref.shape[0], kvb_ref.shape[1] // fold
    all_ref[:, :QW] = qa_ref[:, :QW]
    for i in range(fold):
        all_ref[i * rows : (i + 1) * rows, QW : QW + wide] = kvb_ref[:, i * wide : (i + 1) * wide]
    all_ref[:, QW + wide : QW + wide + D] = out_ref[...]
    rest = jnp.zeros((all_ref.shape[0], LW - LATENT - ROPE), all_ref.dtype)
    all_ref[:, QW + wide + D :] = jnp.concatenate([qa_ref[:, QW:], rest], 1)


def pack_weights(core, w_qa, w_kvb, w_out, replicas):
    parts = 2 if replicas % 2 == 0 else 1
    height, kvb_rows = w_out.shape[0] // parts, w_kvb.shape[0] // parts
    fold = height // kvb_rows
    wide = w_kvb.shape[1] // fold
    width = QW + wide + D + LW
    mine = (core % parts).reshape(1)
    share = lambda n, w: pl.BlockSpec((n, w.shape[1]), lambda i, s: (s[0], 0))
    spec = pltpu.PrefetchScalarGridSpec(
        num_scalar_prefetch=1,
        grid=(1,),
        in_specs=[share(height, w_qa), share(kvb_rows, w_kvb), share(height, w_out)],
        out_specs=pl.BlockSpec((height, width), lambda i, s: (0, 0)),
    )
    packed = pl.pallas_call(
        functools.partial(pack_kernel, fold=fold),
        grid_spec=spec,
        out_shape=jax.ShapeDtypeStruct((height, width), bf16),
        compiler_params=params(1),
        cost_estimate=cost(0, height * width * 4),
        name="pack_weights",
    )(mine, w_qa, w_kvb, w_out)
    return kvb_rows, fold, wide, packed


def own_share(w, replicas, zero=0):
    if replicas % 2:
        return w
    half = w.shape[0] // 2
    return lax.dynamic_slice_in_dim(w, lax.axis_index("replica") % 2 * half + zero, half, 0)


class Swaps:
    def __init__(self, ring, walk, replicas):
        self.ring, self.walk, self.replicas = ring, walk, replicas
        self.pairs = []

    def swap(self, blocks):
        got = [pair_swap(v, self.replicas) for v in blocks] if self.replicas % 2 == 0 else []
        self.pairs.append(got)
        return got

    def rows(self, i, n):
        walk, k = self.walk, len(self.walk.own)
        paired = self.replicas % 2 == 0
        far = self.ring.count // 2
        half = walk.own[i].shape[0] // 2
        got = [(0, 0, walk.own, i)]
        for h, pair in enumerate(walk.pairs):
            got += [(-h - 1, 0, pair, i), (h + 1, 0, pair, k + i)]
        got += [(far, 0, walk.halves, i), (far, half, walk.halves, k + i)]
        sets = [walk.own] + list(walk.pairs) + [walk.halves]
        places, out = [], []
        for off, row, blocks, j in got:
            where = next(m for m, v in enumerate(sets) if v is blocks)
            step = n // 2 if paired else 0
            places.append((off, n, row, step, False))
            out.append(blocks[j])
            if paired:
                places.append((off, n, row, step, True))
                out.append(self.pairs[where][j])
        return places, out


def rotate_pair(lane, v):
    half = ROPE // 2
    return jnp.where(lane < half, -pltpu.roll(v, LANES - half, 1), pltpu.roll(v, half, 1))


def unrotate_pair(lane, v):
    half = ROPE // 2
    return jnp.where(lane < half, pltpu.roll(v, LANES - half, 1), -pltpu.roll(v, half, 1))


def query_kernel(info, hb_ref, r_ref, up_ref, cos_ref, sin_ref, *rest, places):
    blocks, q_ref, w_ref = rest[:-2], rest[-2], rest[-1]
    fill_rows(info, places, blocks, w_ref)
    acc = dot(hb_ref[...], w_ref[...]) + dot(r_ref[...], up_ref[...])
    lane = lax.broadcasted_iota(jnp.int32, (acc.shape[0], LANES), 1)
    for i in range(2):
        own = acc if i == 0 else pltpu.roll(acc, NOPE + ROPE, 1)
        rope = own[:, LANES : 2 * LANES]
        turned = rope * cos_ref[...] + rotate_pair(lane, rope) * sin_ref[...]
        turned = jnp.where(lane == LANES - 1, 1.0, turned)
        q_ref[i] = jnp.concatenate([own[:, :LANES], turned], 1).astype(bf16)


def query_heads(info, hb, r, places, blocks, up, cos, sin):
    tokens = hb.shape[0]
    width = 2 * (NOPE + ROPE)
    whole = lambda a: pl.BlockSpec(a.shape, lambda i, s: (0,) * a.ndim)
    column = lambda a: pl.BlockSpec((a.shape[0], width), lambda i, s: (0, i))
    spec = pltpu.PrefetchScalarGridSpec(
        num_scalar_prefetch=1,
        grid=(HEADS // 2,),
        in_specs=[whole(hb), whole(r), column(up), whole(cos), whole(sin)]
        + [column(block) for block in blocks],
        out_specs=pl.BlockSpec((2, tokens, 2 * LANES), lambda i, s: (i, 0, 0)),
        scratch_shapes=[pltpu.VMEM((D, width), bf16)],
    )
    return pl.pallas_call(
        functools.partial(query_kernel, places=places),
        grid_spec=spec,
        out_shape=jax.ShapeDtypeStruct((HEADS, tokens, 2 * LANES), bf16),
        compiler_params=params(1),
        cost_estimate=cost(2 * tokens * D * QW, D * QW * 2),
        name="query_heads",
    )(info, hb, r, up, cos, sin, *blocks)


def query_back_kernel(info, dq_ref, up_ref, rt_ref, *rest, places):
    blocks = rest[:-6]
    dhb_ref, dr_ref, dup_ref, acc, racc, w_ref = rest[-6:]
    i = pl.program_id(0)
    tokens = dq_ref.shape[1]

    @pl.when(i == 0)
    def _():
        acc[...] = jnp.zeros_like(acc)
        racc[...] = jnp.zeros_like(racc)

    fill_rows(info, places, blocks, w_ref)
    pad = jnp.zeros((tokens, LANES), f32)
    first = jnp.concatenate([dq_ref[0].astype(f32), pad], 1)
    second = jnp.concatenate([dq_ref[1].astype(f32), pad], 1)
    both = (first + pltpu.roll(second, NOPE + ROPE, 1)).astype(bf16)
    acc[...] += dot(both, w_ref[...], NT)
    racc[...] += dot(both, up_ref[...], NT)
    dup_ref[...] = dot(rt_ref[...], both)

    @pl.when(i == pl.num_programs(0) - 1)
    def _():
        dhb_ref[...] = acc[...]
        dr_ref[...] = racc[...]


def query_back(info, dq, places, blocks, up, rt):
    tokens = dq.shape[1]
    width = 2 * (NOPE + ROPE)
    column = lambda a: pl.BlockSpec((a.shape[0], width), lambda i, s: (0, i))
    still = lambda *shape: pl.BlockSpec(shape, lambda i, s: (0, 0))
    spec = pltpu.PrefetchScalarGridSpec(
        num_scalar_prefetch=1,
        grid=(HEADS // 2,),
        in_specs=[
            pl.BlockSpec((2, tokens, 2 * LANES), lambda i, s: (i, 0, 0)),
            column(up),
            still(*rt.shape),
        ]
        + [column(block) for block in blocks],
        out_specs=[still(tokens, D), still(tokens, LANES), column(up)],
        scratch_shapes=[
            pltpu.VMEM((tokens, D), f32),
            pltpu.VMEM((tokens, LANES), f32),
            pltpu.VMEM((D, width), bf16),
        ],
    )
    return pl.pallas_call(
        functools.partial(query_back_kernel, places=places),
        grid_spec=spec,
        out_shape=[
            jax.ShapeDtypeStruct((tokens, D), f32),
            jax.ShapeDtypeStruct((tokens, LANES), f32),
            jax.ShapeDtypeStruct((LANES, QW), f32),
        ],
        compiler_params=params(1),
        cost_estimate=cost(2 * tokens * D * QW, D * QW * 2),
        name="query_back",
    )(info, dq, up, rt, *blocks)


LOG2E = math.log2(math.e)


PER_STEP = 2


def attend_kernel(l_ref, w_ref, u_ref, q_ref, mix_ref, lse_ref, kv_ref):
    wide = NOPE + VDIM
    w = w_ref[...].reshape(LATENT, PER_STEP * wide)
    both_kv = dot(l_ref[:, :LATENT], w) + dot(l_ref[:, LATENT:], u_ref[...])
    both_kv = both_kv.astype(bf16)
    kv_ref[...] = both_kv
    ones = jnp.ones((both_kv.shape[0], LANES), bf16)
    for i in range(PER_STEP):
        kv = both_kv[:, i * wide : (i + 1) * wide]
        keys = jnp.concatenate([kv[:, :NOPE], l_ref[:, LATENT:]], 1)
        values = jnp.concatenate([kv[:, NOPE:], ones], 1)
        scores = dot(q_ref[i], keys, NT)
        top = jnp.max(scores, axis=1, keepdims=True)
        weights = jnp.exp2((scores - top) * (SCALE * LOG2E)).astype(bf16)
        both = dot(weights, values)
        total = both[:, VDIM:]
        mix_ref[:, i * VDIM : (i + 1) * VDIM] = (both[:, :VDIM] / total).astype(bf16)
        lse = top * (SCALE * LOG2E) + jnp.log2(total)
        lse_ref[i] = lse.T[:8]


def folded(w_kvb, at):
    pieces, _, rows, width = w_kvb.shape
    wide = PER_STEP * (NOPE + VDIM)
    per = width // wide
    return pl.BlockSpec(
        (pieces, 1, rows, wide), lambda h, *s: (0, (at + h) // per, 0, (at + h) % per)
    )


def attend(l_all, w_kvb, u_kvb, q):
    length = l_all.shape[0]
    tokens = q.shape[1]
    wide = NOPE + VDIM
    column = lambda n, w: pl.BlockSpec((n, PER_STEP * w), lambda h: (0, h))
    head = lambda *shape: pl.BlockSpec((PER_STEP,) + shape, lambda h: (h, 0, 0))
    return pl.pallas_call(
        attend_kernel,
        grid=(HEADS // PER_STEP,),
        in_specs=[
            pl.BlockSpec((length, LW), lambda h: (0, 0)),
            folded(w_kvb, 0),
            column(LANES, wide),
            head(tokens, 2 * LANES),
        ],
        out_specs=[column(tokens, VDIM), head(8, tokens), column(length, wide)],
        out_shape=[
            jax.ShapeDtypeStruct((tokens, HEADS * VDIM), bf16),
            jax.ShapeDtypeStruct((HEADS, 8, tokens), f32),
            jax.ShapeDtypeStruct((length, HEADS * wide), bf16),
        ],
        compiler_params=params(1),
        cost_estimate=cost(HEADS * 2 * length * (LW * 256 + tokens * 512), 8e6),
        name="attend",
    )(l_all, w_kvb, u_kvb, q)


def attend_back_kernel(
    info,
    l_ref,
    lt_ref,
    w_ref,
    u_ref,
    kv_ref,
    q_ref,
    lse_ref,
    delta_ref,
    dm_ref,
    cos_ref,
    sin_ref,
    was_ref,
    dq_ref,
    dl_ref,
    du_ref,
    acc,
):
    h = pl.program_id(0)
    wide = NOPE + VDIM
    count = info.shape[0] - 1
    rows = acc.shape[0] // count
    at = lambda k: pl.ds(pl.multiple_of(info[k] * rows, rows), rows)

    @pl.when(h == 0)
    def _():
        if len(was_ref.shape) == 3:
            for k in range(count):
                acc[at(k), :] = was_ref[k].astype(f32)
        else:
            acc[...] = jnp.zeros_like(acc)

    dkvs, drope = [], 0.0
    for i in range(PER_STEP):
        kv = kv_ref[:, i * wide : (i + 1) * wide]
        keys = jnp.concatenate([kv[:, :NOPE], l_ref[:, LATENT:]], 1)
        values = kv[:, NOPE:]
        dm = dm_ref[:, i * VDIM : (i + 1) * VDIM]
        scores = dot(keys, q_ref[i], NT)
        probs = jnp.exp2(scores * (SCALE * LOG2E) - lse_ref[i, :1])
        dvalues = dot(probs.astype(bf16), dm)
        dprobs = dot(values, dm, NT)
        dscores = (probs * (dprobs - delta_ref[i, :1])).astype(bf16)
        dq = dot(dscores, keys, TN) * SCALE
        lane = lax.broadcasted_iota(jnp.int32, (dq.shape[0], LANES), 1)
        rope = dq[:, LANES:]
        rope = rope * cos_ref[...] + unrotate_pair(lane, rope) * sin_ref[...]
        dq_ref[i] = jnp.concatenate([dq[:, :LANES], rope], 1).astype(bf16)
        dkeys = dot(dscores, q_ref[i]) * SCALE
        dkvs += [dkeys[:, :NOPE].astype(bf16), dvalues.astype(bf16)]
        drope += dkeys[:, NOPE:]
    dkv = jnp.concatenate(dkvs, 1)
    w = w_ref[...].reshape(LATENT, PER_STEP * wide)
    acc[:, :LATENT] += dot(dkv, w, NT)
    acc[:, LATENT:] += dot(dkv, u_ref[...], NT) + drope
    du_ref[...] = dot(lt_ref[...], dkv)

    @pl.when(h == pl.num_programs(0) - 1)
    def _():
        for k in range(count):
            dl_ref[k] = acc[at(k), :].astype(bf16)


def attend_back(info, part, l_all, lt, w_kvb, u_kvb, kv, q, lse, delta, dmix, cos, sin, was):
    length = l_all.shape[0]
    tokens = q.shape[1]
    wide = NOPE + VDIM
    heads = HEADS // 2
    count = info.shape[0] - 1
    at = part * heads // PER_STEP
    still = lambda a: pl.BlockSpec(a.shape, lambda h, s: (0,) * a.ndim)
    column = lambda n, w: pl.BlockSpec((n, PER_STEP * w), lambda h, s: (0, at + h))
    head = lambda *shape: pl.BlockSpec((PER_STEP,) + shape, lambda h, s: (at + h, 0, 0))
    spec = pltpu.PrefetchScalarGridSpec(
        num_scalar_prefetch=1,
        grid=(heads // PER_STEP,),
        in_specs=[
            still(l_all),
            still(lt),
            folded(w_kvb, at),
            column(LANES, wide),
            column(length, wide),
            head(tokens, 2 * LANES),
            head(8, tokens),
            head(8, tokens),
            column(tokens, VDIM),
            still(cos),
            still(sin),
            still(was),
        ],
        out_specs=[
            pl.BlockSpec((PER_STEP, tokens, 2 * LANES), lambda h, s: (h, 0, 0)),
            pl.BlockSpec((count, length // count, LW), lambda h, s: (0, 0, 0)),
            pl.BlockSpec((LANES, PER_STEP * wide), lambda h, s: (0, h)),
        ],
        scratch_shapes=[pltpu.VMEM((length, LW), f32)],
    )
    return pl.pallas_call(
        attend_back_kernel,
        grid_spec=spec,
        out_shape=[
            jax.ShapeDtypeStruct((heads, tokens, 2 * LANES), bf16),
            jax.ShapeDtypeStruct((count, length // count, LW), bf16),
            jax.ShapeDtypeStruct((LANES, heads * wide), f32),
        ],
        compiler_params=params(1),
        cost_estimate=cost(heads * 2 * length * (LW * 256 + tokens * 1024), 30e6),
        name="attend_back",
    )(info, l_all, lt, w_kvb, u_kvb, kv, q, lse, delta, dmix, cos, sin, was)


def picks(slot_row, slots):
    row = lax.broadcasted_iota(jnp.int32, (slots, slot_row.shape[1]), 0)
    return jnp.where(row == slot_row, 1.0, 0.0).astype(bf16)


def silu_parts(gate):
    sig = 1.0 / (1.0 + jnp.exp(-gate))
    return gate * sig, sig * (1.0 + gate * (1.0 - sig))


def router_probs(logits, experts):
    lane = lax.broadcasted_iota(jnp.int32, logits.shape, 1)
    logits = jnp.where(lane < experts, logits, -1e30)
    odds = jnp.exp(logits - jnp.max(logits, axis=1, keepdims=True))
    return odds / jnp.sum(odds, axis=1, keepdims=True)


def routed_kernel(info, slot_ref, wr_ref, w_in, w_out, *rest, offs, slots, wide, experts):
    chunks, count = len(offs), info.shape[0] - 1
    x_refs, g_refs = rest[:chunks], rest[chunks : 2 * chunks]
    y_ref, dx_ref, pull_ref, rows, grads, hidden, dacts = rest[2 * chunks :]
    e = pl.program_id(0)
    ff = w_out.shape[1]
    weights = []
    for c in range(chunks):
        pick = picks(slot_ref[info[1 + offs[c] % count], pl.ds(e, 1), :], slots)
        at = pl.ds(c * slots, slots)
        x = dot(pick, x_refs[c][...]).astype(bf16)
        rows[at, :] = x
        weight = router_probs(dot(x, wr_ref[...]), experts)
        lane = lax.broadcasted_iota(jnp.int32, weight.shape, 1)
        weight = jnp.sum(jnp.where(lane == info[0] + e, weight, 0.0), axis=1, keepdims=True)
        weights.append(weight)
        grads[at, :] = (dot(pick, g_refs[c][...]) * weight).astype(bf16)
    weight = jnp.concatenate(weights, 0)
    for a in range(0, ff, wide):
        b = min(a + wide, ff)
        gate = dot(rows[...], w_in[0, :, a:b])
        up = dot(rows[...], w_in[0, :, ff + a : ff + b])
        dhid = dot(grads[...], w_out[0, a:b, :], NT)
        silu, slope = silu_parts(gate)
        hidden[:, a:b] = (silu * up).astype(bf16)
        dacts[:, a:b] = (dhid * up * slope).astype(bf16)
        dacts[:, ff + a : ff + b] = (dhid * silu).astype(bf16)
    pull = jnp.zeros((rows.shape[0], 1), f32)
    step = 2 * wide
    for a in range(0, D, step):
        y = dot(hidden[...], w_out[0, :, a : a + step])
        pull += jnp.sum(y * grads[:, a : a + step].astype(f32), axis=1, keepdims=True)
        y_ref[0, :, a : a + step] = (y * weight).astype(bf16)
        dx_ref[0, :, a : a + step] = dot(dacts[...], w_in[0, a : a + step, :], NT).astype(bf16)
    lane = lax.broadcasted_iota(jnp.int32, (rows.shape[0], LANES), 1)
    pull_ref[0] = jnp.where(lane == info[0] + e, pull, 0.0).astype(bf16)


def routed(info, offs, xs, gs, slot_all, w_router, experts, w_in, w_out):
    chunks, tokens = len(xs), xs[0].shape[0]
    local = w_in.shape[0]
    ff = w_out.shape[1]
    slots = tokens // 2
    rows = chunks * slots
    once = pl.Buffered(1)
    whole = lambda a: pl.BlockSpec(a.shape, lambda e, s: (0,) * a.ndim, pipeline_mode=once)
    out = pl.BlockSpec((1, rows, D), lambda e, s: (e, 0, 0))
    spec = pltpu.PrefetchScalarGridSpec(
        num_scalar_prefetch=1,
        grid=(local,),
        in_specs=[
            whole(slot_all),
            whole(w_router),
            pl.BlockSpec((1, D, 2 * ff), lambda e, s: (e, 0, 0)),
            pl.BlockSpec((1, ff, D), lambda e, s: (e, 0, 0)),
        ]
        + [whole(v) for v in (*xs, *gs)],
        out_specs=[out, out, pl.BlockSpec((1, rows, LANES), lambda e, s: (e, 0, 0))],
        scratch_shapes=[
            pltpu.VMEM((rows, D), bf16),
            pltpu.VMEM((rows, D), bf16),
            pltpu.VMEM((rows, ff), bf16),
            pltpu.VMEM((rows, 2 * ff), bf16),
        ],
    )
    shape = jax.ShapeDtypeStruct((local, rows, D), bf16)
    return pl.pallas_call(
        functools.partial(
            routed_kernel, offs=offs, slots=slots, wide=2 * LANES, experts=experts
        ),
        grid_spec=spec,
        out_shape=[shape, shape, jax.ShapeDtypeStruct((local, rows, LANES), bf16)],
        compiler_params=params(1),
        cost_estimate=cost(local * rows * D * ff * 12, local * D * ff * 6),
        name="routed",
    )(info, slot_all, w_router, w_in, w_out, *xs, *gs)


def shared_kernel(
    info,
    slot_ref,
    y_ref,
    dx_ref,
    pull_ref,
    wi_ref,
    wo_ref,
    u_ref,
    dn_ref,
    *rest,
    offs,
    slots,
    experts,
):
    blocks = rest[:-8]
    out_ref, dout_ref, gu_up_ref, gu_down_ref, dn_up_ref, dn_down_ref, x_ref, g_ref = rest[-8:]
    c = pl.program_id(0)
    chunks, count = len(offs), info.shape[0] - 1
    spot = sum(jnp.where(c == i, off % count, 0) for i, off in enumerate(offs))
    owner = info[1 + spot]
    for i in range(chunks):

        @pl.when(c == i)
        def _(i=i):
            x_ref[...] = blocks[i][...]
            g_ref[...] = blocks[chunks + i][...]

    local = y_ref.shape[0]
    half = dn_ref.shape[0]
    x, g = x_ref[...], g_ref[...]
    proj = dot(x, wi_ref[...])
    r = proj[:, 2 * half :].astype(bf16)
    prob = router_probs(proj[:, 2 * half :], experts)
    acts = proj[:, : 2 * half] + dot(r, u_ref[...])
    gate, up = acts[:, :half], acts[:, half:]
    silu, slope = silu_parts(gate)
    inner = (silu * up).astype(bf16)
    rdn = dot(inner, dn_ref[...]).astype(bf16)
    back = dot(g, wo_ref[...], NT)
    drdn = back[:, half:].astype(bf16)
    dinner = back[:, :half] + dot(drdn, dn_ref[...], NT)
    dboth = jnp.concatenate([dinner * up * slope, dinner * silu], 1).astype(bf16)
    dr = dot(dboth, u_ref[...], NT)

    pick = jnp.concatenate([picks(slot_ref[owner, e : e + 1, :], slots) for e in range(local)], 0)
    rows = lambda ref: jnp.concatenate([ref[e] for e in range(local)], 0)
    out = dot(jnp.concatenate([inner, rdn], 1), wo_ref[...]) + dot(pick, rows(y_ref), TN)
    out_ref[0] = out.astype(bf16)
    pulls = dot(pick, rows(pull_ref), TN)
    dlogit = pulls - prob * jnp.sum(pulls, axis=1, keepdims=True)
    dsmall = (dr + dlogit).astype(bf16)
    dx = dot(jnp.concatenate([dboth, dsmall], 1), wi_ref[...], NT)
    dout_ref[0] = (dx + dot(pick, rows(dx_ref), TN)).astype(bf16)

    @pl.when(c == 0)
    def _():
        gu_up_ref[...] = jnp.zeros_like(gu_up_ref)
        gu_down_ref[...] = jnp.zeros_like(gu_down_ref)
        dn_up_ref[...] = jnp.zeros_like(dn_up_ref)
        dn_down_ref[...] = jnp.zeros_like(dn_down_ref)

    gu_up_ref[...] += dot(r, dboth, TN)
    gu_down_ref[...] += dot(dr.astype(bf16), x, TN)
    dn_up_ref[...] += dot(rdn, g, TN)
    dn_down_ref[...] += dot(drdn, inner, TN)


def shared(info, offs, xs, gs, slot_all, experts, y, dx, pull, wi, wo, u, dn):
    chunks, tokens = len(xs), xs[0].shape[0]
    local = y.shape[0]
    slots = tokens // 2
    half = dn.shape[0]
    whole = lambda a: pl.BlockSpec(a.shape, lambda c, s: (0,) * a.ndim)
    one = pl.BlockSpec((1, tokens, D), lambda c, s: (c, 0, 0))
    rows = lambda a: pl.BlockSpec((local, slots, a.shape[2]), lambda c, s: (0, c, 0))
    still = lambda *shape: pl.BlockSpec(shape, lambda c, s: (0, 0))
    operands = [slot_all, y, dx, pull, wi, wo, u, dn, *xs, *gs]
    specs = [whole(slot_all), rows(y), rows(dx), rows(pull)]
    specs += [whole(a) for a in operands[4:]]
    spec = pltpu.PrefetchScalarGridSpec(
        num_scalar_prefetch=1,
        grid=(chunks,),
        in_specs=specs,
        out_specs=[
            one,
            one,
            still(LANES, 2 * half),
            still(LANES, D),
            still(LANES, D),
            still(LANES, half),
        ],
        scratch_shapes=[pltpu.VMEM((tokens, D), bf16)] * 2,
    )
    return pl.pallas_call(
        functools.partial(shared_kernel, offs=offs, slots=slots, experts=experts),
        grid_spec=spec,
        out_shape=[
            jax.ShapeDtypeStruct((chunks, tokens, D), bf16),
            jax.ShapeDtypeStruct((chunks, tokens, D), bf16),
            jax.ShapeDtypeStruct((LANES, 2 * half), f32),
            jax.ShapeDtypeStruct((LANES, D), f32),
            jax.ShapeDtypeStruct((LANES, D), f32),
            jax.ShapeDtypeStruct((LANES, half), f32),
        ],
        compiler_params=params(1),
        cost_estimate=cost(chunks * 4e9, chunks * 8e6),
        name="shared",
    )(info, *operands)


def rms_scale(v):
    return lax.rsqrt(jnp.mean(v * v, axis=-1, keepdims=True) + EPS)


def rms_back(v, scale, gain, dy):
    unit = v * scale
    gdy = gain * dy
    return (gdy - unit * jnp.mean(unit * gdy, axis=-1, keepdims=True)) * scale


def angles(positions):
    half = ROPE // 2
    ladder = jnp.arange(half).astype(f32)
    frequency = jnp.exp(ladder * (-2.0 * math.log(10000.0) / ROPE))
    turn = positions.astype(f32)[:, None] * frequency[None, :]
    return jnp.cos(turn), jnp.sin(turn)


def pad_lanes(v, width, before=0):
    return jnp.pad(v, ((0, 0), (before, width - before - v.shape[1])))


def pad_rows(v, height, before=0):
    return jnp.pad(v, ((before, height - before - v.shape[0]), (0, 0)))


def round_up(n, m):
    return -(-n // m) * m


def pack(parts, unit=LANES):
    return jnp.concatenate([pad_lanes(v, round_up(v.shape[1], unit)) for v in parts], 1)


def unpack(v, widths, unit=LANES):
    out, at = [], 0
    for w in widths:
        out.append(v[:, at : at + w])
        at += round_up(w, unit)
    return out


class Totals:
    def __init__(self, parts, shards):
        self.shards = shards
        self.widths = [v.shape[1] for v in parts]
        packed = pack(parts)
        self.columns = round_up(packed.shape[1], shards * LANES)
        packed = pad_lanes(packed, self.columns).astype(bf16)
        self.cut = self.columns // shards
        self.packed = packed.reshape(RANK, shards, self.cut).transpose(1, 0, 2)

    def deal(self):
        mine = lax.all_to_all(self.packed, "shard", split_axis=0, concat_axis=0, tiled=True)
        self.mine = jnp.sum(mine.astype(f32), axis=0).astype(bf16)
        return self.mine

    def gather(self, ids):
        seqs = lax.all_gather(self.mine, "replica", axis=0)
        chosen = (ids[None, :] == jnp.arange(ADAPTERS)[:, None]).astype(f32)
        sums = jnp.sum(chosen[:, :, None, None] * seqs.astype(f32)[None], axis=1).astype(bf16)
        self.sums = sums.reshape(self.shards, ADAPTERS // self.shards, RANK, self.cut)
        return self.sums

    def home(self):
        full = lax.all_to_all(self.sums, "shard", split_axis=0, concat_axis=0, tiled=True)
        full = full.transpose(1, 2, 0, 3).reshape(ADAPTERS // self.shards, RANK, self.columns)
        out, at = [], 0
        for w in self.widths:
            out.append(full[:, :, at : at + w].astype(f32))
            at += round_up(w, LANES)
        return out


def body(
    hidden_in,
    out_grad,
    routes,
    seq_adapter,
    attn_gain,
    latent_gain,
    ffn_gain,
    w_qa,
    w_kvb,
    w_out,
    w_router,
    w_shared_in,
    w_shared_out,
    w_expert_in,
    w_expert_out,
    qa_down,
    qa_up,
    kvb_down,
    kvb_up,
    out_down,
    out_up,
    gu_down,
    gu_up,
    dn_down,
    dn_up,
):
    shards = lax.axis_size("shard")
    replicas = lax.axis_size("replica")
    place = lax.axis_index("shard")
    tokens = hidden_in.shape[0]
    local = w_expert_in.shape[0]
    experts = local * shards
    ring = Ring(shards)
    adapter_id = seq_adapter[0]
    core = (lax.axis_index("replica") % 2).astype(jnp.int32)
    spots = jnp.concatenate([ring.owners, core.reshape(1)])
    ids = lax.all_gather(seq_adapter, "replica", axis=0, tiled=True)
    first = (place * local).astype(jnp.int32).reshape(1)

    tables = [qa_down, qa_up[:, :, :QW], qa_up[:, :, QW:], kvb_down, kvb_up, out_down, out_up]
    tables = [t[0] for t in tables + [gu_down, gu_up, dn_down, dn_up]]
    dealt = pack(tables)
    cut = round_up(dealt.shape[1], shards * LANES) // shards
    dealt = pad_lanes(dealt, cut * shards).reshape(RANK, shards, cut).transpose(1, 0, 2)
    dealt = lax.all_to_all(dealt, "shard", split_axis=0, concat_axis=0, tiled=True)
    dealt = lax.dynamic_index_in_dim(dealt, adapter_id, 0, keepdims=True)
    dealt = jnp.broadcast_to(dealt, (shards, RANK, cut))
    dealt = lax.all_to_all(dealt, "shard", split_axis=0, concat_axis=0, tiled=True)
    dealt = dealt.transpose(1, 0, 2).reshape(RANK, shards * cut)
    a_qd, a_quq, a_qul, a_kd, a_ku, a_od, a_ou, a_gd, a_gu, a_nd, a_nu = unpack(
        dealt, [t.shape[1] for t in tables]
    )

    kvb_rows, fold, kvb_wide, own_weights = pack_weights(core, w_qa, w_kvb, w_out, replicas)
    w_walk = Walk(ring, own_weights)
    w_swaps = Swaps(ring, w_walk, replicas)
    w1 = w_walk.hop()
    own_swap = w_swaps.swap(w_walk.own)
    w2 = w_walk.hop(*own_swap)
    width = w_shared_out.shape[0]
    half = round_up(width, LANES)
    rows_in = w_shared_in.shape[0]
    if replicas % 2 == 0:
        core = lax.axis_index("replica") % 2
    mine = own_share(w_shared_in, replicas, zero_after(*w1))
    mine = mine.reshape(mine.shape[0], 2, shards, width).transpose(2, 0, 1, 3)
    mine = jnp.pad(mine, ((0, 0), (0, 0), (0, 0), (0, half - width)))
    mine = mine.reshape(shards, mine.shape[1], 2 * half)
    ready = mine
    inputs = hidden_in.astype(f32)
    in_scale = rms_scale(inputs)
    hb = (inputs * in_scale * attn_gain).astype(bf16)
    swap1 = w_swaps.swap(w_walk.pairs[0])
    w3 = w_walk.hop(*swap1, ready, hb)
    swap2 = w_swaps.swap(w_walk.pairs[1])
    w4 = w_walk.hop(*swap2, ids)
    u_q = pad_rows(a_quq, LANES)
    u_kvb = pad_rows(a_ku, LANES, ROPE)
    wr = pad_lanes(w_router, LANES)
    r_qa = dot(hb, a_qd, NT).astype(bf16)
    w_swaps.swap(w_walk.pairs[2])
    w_swaps.swap(w_walk.halves)
    w_at, w_blocks = w_swaps.rows(0, w_out.shape[0])
    kvb_at, out_at, lat_at = QW, QW + kvb_wide, QW + kvb_wide + D
    w_lat = place_rows(spots, w_at, w_blocks, D, lat_at, LW, LANES)[:, : LATENT + ROPE]
    full_kvb = place_rows(spots, w_at, w_blocks, D, kvb_at, kvb_wide, kvb_wide)
    full_kvb = full_kvb.reshape(LATENT // kvb_rows, fold, kvb_rows, kvb_wide)
    full_out = place_rows(spots, w_at, w_blocks, D, out_at, D, D // 2)

    lat_raw = dot(hb, w_lat) + dot(r_qa, a_qul)
    latent_raw, rope_raw = lat_raw[:, :LATENT], lat_raw[:, LATENT:]
    lat_scale = rms_scale(latent_raw)
    latent = (latent_raw * lat_scale * latent_gain).astype(bf16)
    positions = place * tokens + jnp.arange(tokens)
    cos_half, sin_half = angles(positions)
    rh = ROPE // 2
    rope_a, rope_b = rope_raw[:, :rh], rope_raw[:, rh:]
    rope = jnp.concatenate(
        [rope_a * cos_half - rope_b * sin_half, rope_b * cos_half + rope_a * sin_half], 1
    ).astype(bf16)
    r_kv = dot(latent, a_kd, NT).astype(bf16)
    l_own = jnp.concatenate([latent, rope, r_kv, routes.astype(bf16)], 1)
    l_own = pad_lanes(l_own, LW)
    l_walk = Walk(ring, l_own)
    l_walk.hop()
    l_walk.hop(full_out)
    l3 = l_walk.hop(full_kvb)
    l4 = l_walk.hop(u_q, u_kvb)
    (hb_late,) = gate((hb,), l3)
    g_walk = Walk(ring, out_grad)
    g1 = g_walk.hop(*l4)
    (mine,) = gate((ready,), l4)
    mine = lax.all_to_all(mine, "shard", split_axis=0, concat_axis=0, tiled=True)
    if replicas % 2 == 0:
        other = pair_swap(mine, replicas)
        w_si = jnp.concatenate(
            [jnp.where(core == 0, mine, other), jnp.where(core == 0, other, mine)], 1
        )
    else:
        w_si = mine
    w_si = w_si.reshape(shards * rows_in, 2 * half)

    w_i = jnp.concatenate([w_si, pad_lanes(jnp.concatenate([w_router, a_gd.T], 1), LANES)], 1)
    w_o = jnp.concatenate([pad_rows(w_shared_out, half), pad_rows(a_nu, LANES)], 0)
    gu_g = lax.dynamic_slice_in_dim(a_gu, place * width, width, 1)
    gu_u = lax.dynamic_slice_in_dim(a_gu, shards * width + place * width, width, 1)
    u_gu = jnp.concatenate([pad_lanes(gu_g, half), pad_lanes(gu_u, half)], 1)
    u_gu = pad_rows(u_gu, LANES, experts)
    nd_own = lax.dynamic_slice_in_dim(a_nd, place * width, width, 1)
    dn_own = pad_rows(pad_lanes(nd_own.T, LANES), half)

    l_all = all_latents(spots, l_walk.blocks(), tokens)
    cos = pad_lanes(jnp.concatenate([cos_half, cos_half], 1), LANES)
    sin = pad_lanes(jnp.concatenate([sin_half, sin_half], 1), LANES)
    q = query_heads(
        spots, hb_late, pad_lanes(r_qa, LANES), w_at, w_blocks, u_q, cos, sin
    )

    mixture, lse, kv = attend(l_all, full_kvb, u_kvb, q)
    (mixture,) = gate((mixture,), g1)
    r_out = dot(mixture, a_od, NT).astype(bf16)
    after_attn = inputs + dot(mixture, full_out) + dot(r_out, a_ou)
    ffn_scale = rms_scale(after_attn)
    ffn_low = (after_attn * ffn_scale * ffn_gain).astype(bf16)

    at = LATENT + ROPE + RANK
    routes_all = l_all[:, at : at + TOPK].astype(jnp.int32).reshape(shards, tokens, TOPK)
    wanted = first[0] + jnp.arange(local)
    mask = jnp.any(routes_all[:, None, :, :] == wanted[None, :, None, None], axis=-1)
    before = jnp.triu(jnp.ones((tokens, tokens), bf16), 1)
    rank = lax.dot_general(
        mask.astype(bf16), before, (((2,), (0,)), ((), ())), preferred_element_type=f32
    )
    slot_all = jnp.where(mask, rank.astype(jnp.int32), -1)

    out_piece, dx_piece, small = {}, {}, []


    info = jnp.concatenate([first, ring.owners])

    def run_routed(members, *after):
        offs, xs, gs = ([m[i] for m in members] for i in range(3))
        if after:
            xs = gate(xs, after)
        return offs, xs, gs, *routed(
            info, offs, xs, gs, slot_all, wr, experts, w_expert_in, w_expert_out
        )

    def run_shared(offs, xs, gs, y, dxr, pull):
        out, dx, *grads = shared(
            info, offs, xs, gs, slot_all, experts, y, dxr, pull, w_i, w_o, u_gu, dn_own
        )
        small.append(grads)
        for i, off in enumerate(offs):
            out_piece[off], dx_piece[off] = out[i], dx[i]
        return grads[-1]

    far = shards // 2
    walk = Walk(ring, ffn_low)
    members = lambda h: [
        (off, x, g) for off, x, g in zip((-h, h), walk.pairs[h - 1], g_walk.pairs[h - 1])
    ]
    x1 = walk.hop()
    done = run_routed([(0, ffn_low, out_grad)])
    walk.hop(done[3])
    g_walk.hop(*x1)
    mark = run_shared(*done)
    done = run_routed(members(1), mark)
    x3 = walk.hop(done[3])
    g_walk.hop(*walk.pairs[1])
    mark = run_shared(*done)
    done = run_routed(members(2), mark)
    walk.hop(done[3])
    g_walk.hop(*walk.pairs[2])
    mark = run_shared(*done)
    opposite = (far, jnp.concatenate(walk.halves, 0), jnp.concatenate(g_walk.halves, 0))
    run_shared(*run_routed(members(3) + [opposite], mark))
    out_piece[-far], dx_piece[-far] = out_piece[far], dx_piece[far]
    small = [sum(parts[1:], parts[0]) for parts in zip(*small)]

    def spread(v, cols):
        return jnp.concatenate(
            [
                lax.dynamic_update_slice_in_dim(
                    jnp.zeros((RANK, cols), f32), part, place * width, 1
                )
                for part in v
            ],
            1,
        )

    g_gu_up = small[0][experts : experts + RANK]
    g_gu_up = spread([g_gu_up[:, :width], g_gu_up[:, half : half + width]], shards * width)
    g_gu_down = small[1][experts : experts + RANK]
    g_dn_up = small[2][:RANK]
    g_dn_down = spread([small[3][:RANK, :width]], shards * width)

    seen = {}
    ffn_grad = ring.scatter_sum(lambda off: dx_piece[off], {})

    d_after = out_grad.astype(f32) + rms_back(after_attn, ffn_scale, ffn_gain, ffn_grad)
    d_after_low = d_after.astype(bf16)
    dr_out = dot(d_after_low, a_ou, NT).astype(bf16)
    dmix = (dot(d_after_low, full_out, NT) + dot(dr_out, a_od)).astype(bf16)
    g_out_up = dot(r_out, d_after_low, TN)
    g_out_down = dot(dr_out, mixture, TN)
    delta = (dmix.astype(f32) * mixture.astype(f32)).reshape(tokens, HEADS, VDIM).sum(-1).T
    delta = jnp.broadcast_to(delta[:, None, :], (HEADS, 8, tokens))
    lt = l_all[:, LATENT:].T
    parts = []

    def back(*marks):
        was = parts[-1][1] if parts else jnp.zeros((8, LANES), bf16)
        (marked,) = gate((lse,), marks) if not parts else gate((lse + 0.0,), marks)
        parts.append(
            attend_back(
                spots, len(parts), l_all, lt, full_kvb, u_kvb, kv, q, marked, delta, dmix, cos, sin, was
            )
        )
        return (parts[-1][2],)

    def first_arrived(r, l):
        seen["far"] = (r[:16], l[:16])
        return ()

    def next_arrived(r, l):
        seen["next"] = (r[:16], l[:16])
        return back(*seen["far"])

    def last_arrived(r, l):
        back(*seen["next"])
        dl = parts[-1][1]
        seen["dl"] = ring.scatter_sum(
            lambda off: dl[off % shards],
            {far - 2: query_grads, far - 3: dl_arrived},
        )
        return seen["dl near"]

    def query_grads(r, l):
        dq = jnp.concatenate([part[0] for part in parts], 0)
        seen["q"] = query_back(spots, dq, w_at, w_blocks, u_q, pad_lanes(r_qa, LANES).T)
        return (seen["q"][1],)

    def dl_arrived(r, l):
        seen["dl near"] = (r[:16], l[:16])
        return ()

    out_sum = ring.scatter_sum(
        lambda off: out_piece[off],
        {
            far: lambda: (ffn_grad,),
            far - 1: first_arrived,
            far - 2: next_arrived,
            far - 3: last_arrived,
        },
    )
    block_out = (after_attn + out_sum).astype(bf16)
    g_ku = jnp.concatenate([part[2] for part in parts], 1)
    g_kvb_up = g_ku[ROPE : ROPE + RANK]
    dhb_q, dr_q, g_qu = seen["q"]
    dl_own = seen["dl"]
    dr_kv = dl_own[:, LATENT + ROPE : LATENT + ROPE + RANK].astype(bf16)
    d_latent = dl_own[:, :LATENT] + dot(dr_kv, a_kd)
    g_kvb_down = dot(dr_kv, latent, TN)
    d_latent = rms_back(latent_raw, lat_scale, latent_gain, d_latent)
    drope = dl_own[:, LATENT : LATENT + ROPE]
    drope_a, drope_b = drope[:, :rh], drope[:, rh:]
    drope = jnp.concatenate(
        [drope_a * cos_half + drope_b * sin_half, drope_b * cos_half - drope_a * sin_half], 1
    )
    d_lat = jnp.concatenate([d_latent, drope], 1).astype(bf16)
    dr_qa = (dr_q[:, :RANK] + dot(d_lat, a_qul, NT)).astype(bf16)
    dhb = dhb_q + dot(d_lat, w_lat, NT) + dot(dr_qa, a_qd)
    g_qa_up = jnp.concatenate([g_qu[:RANK], dot(r_qa, d_lat, TN)], 1)
    g_qa_down = dot(dr_qa, hb, TN)
    hidden_grad = d_after + rms_back(inputs, in_scale, attn_gain, dhb)

    t_attn = Totals(
        [g_qa_down, g_qa_up, g_kvb_down, g_kvb_up, g_out_down, g_out_up]
        + [g_gu_down, g_gu_up, g_dn_down, g_dn_up],
        shards,
    )
    t_attn.deal()
    t_attn.gather(ids)
    return (block_out, hidden_grad, *t_attn.home())


def solution(mesh):
    rows = P(("replica", "shard"), None)
    cut2 = P("shard", None)
    cut3 = P("shard", None, None)
    in_specs = (
        (rows, rows, rows, P("replica"), P(), P(), P())
        + (cut2, cut2, cut2, P(), cut2, cut2, cut3, cut3)
        + (cut3,) * 10
    )
    out_specs = (rows, rows) + (cut3,) * 10
    return jax.shard_map(body, mesh=mesh, in_specs=in_specs, out_specs=out_specs, check_vma=False)
```

```python
import functools
import math

import jax
import jax.numpy as jnp
from jax import lax
from jax.experimental import pallas as pl
from jax.experimental.pallas import tpu as pltpu
from jax.sharding import PartitionSpec as P

D = 2048
HEADS = 16
NOPE = 128
ROPE = 64
VDIM = 128
LATENT = 512
TOPK = 6
RANK = 16
ADAPTERS = 8
BLOCK = 256
QW = HEADS * (NOPE + ROPE)
LW = LATENT + 2 * ROPE
LANES = 128
VMEM_LIMIT = 60 * 1024 * 1024
SCALE = (NOPE + ROPE) ** (-0.5)
EPS = 1e-06
f32 = jnp.float32
bf16 = jnp.bfloat16

NN = (((1,), (0,)), ((), ()))
NT = (((1,), (1,)), ((), ()))
TN = (((0,), (0,)), ((), ()))


def dot(a, b, dims=NN):
    return lax.dot_general(a, b, dims, preferred_element_type=f32)


def params(n):
    return pltpu.CompilerParams(
        dimension_semantics=("arbitrary",) * n, vmem_limit_bytes=VMEM_LIMIT
    )


def cost(flops, nbytes):
    return pl.CostEstimate(flops=int(flops), bytes_accessed=int(nbytes), transcendentals=0)


def gate_kernel(*refs):
    del refs


def gate(values, marks):
    anywhere = pl.BlockSpec(memory_space=pl.ANY)
    values, marks = tuple(values), tuple(marks)
    return pl.pallas_call(
        gate_kernel,
        in_specs=[anywhere] * len(values + marks),
        out_specs=[anywhere] * len(values),
        out_shape=[jax.ShapeDtypeStruct(v.shape, v.dtype) for v in values],
        input_output_aliases={i: i for i in range(len(values))},
        cost_estimate=cost(0, 0),
        name="gate",
    )(*values, *marks)


def zero_kernel(*refs):
    refs[-1][0] = 0


def zero_after(*marks):
    anywhere = pl.BlockSpec(memory_space=pl.ANY)
    return pl.pallas_call(
        zero_kernel,
        in_specs=[anywhere] * len(marks),
        out_specs=pl.BlockSpec(memory_space=pltpu.SMEM),
        out_shape=jax.ShapeDtypeStruct((1,), jnp.int32),
        cost_estimate=cost(0, 0),
        name="zero_after",
    )(*marks)[0]


def ring_of(count):
    return list(range(0, count, 2)) + list(range(count - 1, 0, -2))


class Ring:
    def __init__(self, count):
        order = ring_of(count)
        place_of = [order.index(i) for i in range(count)]
        self.count = count
        pos = jnp.asarray(place_of, jnp.int32)[lax.axis_index("shard")]
        self.owners = jnp.asarray(order, jnp.int32)[(pos + jnp.arange(count)) % count]
        self.right = [(order[i], order[(i + 1) % count]) for i in range(count)]
        self.left = [(order[i], order[(i - 1) % count]) for i in range(count)]

    def owner(self, off):
        return self.owners[off % self.count]

    def send_right(self, v):
        return lax.ppermute(v, "shard", self.right)

    def send_left(self, v):
        return lax.ppermute(v, "shard", self.left)

    def scatter_sum(self, piece, holds):
        half = self.count // 2
        far = piece(half)
        n = far.shape[0] // 2
        r, l = far[:n], far[n:]
        if half in holds:
            r, l = gate((r, l), holds[half]())
        r, l = self.send_right(r), self.send_left(l)
        for h in range(half - 1, 0, -1):
            up, down = piece(h), piece(-h)
            if h in holds:
                r, l = gate((r, l), holds[h](r, l))
            if r.shape[0] == n:
                up = jnp.concatenate([up[:n].astype(f32) + r.astype(f32), up[n:].astype(f32)], 0)
                down = jnp.concatenate([down[:n].astype(f32), down[n:].astype(f32) + l.astype(f32)], 0)
            else:
                up = up.astype(f32) + r.astype(f32)
                down = down.astype(f32) + l.astype(f32)
            r, l = self.send_right(up.astype(bf16)), self.send_left(down.astype(bf16))
        return piece(0).astype(f32) + r.astype(f32) + l.astype(f32)


class Walk:
    def __init__(self, ring, *arrays):
        self.ring, self.own, self.pairs, self.halves = ring, list(arrays), [], None

    def hop(self, *marks):
        half, k = self.ring.count // 2, len(self.own)
        if self.pairs:
            held = gate(self.pairs[-1], marks)
            self.pairs[-1] = held
            r, l = held[:k], held[k:]
        else:
            if marks:
                self.own = gate(self.own, marks)
            r = l = self.own
        if len(self.pairs) < half - 1:
            right = [self.ring.send_right(v) for v in r]
            left = [self.ring.send_left(v) for v in l]
            self.pairs.append(right + left)
            return self.pairs[-1]
        right = [self.ring.send_right(v[: v.shape[0] // 2]) for v in r]
        left = [self.ring.send_left(v[v.shape[0] // 2 :]) for v in l]
        self.halves = right + left
        return self.halves

    def blocks(self, i=0):
        k = len(self.own)
        out = [(0, 0, self.own[i])]
        for h, pair in enumerate(self.pairs):
            out += [(-h - 1, 0, pair[i]), (h + 1, 0, pair[k + i])]
        far = self.ring.count // 2
        n = self.own[i].shape[0] // 2
        return out + [(far, 0, self.halves[i]), (far, n, self.halves[k + i])]


def pair_swap(v, replicas):
    return lax.ppermute(v, "replica", [(i, i ^ 1) for i in range(replicas)])


def fill_rows(info, places, blocks, out):
    count = info.shape[0] - 1
    for (off, n, row, half, other), block in zip(places, blocks):
        core = info[count]
        at = info[off % count] * n + row + half * (1 - core if other else core)
        out[pl.ds(pl.multiple_of(at, 16), block.shape[0]), :] = block[...]


def place_kernel(info, *refs, places):
    fill_rows(info, places, refs[:-1], refs[-1])


def place_rows(info, places, blocks, height, first=0, width=None, cut=None):
    width = width or blocks[0].shape[1]
    cut = cut or next((c for c in (2048, 1024) if width % c == 0 and height * c <= 1 << 21), width)
    at = first // cut
    spec = pltpu.PrefetchScalarGridSpec(
        num_scalar_prefetch=1,
        grid=(width // cut,),
        in_specs=[pl.BlockSpec((b.shape[0], cut), lambda i, s: (0, at + i)) for b in blocks],
        out_specs=pl.BlockSpec((height, cut), lambda i, s: (0, i)),
    )
    return pl.pallas_call(
        functools.partial(place_kernel, places=places),
        grid_spec=spec,
        out_shape=jax.ShapeDtypeStruct((height, width), blocks[0].dtype),
        compiler_params=params(1),
        cost_estimate=cost(0, height * width * 4),
        name="place_rows",
    )(info, *blocks)


def latents_kernel(info, *refs, places):
    blocks, out = refs[:-1], refs[-1]
    count = info.shape[0] - 1
    for (off, n, row, _, _), block in zip(places, blocks):
        rows = block.shape[0]
        at = pl.ds(pl.multiple_of(info[off % count] * n + row, 16), rows)
        hide = jnp.where(info[off % count] > info[0], -1e30, 0.0)
        lane = lax.broadcasted_iota(jnp.int32, (rows, LANES), 1)
        tail = jnp.where(lane == LANES - 1, hide, block[:, LATENT:].astype(f32))
        out[at, :LATENT] = block[:, :LATENT]
        out[at, LATENT:] = tail.astype(bf16)


def all_latents(info, blocks, n):
    places = [(off, n, row, 0, False) for off, row, _ in blocks]
    blocks = [v for _, _, v in blocks]
    height = (info.shape[0] - 1) * n
    spec = pltpu.PrefetchScalarGridSpec(
        num_scalar_prefetch=1,
        grid=(1,),
        in_specs=[pl.BlockSpec(b.shape, lambda i, s: (0, 0)) for b in blocks],
        out_specs=pl.BlockSpec((height, LW), lambda i, s: (0, 0)),
    )
    return pl.pallas_call(
        functools.partial(latents_kernel, places=places),
        grid_spec=spec,
        out_shape=jax.ShapeDtypeStruct((height, LW), bf16),
        compiler_params=params(1),
        cost_estimate=cost(0, height * LW * 4),
        name="all_latents",
    )(info, *blocks)


def whole_rows(info, blocks, n):
    places = [(off, n, row, 0, False) for off, row, _ in blocks]
    return place_rows(info, places, [v for _, _, v in blocks], (info.shape[0] - 1) * n)


def pack_kernel(core, qa_ref, kvb_ref, out_ref, all_ref, *, fold):
    del core
    rows, wide = kvb_ref.shape[0], kvb_ref.shape[1] // fold
    all_ref[:, :QW] = qa_ref[:, :QW]
    for i in range(fold):
        all_ref[i * rows : (i + 1) * rows, QW : QW + wide] = kvb_ref[:, i * wide : (i + 1) * wide]
    all_ref[:, QW + wide : QW + wide + D] = out_ref[...]
    rest = jnp.zeros((all_ref.shape[0], LW - LATENT - ROPE), all_ref.dtype)
    all_ref[:, QW + wide + D :] = jnp.concatenate([qa_ref[:, QW:], rest], 1)


def pack_weights(core, w_qa, w_kvb, w_out, replicas):
    parts = 2 if replicas % 2 == 0 else 1
    height, kvb_rows = w_out.shape[0] // parts, w_kvb.shape[0] // parts
    fold = height // kvb_rows
    wide = w_kvb.shape[1] // fold
    width = QW + wide + D + LW
    mine = (core % parts).reshape(1)
    share = lambda n, w: pl.BlockSpec((n, w.shape[1]), lambda i, s: (s[0], 0))
    spec = pltpu.PrefetchScalarGridSpec(
        num_scalar_prefetch=1,
        grid=(1,),
        in_specs=[share(height, w_qa), share(kvb_rows, w_kvb), share(height, w_out)],
        out_specs=pl.BlockSpec((height, width), lambda i, s: (0, 0)),
    )
    packed = pl.pallas_call(
        functools.partial(pack_kernel, fold=fold),
        grid_spec=spec,
        out_shape=jax.ShapeDtypeStruct((height, width), bf16),
        compiler_params=params(1),
        cost_estimate=cost(0, height * width * 4),
        name="pack_weights",
    )(mine, w_qa, w_kvb, w_out)
    return kvb_rows, fold, wide, packed


def own_share(w, replicas, zero=0):
    if replicas % 2:
        return w
    half = w.shape[0] // 2
    return lax.dynamic_slice_in_dim(w, lax.axis_index("replica") % 2 * half + zero, half, 0)


class Swaps:
    def __init__(self, ring, walk, replicas):
        self.ring, self.walk, self.replicas = ring, walk, replicas
        self.pairs = []

    def swap(self, blocks):
        got = [pair_swap(v, self.replicas) for v in blocks] if self.replicas % 2 == 0 else []
        self.pairs.append(got)
        return got

    def rows(self, i, n):
        walk, k = self.walk, len(self.walk.own)
        paired = self.replicas % 2 == 0
        far = self.ring.count // 2
        half = walk.own[i].shape[0] // 2
        got = [(0, 0, walk.own, i)]
        for h, pair in enumerate(walk.pairs):
            got += [(-h - 1, 0, pair, i), (h + 1, 0, pair, k + i)]
        got += [(far, 0, walk.halves, i), (far, half, walk.halves, k + i)]
        sets = [walk.own] + list(walk.pairs) + [walk.halves]
        places, out = [], []
        for off, row, blocks, j in got:
            where = next(m for m, v in enumerate(sets) if v is blocks)
            step = n // 2 if paired else 0
            places.append((off, n, row, step, False))
            out.append(blocks[j])
            if paired:
                places.append((off, n, row, step, True))
                out.append(self.pairs[where][j])
        return places, out


def rotate_pair(lane, v):
    half = ROPE // 2
    return jnp.where(lane < half, -pltpu.roll(v, LANES - half, 1), pltpu.roll(v, half, 1))


def unrotate_pair(lane, v):
    half = ROPE // 2
    return jnp.where(lane < half, pltpu.roll(v, LANES - half, 1), -pltpu.roll(v, half, 1))


def query_kernel(info, hb_ref, r_ref, up_ref, cos_ref, sin_ref, *rest, places):
    blocks, q_ref, w_ref = rest[:-2], rest[-2], rest[-1]
    fill_rows(info, places, blocks, w_ref)
    acc = dot(hb_ref[...], w_ref[...]) + dot(r_ref[...], up_ref[...])
    lane = lax.broadcasted_iota(jnp.int32, (acc.shape[0], LANES), 1)
    for i in range(2):
        own = acc if i == 0 else pltpu.roll(acc, NOPE + ROPE, 1)
        rope = own[:, LANES : 2 * LANES]
        turned = rope * cos_ref[...] + rotate_pair(lane, rope) * sin_ref[...]
        turned = jnp.where(lane == LANES - 1, 1.0, turned)
        q_ref[i] = jnp.concatenate([own[:, :LANES], turned], 1).astype(bf16)


def query_heads(info, hb, r, places, blocks, up, cos, sin):
    tokens = hb.shape[0]
    width = 2 * (NOPE + ROPE)
    whole = lambda a: pl.BlockSpec(a.shape, lambda i, s: (0,) * a.ndim)
    column = lambda a: pl.BlockSpec((a.shape[0], width), lambda i, s: (0, i))
    spec = pltpu.PrefetchScalarGridSpec(
        num_scalar_prefetch=1,
        grid=(HEADS // 2,),
        in_specs=[whole(hb), whole(r), column(up), whole(cos), whole(sin)]
        + [column(block) for block in blocks],
        out_specs=pl.BlockSpec((2, tokens, 2 * LANES), lambda i, s: (i, 0, 0)),
        scratch_shapes=[pltpu.VMEM((D, width), bf16)],
    )
    return pl.pallas_call(
        functools.partial(query_kernel, places=places),
        grid_spec=spec,
        out_shape=jax.ShapeDtypeStruct((HEADS, tokens, 2 * LANES), bf16),
        compiler_params=params(1),
        cost_estimate=cost(2 * tokens * D * QW, D * QW * 2),
        name="query_heads",
    )(info, hb, r, up, cos, sin, *blocks)


def query_back_kernel(info, dq_ref, up_ref, rt_ref, *rest, places):
    blocks = rest[:-6]
    dhb_ref, dr_ref, dup_ref, acc, racc, w_ref = rest[-6:]
    i = pl.program_id(0)
    tokens = dq_ref.shape[1]

    @pl.when(i == 0)
    def _():
        acc[...] = jnp.zeros_like(acc)
        racc[...] = jnp.zeros_like(racc)

    fill_rows(info, places, blocks, w_ref)
    pad = jnp.zeros((tokens, LANES), f32)
    first = jnp.concatenate([dq_ref[0].astype(f32), pad], 1)
    second = jnp.concatenate([dq_ref[1].astype(f32), pad], 1)
    both = (first + pltpu.roll(second, NOPE + ROPE, 1)).astype(bf16)
    acc[...] += dot(both, w_ref[...], NT)
    racc[...] += dot(both, up_ref[...], NT)
    dup_ref[...] = dot(rt_ref[...], both)

    @pl.when(i == pl.num_programs(0) - 1)
    def _():
        dhb_ref[...] = acc[...]
        dr_ref[...] = racc[...]


def query_back(info, dq, places, blocks, up, rt):
    tokens = dq.shape[1]
    width = 2 * (NOPE + ROPE)
    column = lambda a: pl.BlockSpec((a.shape[0], width), lambda i, s: (0, i))
    still = lambda *shape: pl.BlockSpec(shape, lambda i, s: (0, 0))
    spec = pltpu.PrefetchScalarGridSpec(
        num_scalar_prefetch=1,
        grid=(HEADS // 2,),
        in_specs=[
            pl.BlockSpec((2, tokens, 2 * LANES), lambda i, s: (i, 0, 0)),
            column(up),
            still(*rt.shape),
        ]
        + [column(block) for block in blocks],
        out_specs=[still(tokens, D), still(tokens, LANES), column(up)],
        scratch_shapes=[
            pltpu.VMEM((tokens, D), f32),
            pltpu.VMEM((tokens, LANES), f32),
            pltpu.VMEM((D, width), bf16),
        ],
    )
    return pl.pallas_call(
        functools.partial(query_back_kernel, places=places),
        grid_spec=spec,
        out_shape=[
            jax.ShapeDtypeStruct((tokens, D), f32),
            jax.ShapeDtypeStruct((tokens, LANES), f32),
            jax.ShapeDtypeStruct((LANES, QW), f32),
        ],
        compiler_params=params(1),
        cost_estimate=cost(2 * tokens * D * QW, D * QW * 2),
        name="query_back",
    )(info, dq, up, rt, *blocks)


LOG2E = math.log2(math.e)


PER_STEP = 2


def attend_kernel(l_ref, w_ref, u_ref, q_ref, mix_ref, lse_ref, kv_ref):
    wide = NOPE + VDIM
    w = w_ref[...].reshape(LATENT, PER_STEP * wide)
    both_kv = dot(l_ref[:, :LATENT], w) + dot(l_ref[:, LATENT:], u_ref[...])
    both_kv = both_kv.astype(bf16)
    kv_ref[...] = both_kv
    ones = jnp.ones((both_kv.shape[0], LANES), bf16)
    for i in range(PER_STEP):
        kv = both_kv[:, i * wide : (i + 1) * wide]
        keys = jnp.concatenate([kv[:, :NOPE], l_ref[:, LATENT:]], 1)
        values = jnp.concatenate([kv[:, NOPE:], ones], 1)
        scores = dot(q_ref[i], keys, NT)
        top = jnp.max(scores, axis=1, keepdims=True)
        weights = jnp.exp2((scores - top) * (SCALE * LOG2E)).astype(bf16)
        both = dot(weights, values)
        total = both[:, VDIM:]
        mix_ref[:, i * VDIM : (i + 1) * VDIM] = (both[:, :VDIM] / total).astype(bf16)
        lse = top * (SCALE * LOG2E) + jnp.log2(total)
        lse_ref[i] = lse.T[:8]


def folded(w_kvb, at):
    pieces, _, rows, width = w_kvb.shape
    wide = PER_STEP * (NOPE + VDIM)
    per = width // wide
    return pl.BlockSpec(
        (pieces, 1, rows, wide), lambda h, *s: (0, (at + h) // per, 0, (at + h) % per)
    )


def attend(l_all, w_kvb, u_kvb, q):
    length = l_all.shape[0]
    tokens = q.shape[1]
    wide = NOPE + VDIM
    column = lambda n, w: pl.BlockSpec((n, PER_STEP * w), lambda h: (0, h))
    head = lambda *shape: pl.BlockSpec((PER_STEP,) + shape, lambda h: (h, 0, 0))
    return pl.pallas_call(
        attend_kernel,
        grid=(HEADS // PER_STEP,),
        in_specs=[
            pl.BlockSpec((length, LW), lambda h: (0, 0)),
            folded(w_kvb, 0),
            column(LANES, wide),
            head(tokens, 2 * LANES),
        ],
        out_specs=[column(tokens, VDIM), head(8, tokens), column(length, wide)],
        out_shape=[
            jax.ShapeDtypeStruct((tokens, HEADS * VDIM), bf16),
            jax.ShapeDtypeStruct((HEADS, 8, tokens), f32),
            jax.ShapeDtypeStruct((length, HEADS * wide), bf16),
        ],
        compiler_params=params(1),
        cost_estimate=cost(HEADS * 2 * length * (LW * 256 + tokens * 512), 8e6),
        name="attend",
    )(l_all, w_kvb, u_kvb, q)


def attend_back_kernel(
    info,
    l_ref,
    lt_ref,
    w_ref,
    u_ref,
    kv_ref,
    q_ref,
    lse_ref,
    delta_ref,
    dm_ref,
    cos_ref,
    sin_ref,
    was_ref,
    dq_ref,
    dl_ref,
    du_ref,
    acc,
):
    h = pl.program_id(0)
    wide = NOPE + VDIM
    count = info.shape[0] - 1
    rows = acc.shape[0] // count
    at = lambda k: pl.ds(pl.multiple_of(info[k] * rows, rows), rows)

    @pl.when(h == 0)
    def _():
        if len(was_ref.shape) == 3:
            for k in range(count):
                acc[at(k), :] = was_ref[k].astype(f32)
        else:
            acc[...] = jnp.zeros_like(acc)

    dkvs, drope = [], 0.0
    for i in range(PER_STEP):
        kv = kv_ref[:, i * wide : (i + 1) * wide]
        keys = jnp.concatenate([kv[:, :NOPE], l_ref[:, LATENT:]], 1)
        values = kv[:, NOPE:]
        dm = dm_ref[:, i * VDIM : (i + 1) * VDIM]
        scores = dot(keys, q_ref[i], NT)
        probs = jnp.exp2(scores * (SCALE * LOG2E) - lse_ref[i, :1])
        dvalues = dot(probs.astype(bf16), dm)
        dprobs = dot(values, dm, NT)
        dscores = (probs * (dprobs - delta_ref[i, :1])).astype(bf16)
        dq = dot(dscores, keys, TN) * SCALE
        lane = lax.broadcasted_iota(jnp.int32, (dq.shape[0], LANES), 1)
        rope = dq[:, LANES:]
        rope = rope * cos_ref[...] + unrotate_pair(lane, rope) * sin_ref[...]
        dq_ref[i] = jnp.concatenate([dq[:, :LANES], rope], 1).astype(bf16)
        dkeys = dot(dscores, q_ref[i]) * SCALE
        dkvs += [dkeys[:, :NOPE].astype(bf16), dvalues.astype(bf16)]
        drope += dkeys[:, NOPE:]
    dkv = jnp.concatenate(dkvs, 1)
    w = w_ref[...].reshape(LATENT, PER_STEP * wide)
    acc[:, :LATENT] += dot(dkv, w, NT)
    acc[:, LATENT:] += dot(dkv, u_ref[...], NT) + drope
    du_ref[...] = dot(lt_ref[...], dkv)

    @pl.when(h == pl.num_programs(0) - 1)
    def _():
        for k in range(count):
            dl_ref[k] = acc[at(k), :].astype(bf16)


def attend_back(info, part, l_all, lt, w_kvb, u_kvb, kv, q, lse, delta, dmix, cos, sin, was):
    length = l_all.shape[0]
    tokens = q.shape[1]
    wide = NOPE + VDIM
    heads = HEADS // 2
    count = info.shape[0] - 1
    at = part * heads // PER_STEP
    still = lambda a: pl.BlockSpec(a.shape, lambda h, s: (0,) * a.ndim)
    column = lambda n, w: pl.BlockSpec((n, PER_STEP * w), lambda h, s: (0, at + h))
    head = lambda *shape: pl.BlockSpec((PER_STEP,) + shape, lambda h, s: (at + h, 0, 0))
    spec = pltpu.PrefetchScalarGridSpec(
        num_scalar_prefetch=1,
        grid=(heads // PER_STEP,),
        in_specs=[
            still(l_all),
            still(lt),
            folded(w_kvb, at),
            column(LANES, wide),
            column(length, wide),
            head(tokens, 2 * LANES),
            head(8, tokens),
            head(8, tokens),
            column(tokens, VDIM),
            still(cos),
            still(sin),
            still(was),
        ],
        out_specs=[
            pl.BlockSpec((PER_STEP, tokens, 2 * LANES), lambda h, s: (h, 0, 0)),
            pl.BlockSpec((count, length // count, LW), lambda h, s: (0, 0, 0)),
            pl.BlockSpec((LANES, PER_STEP * wide), lambda h, s: (0, h)),
        ],
        scratch_shapes=[pltpu.VMEM((length, LW), f32)],
    )
    return pl.pallas_call(
        attend_back_kernel,
        grid_spec=spec,
        out_shape=[
            jax.ShapeDtypeStruct((heads, tokens, 2 * LANES), bf16),
            jax.ShapeDtypeStruct((count, length // count, LW), bf16),
            jax.ShapeDtypeStruct((LANES, heads * wide), f32),
        ],
        compiler_params=params(1),
        cost_estimate=cost(heads * 2 * length * (LW * 256 + tokens * 1024), 30e6),
        name="attend_back",
    )(info, l_all, lt, w_kvb, u_kvb, kv, q, lse, delta, dmix, cos, sin, was)


def picks(slot_row, slots):
    row = lax.broadcasted_iota(jnp.int32, (slots, slot_row.shape[1]), 0)
    return jnp.where(row == slot_row, 1.0, 0.0).astype(bf16)


def silu_parts(gate):
    sig = 1.0 / (1.0 + jnp.exp(-gate))
    return gate * sig, sig * (1.0 + gate * (1.0 - sig))


def router_probs(logits, experts):
    lane = lax.broadcasted_iota(jnp.int32, logits.shape, 1)
    logits = jnp.where(lane < experts, logits, -1e30)
    odds = jnp.exp(logits - jnp.max(logits, axis=1, keepdims=True))
    return odds / jnp.sum(odds, axis=1, keepdims=True)


def routed_kernel(info, slot_ref, wr_ref, w_in, w_out, *rest, offs, slots, wide, experts):
    chunks, count = len(offs), info.shape[0] - 1
    x_refs, g_refs = rest[:chunks], rest[chunks : 2 * chunks]
    y_ref, dx_ref, pull_ref, rows, grads, hidden, dacts = rest[2 * chunks :]
    e = pl.program_id(0)
    ff = w_out.shape[1]
    weights = []
    for c in range(chunks):
        pick = picks(slot_ref[info[1 + offs[c] % count], pl.ds(e, 1), :], slots)
        at = pl.ds(c * slots, slots)
        x = dot(pick, x_refs[c][...]).astype(bf16)
        rows[at, :] = x
        weight = router_probs(dot(x, wr_ref[...]), experts)
        lane = lax.broadcasted_iota(jnp.int32, weight.shape, 1)
        weight = jnp.sum(jnp.where(lane == info[0] + e, weight, 0.0), axis=1, keepdims=True)
        weights.append(weight)
        grads[at, :] = (dot(pick, g_refs[c][...]) * weight).astype(bf16)
    weight = jnp.concatenate(weights, 0)
    for a in range(0, ff, wide):
        b = min(a + wide, ff)
        gate = dot(rows[...], w_in[0, :, a:b])
        up = dot(rows[...], w_in[0, :, ff + a : ff + b])
        dhid = dot(grads[...], w_out[0, a:b, :], NT)
        silu, slope = silu_parts(gate)
        hidden[:, a:b] = (silu * up).astype(bf16)
        dacts[:, a:b] = (dhid * up * slope).astype(bf16)
        dacts[:, ff + a : ff + b] = (dhid * silu).astype(bf16)
    pull = jnp.zeros((rows.shape[0], 1), f32)
    step = 2 * wide
    for a in range(0, D, step):
        y = dot(hidden[...], w_out[0, :, a : a + step])
        pull += jnp.sum(y * grads[:, a : a + step].astype(f32), axis=1, keepdims=True)
        y_ref[0, :, a : a + step] = (y * weight).astype(bf16)
        dx_ref[0, :, a : a + step] = dot(dacts[...], w_in[0, a : a + step, :], NT).astype(bf16)
    lane = lax.broadcasted_iota(jnp.int32, (rows.shape[0], LANES), 1)
    pull_ref[0] = jnp.where(lane == info[0] + e, pull, 0.0).astype(bf16)


def routed(info, offs, xs, gs, slot_all, w_router, experts, w_in, w_out):
    chunks, tokens = len(xs), xs[0].shape[0]
    local = w_in.shape[0]
    ff = w_out.shape[1]
    slots = tokens // 2
    rows = chunks * slots
    once = pl.Buffered(1)
    whole = lambda a: pl.BlockSpec(a.shape, lambda e, s: (0,) * a.ndim, pipeline_mode=once)
    out = pl.BlockSpec((1, rows, D), lambda e, s: (e, 0, 0))
    spec = pltpu.PrefetchScalarGridSpec(
        num_scalar_prefetch=1,
        grid=(local,),
        in_specs=[
            whole(slot_all),
            whole(w_router),
            pl.BlockSpec((1, D, 2 * ff), lambda e, s: (e, 0, 0)),
            pl.BlockSpec((1, ff, D), lambda e, s: (e, 0, 0)),
        ]
        + [whole(v) for v in (*xs, *gs)],
        out_specs=[out, out, pl.BlockSpec((1, rows, LANES), lambda e, s: (e, 0, 0))],
        scratch_shapes=[
            pltpu.VMEM((rows, D), bf16),
            pltpu.VMEM((rows, D), bf16),
            pltpu.VMEM((rows, ff), bf16),
            pltpu.VMEM((rows, 2 * ff), bf16),
        ],
    )
    shape = jax.ShapeDtypeStruct((local, rows, D), bf16)
    return pl.pallas_call(
        functools.partial(
            routed_kernel, offs=offs, slots=slots, wide=2 * LANES, experts=experts
        ),
        grid_spec=spec,
        out_shape=[shape, shape, jax.ShapeDtypeStruct((local, rows, LANES), bf16)],
        compiler_params=params(1),
        cost_estimate=cost(local * rows * D * ff * 12, local * D * ff * 6),
        name="routed",
    )(info, slot_all, w_router, w_in, w_out, *xs, *gs)


def shared_kernel(
    info,
    slot_ref,
    y_ref,
    dx_ref,
    pull_ref,
    wi_ref,
    wo_ref,
    u_ref,
    dn_ref,
    *rest,
    offs,
    slots,
    experts,
):
    chunks, count = len(offs), info.shape[0] - 1
    blocks = rest[: 2 * chunks]
    out_ref, dout_ref, gu_up_ref, gu_down_ref, dn_up_ref, dn_down_ref = rest[2 * chunks :]
    local = y_ref.shape[0]
    half = dn_ref.shape[0]
    tokens = blocks[0].shape[0]
    x = jnp.concatenate([ref[...] for ref in blocks[:chunks]], 0)
    g = jnp.concatenate([ref[...] for ref in blocks[chunks:]], 0)
    proj = dot(x, wi_ref[...])
    r = proj[:, 2 * half :].astype(bf16)
    prob = router_probs(proj[:, 2 * half :], experts)
    acts = proj[:, : 2 * half] + dot(r, u_ref[...])
    gate, up = acts[:, :half], acts[:, half:]
    silu, slope = silu_parts(gate)
    inner = (silu * up).astype(bf16)
    rdn = dot(inner, dn_ref[...]).astype(bf16)
    back = dot(g, wo_ref[...], NT)
    drdn = back[:, half:].astype(bf16)
    dinner = back[:, :half] + dot(drdn, dn_ref[...], NT)
    dboth = jnp.concatenate([dinner * up * slope, dinner * silu], 1).astype(bf16)
    dr = dot(dboth, u_ref[...], NT)

    def rows(ref, c, a, b):
        return jnp.concatenate([ref[e, c * slots : (c + 1) * slots, a:b] for e in range(local)], 0)

    chosen, pulls = [], []
    for c in range(chunks):
        owner = info[1 + offs[c] % count]
        pick = [picks(slot_ref[owner, e : e + 1, :], slots) for e in range(local)]
        chosen.append(jnp.concatenate(pick, 0))
        pulls.append(dot(chosen[c], rows(pull_ref, c, 0, LANES), TN))
    pulls = jnp.concatenate(pulls, 0)
    dlogit = pulls - prob * jnp.sum(pulls, axis=1, keepdims=True)
    both = jnp.concatenate([inner, rdn], 1)
    dall = jnp.concatenate([dboth, (dr + dlogit).astype(bf16)], 1)
    step = 4 * LANES
    for a in range(0, D, step):
        out = dot(both, wo_ref[:, a : a + step])
        dx = dot(dall, wi_ref[a : a + step, :], NT)
        for c in range(chunks):
            at = slice(c * tokens, (c + 1) * tokens)
            put = lambda ref: dot(chosen[c], rows(ref, c, a, a + step), TN)
            out_ref[c, :, a : a + step] = (out[at] + put(y_ref)).astype(bf16)
            dout_ref[c, :, a : a + step] = (dx[at] + put(dx_ref)).astype(bf16)
    gu_up_ref[...] = dot(r, dboth, TN)
    gu_down_ref[...] = dot(dr.astype(bf16), x, TN)
    dn_up_ref[...] = dot(rdn, g, TN)
    dn_down_ref[...] = dot(drdn, inner, TN)


def shared(info, offs, xs, gs, slot_all, experts, y, dx, pull, wi, wo, u, dn):
    chunks, tokens = len(xs), xs[0].shape[0]
    slots = tokens // 2
    half = dn.shape[0]
    once = pl.Buffered(1)
    whole = lambda a: pl.BlockSpec(a.shape, lambda c, s: (0,) * a.ndim, pipeline_mode=once)
    still = lambda *shape: pl.BlockSpec(shape, lambda c, s: (0,) * len(shape))
    operands = [slot_all, y, dx, pull, wi, wo, u, dn, *xs, *gs]
    shapes = [(chunks, tokens, D)] * 2
    shapes += [(LANES, 2 * half), (LANES, D), (LANES, D), (LANES, half)]
    spec = pltpu.PrefetchScalarGridSpec(
        num_scalar_prefetch=1,
        grid=(1,),
        in_specs=[whole(a) for a in operands],
        out_specs=[still(*shape) for shape in shapes],
    )
    return pl.pallas_call(
        functools.partial(shared_kernel, offs=offs, slots=slots, experts=experts),
        grid_spec=spec,
        out_shape=[
            jax.ShapeDtypeStruct(shape, bf16 if i < 2 else f32) for i, shape in enumerate(shapes)
        ],
        compiler_params=params(1),
        cost_estimate=cost(chunks * 4e9, chunks * 8e6),
        name="shared",
    )(info, *operands)


def rms_scale(v):
    return lax.rsqrt(jnp.mean(v * v, axis=-1, keepdims=True) + EPS)


def rms_back(v, scale, gain, dy):
    unit = v * scale
    gdy = gain * dy
    return (gdy - unit * jnp.mean(unit * gdy, axis=-1, keepdims=True)) * scale


def angles(positions):
    half = ROPE // 2
    ladder = jnp.arange(half).astype(f32)
    frequency = jnp.exp(ladder * (-2.0 * math.log(10000.0) / ROPE))
    turn = positions.astype(f32)[:, None] * frequency[None, :]
    return jnp.cos(turn), jnp.sin(turn)


def pad_lanes(v, width, before=0):
    return jnp.pad(v, ((0, 0), (before, width - before - v.shape[1])))


def pad_rows(v, height, before=0):
    return jnp.pad(v, ((before, height - before - v.shape[0]), (0, 0)))


def round_up(n, m):
    return -(-n // m) * m


def pack(parts, unit=LANES):
    return jnp.concatenate([pad_lanes(v, round_up(v.shape[1], unit)) for v in parts], 1)


def unpack(v, widths, unit=LANES):
    out, at = [], 0
    for w in widths:
        out.append(v[:, at : at + w])
        at += round_up(w, unit)
    return out


class Totals:
    def __init__(self, parts, shards):
        self.shards = shards
        self.widths = [v.shape[1] for v in parts]
        packed = pack(parts)
        self.columns = round_up(packed.shape[1], shards * LANES)
        packed = pad_lanes(packed, self.columns).astype(bf16)
        self.cut = self.columns // shards
        self.packed = packed.reshape(RANK, shards, self.cut).transpose(1, 0, 2)

    def deal(self):
        mine = lax.all_to_all(self.packed, "shard", split_axis=0, concat_axis=0, tiled=True)
        self.mine = jnp.sum(mine.astype(f32), axis=0).astype(bf16)
        return self.mine

    def gather(self, ids):
        seqs = lax.all_gather(self.mine, "replica", axis=0)
        chosen = (ids[None, :] == jnp.arange(ADAPTERS)[:, None]).astype(f32)
        sums = jnp.sum(chosen[:, :, None, None] * seqs.astype(f32)[None], axis=1).astype(bf16)
        self.sums = sums.reshape(self.shards, ADAPTERS // self.shards, RANK, self.cut)
        return self.sums

    def home(self):
        full = lax.all_to_all(self.sums, "shard", split_axis=0, concat_axis=0, tiled=True)
        full = full.transpose(1, 2, 0, 3).reshape(ADAPTERS // self.shards, RANK, self.columns)
        out, at = [], 0
        for w in self.widths:
            out.append(full[:, :, at : at + w].astype(f32))
            at += round_up(w, LANES)
        return out


def body(
    hidden_in,
    out_grad,
    routes,
    seq_adapter,
    attn_gain,
    latent_gain,
    ffn_gain,
    w_qa,
    w_kvb,
    w_out,
    w_router,
    w_shared_in,
    w_shared_out,
    w_expert_in,
    w_expert_out,
    qa_down,
    qa_up,
    kvb_down,
    kvb_up,
    out_down,
    out_up,
    gu_down,
    gu_up,
    dn_down,
    dn_up,
):
    shards = lax.axis_size("shard")
    replicas = lax.axis_size("replica")
    place = lax.axis_index("shard")
    tokens = hidden_in.shape[0]
    local = w_expert_in.shape[0]
    experts = local * shards
    ring = Ring(shards)
    adapter_id = seq_adapter[0]
    core = (lax.axis_index("replica") % 2).astype(jnp.int32)
    spots = jnp.concatenate([ring.owners, core.reshape(1)])
    ids = lax.all_gather(seq_adapter, "replica", axis=0, tiled=True)
    first = (place * local).astype(jnp.int32).reshape(1)

    tables = [qa_down, qa_up[:, :, :QW], qa_up[:, :, QW:], kvb_down, kvb_up, out_down, out_up]
    tables = [t[0] for t in tables + [gu_down, gu_up, dn_down, dn_up]]
    dealt = pack(tables)
    cut = round_up(dealt.shape[1], shards * LANES) // shards
    dealt = pad_lanes(dealt, cut * shards).reshape(RANK, shards, cut).transpose(1, 0, 2)
    dealt = lax.all_to_all(dealt, "shard", split_axis=0, concat_axis=0, tiled=True)
    dealt = lax.dynamic_index_in_dim(dealt, adapter_id, 0, keepdims=True)
    dealt = jnp.broadcast_to(dealt, (shards, RANK, cut))
    dealt = lax.all_to_all(dealt, "shard", split_axis=0, concat_axis=0, tiled=True)
    dealt = dealt.transpose(1, 0, 2).reshape(RANK, shards * cut)
    a_qd, a_quq, a_qul, a_kd, a_ku, a_od, a_ou, a_gd, a_gu, a_nd, a_nu = unpack(
        dealt, [t.shape[1] for t in tables]
    )

    kvb_rows, fold, kvb_wide, own_weights = pack_weights(core, w_qa, w_kvb, w_out, replicas)
    w_walk = Walk(ring, own_weights)
    w_swaps = Swaps(ring, w_walk, replicas)
    w1 = w_walk.hop()
    own_swap = w_swaps.swap(w_walk.own)
    w2 = w_walk.hop(*own_swap)
    width = w_shared_out.shape[0]
    half = round_up(width, LANES)
    rows_in = w_shared_in.shape[0]
    if replicas % 2 == 0:
        core = lax.axis_index("replica") % 2
    mine = own_share(w_shared_in, replicas, zero_after(*w1))
    mine = mine.reshape(mine.shape[0], 2, shards, width).transpose(2, 0, 1, 3)
    mine = jnp.pad(mine, ((0, 0), (0, 0), (0, 0), (0, half - width)))
    mine = mine.reshape(shards, mine.shape[1], 2 * half)
    ready = mine
    inputs = hidden_in.astype(f32)
    in_scale = rms_scale(inputs)
    hb = (inputs * in_scale * attn_gain).astype(bf16)
    swap1 = w_swaps.swap(w_walk.pairs[0])
    w3 = w_walk.hop(*swap1, ready[0, :16], hb[:16])
    swap2 = w_swaps.swap(w_walk.pairs[1])
    w4 = w_walk.hop(*swap2, ids)
    u_q = pad_rows(a_quq, LANES)
    u_kvb = pad_rows(a_ku, LANES, ROPE)
    wr = pad_lanes(w_router, LANES)
    r_qa = dot(hb, a_qd, NT).astype(bf16)
    w_swaps.swap(w_walk.pairs[2])
    w_swaps.swap(w_walk.halves)
    w_at, w_blocks = w_swaps.rows(0, w_out.shape[0])
    kvb_at, out_at, lat_at = QW, QW + kvb_wide, QW + kvb_wide + D
    w_lat = place_rows(spots, w_at, w_blocks, D, lat_at, LW, LANES)[:, : LATENT + ROPE]
    full_kvb = place_rows(spots, w_at, w_blocks, D, kvb_at, kvb_wide, kvb_wide)
    full_kvb = full_kvb.reshape(LATENT // kvb_rows, fold, kvb_rows, kvb_wide)
    full_out = place_rows(spots, w_at, w_blocks, D, out_at, D, D // 2)

    lat_raw = dot(hb, w_lat) + dot(r_qa, a_qul)
    latent_raw, rope_raw = lat_raw[:, :LATENT], lat_raw[:, LATENT:]
    lat_scale = rms_scale(latent_raw)
    latent = (latent_raw * lat_scale * latent_gain).astype(bf16)
    positions = place * tokens + jnp.arange(tokens)
    cos_half, sin_half = angles(positions)
    rh = ROPE // 2
    rope_a, rope_b = rope_raw[:, :rh], rope_raw[:, rh:]
    rope = jnp.concatenate(
        [rope_a * cos_half - rope_b * sin_half, rope_b * cos_half + rope_a * sin_half], 1
    ).astype(bf16)
    r_kv = dot(latent, a_kd, NT).astype(bf16)
    l_own = jnp.concatenate([latent, rope, r_kv, routes.astype(bf16)], 1)
    l_own = pad_lanes(l_own, LW)
    l_walk = Walk(ring, l_own)
    l_walk.hop()
    l_walk.hop(full_out)
    l3 = l_walk.hop(full_kvb)
    l4 = l_walk.hop(u_q, u_kvb)
    (hb_late,) = gate((hb,), l3)
    g_walk = Walk(ring, out_grad)
    g1 = g_walk.hop(*l4)
    (mine,) = gate((ready,), l4)
    mine = lax.all_to_all(mine, "shard", split_axis=0, concat_axis=0, tiled=True)
    if replicas % 2 == 0:
        other = pair_swap(mine, replicas)
        w_si = jnp.concatenate(
            [jnp.where(core == 0, mine, other), jnp.where(core == 0, other, mine)], 1
        )
    else:
        w_si = mine
    w_si = w_si.reshape(shards * rows_in, 2 * half)

    w_i = jnp.concatenate([w_si, pad_lanes(jnp.concatenate([w_router, a_gd.T], 1), LANES)], 1)
    w_o = jnp.concatenate([pad_rows(w_shared_out, half), pad_rows(a_nu, LANES)], 0)
    gu_g = lax.dynamic_slice_in_dim(a_gu, place * width, width, 1)
    gu_u = lax.dynamic_slice_in_dim(a_gu, shards * width + place * width, width, 1)
    u_gu = jnp.concatenate([pad_lanes(gu_g, half), pad_lanes(gu_u, half)], 1)
    u_gu = pad_rows(u_gu, LANES, experts)
    nd_own = lax.dynamic_slice_in_dim(a_nd, place * width, width, 1)
    dn_own = pad_rows(pad_lanes(nd_own.T, LANES), half)

    l_all = all_latents(spots, l_walk.blocks(), tokens)
    cos = pad_lanes(jnp.concatenate([cos_half, cos_half], 1), LANES)
    sin = pad_lanes(jnp.concatenate([sin_half, sin_half], 1), LANES)
    q = query_heads(
        spots, hb_late, pad_lanes(r_qa, LANES), w_at, w_blocks, u_q, cos, sin
    )

    mixture, lse, kv = attend(l_all, full_kvb, u_kvb, q)
    (mixture,) = gate((mixture,), g1)
    r_out = dot(mixture, a_od, NT).astype(bf16)
    after_attn = inputs + dot(mixture, full_out) + dot(r_out, a_ou)
    ffn_scale = rms_scale(after_attn)
    ffn_low = (after_attn * ffn_scale * ffn_gain).astype(bf16)

    at = LATENT + ROPE + RANK
    routes_all = l_all[:, at : at + TOPK].astype(jnp.int32).reshape(shards, tokens, TOPK)
    wanted = first[0] + jnp.arange(local)
    mask = jnp.any(routes_all[:, None, :, :] == wanted[None, :, None, None], axis=-1)
    before = jnp.triu(jnp.ones((tokens, tokens), bf16), 1)
    rank = lax.dot_general(
        mask.astype(bf16), before, (((2,), (0,)), ((), ())), preferred_element_type=f32
    )
    slot_all = jnp.where(mask, rank.astype(jnp.int32), -1)

    out_piece, dx_piece, small = {}, {}, []


    info = jnp.concatenate([first, ring.owners])

    def run_routed(members, *after):
        offs, xs, gs = ([m[i] for m in members] for i in range(3))
        if after:
            xs = gate(xs, after)
        return offs, xs, gs, *routed(
            info, offs, xs, gs, slot_all, wr, experts, w_expert_in, w_expert_out
        )

    def run_shared(offs, xs, gs, y, dxr, pull):
        out, dx, *grads = shared(
            info, offs, xs, gs, slot_all, experts, y, dxr, pull, w_i, w_o, u_gu, dn_own
        )
        small.append(grads)
        for i, off in enumerate(offs):
            out_piece[off], dx_piece[off] = out[i], dx[i]
        return grads[-1]

    far = shards // 2
    walk = Walk(ring, ffn_low)
    members = lambda h: [
        (off, x, g) for off, x, g in zip((-h, h), walk.pairs[h - 1], g_walk.pairs[h - 1])
    ]
    x1 = walk.hop()
    done = run_routed([(0, ffn_low, out_grad)])
    walk.hop(done[3])
    g_walk.hop(*x1)
    mark = run_shared(*done)
    done = run_routed(members(1), mark)
    x3 = walk.hop(done[3])
    g_walk.hop(*walk.pairs[1])
    mark = run_shared(*done)
    done = run_routed(members(2), mark)
    walk.hop(done[3])
    g_walk.hop(*walk.pairs[2])
    mark = run_shared(*done)
    opposite = (far, jnp.concatenate(walk.halves, 0), jnp.concatenate(g_walk.halves, 0))
    run_shared(*run_routed(members(3) + [opposite], mark))
    out_piece[-far], dx_piece[-far] = out_piece[far], dx_piece[far]
    small = [sum(parts[1:], parts[0]) for parts in zip(*small)]

    def spread(v, cols):
        return jnp.concatenate(
            [
                lax.dynamic_update_slice_in_dim(
                    jnp.zeros((RANK, cols), f32), part, place * width, 1
                )
                for part in v
            ],
            1,
        )

    g_gu_up = small[0][experts : experts + RANK]
    g_gu_up = spread([g_gu_up[:, :width], g_gu_up[:, half : half + width]], shards * width)
    g_gu_down = small[1][experts : experts + RANK]
    g_dn_up = small[2][:RANK]
    g_dn_down = spread([small[3][:RANK, :width]], shards * width)

    seen = {}
    ffn_grad = ring.scatter_sum(lambda off: dx_piece[off], {})

    d_after = out_grad.astype(f32) + rms_back(after_attn, ffn_scale, ffn_gain, ffn_grad)
    d_after_low = d_after.astype(bf16)
    dr_out = dot(d_after_low, a_ou, NT).astype(bf16)
    dmix = (dot(d_after_low, full_out, NT) + dot(dr_out, a_od)).astype(bf16)
    g_out_up = dot(r_out, d_after_low, TN)
    g_out_down = dot(dr_out, mixture, TN)
    delta = (dmix.astype(f32) * mixture.astype(f32)).reshape(tokens, HEADS, VDIM).sum(-1).T
    delta = jnp.broadcast_to(delta[:, None, :], (HEADS, 8, tokens))
    lt = l_all[:, LATENT:].T
    parts = []

    def back(*marks):
        was = parts[-1][1] if parts else jnp.zeros((8, LANES), bf16)
        (marked,) = gate((lse,), marks) if not parts else gate((lse + 0.0,), marks)
        parts.append(
            attend_back(
                spots, len(parts), l_all, lt, full_kvb, u_kvb, kv, q, marked, delta, dmix, cos, sin, was
            )
        )
        return (parts[-1][2],)

    def first_arrived(r, l):
        seen["far"] = (r[:16], l[:16])
        return ()

    def next_arrived(r, l):
        seen["next"] = (r[:16], l[:16])
        return back(*seen["far"])

    def last_arrived(r, l):
        back(*seen["next"])
        dl = parts[-1][1]
        seen["dl"] = ring.scatter_sum(
            lambda off: dl[off % shards],
            {far - 2: query_grads, far - 3: dl_arrived},
        )
        return seen["dl near"]

    def query_grads(r, l):
        dq = jnp.concatenate([part[0] for part in parts], 0)
        seen["q"] = query_back(spots, dq, w_at, w_blocks, u_q, pad_lanes(r_qa, LANES).T)
        return (seen["q"][1],)

    def dl_arrived(r, l):
        seen["dl near"] = (r[:16], l[:16])
        return ()

    out_sum = ring.scatter_sum(
        lambda off: out_piece[off],
        {
            far: lambda: (ffn_grad,),
            far - 1: first_arrived,
            far - 2: next_arrived,
            far - 3: last_arrived,
        },
    )
    block_out = (after_attn + out_sum).astype(bf16)
    g_ku = jnp.concatenate([part[2] for part in parts], 1)
    g_kvb_up = g_ku[ROPE : ROPE + RANK]
    dhb_q, dr_q, g_qu = seen["q"]
    dl_own = seen["dl"]
    dr_kv = dl_own[:, LATENT + ROPE : LATENT + ROPE + RANK].astype(bf16)
    d_latent = dl_own[:, :LATENT] + dot(dr_kv, a_kd)
    g_kvb_down = dot(dr_kv, latent, TN)
    d_latent = rms_back(latent_raw, lat_scale, latent_gain, d_latent)
    drope = dl_own[:, LATENT : LATENT + ROPE]
    drope_a, drope_b = drope[:, :rh], drope[:, rh:]
    drope = jnp.concatenate(
        [drope_a * cos_half + drope_b * sin_half, drope_b * cos_half - drope_a * sin_half], 1
    )
    d_lat = jnp.concatenate([d_latent, drope], 1).astype(bf16)
    dr_qa = (dr_q[:, :RANK] + dot(d_lat, a_qul, NT)).astype(bf16)
    dhb = dhb_q + dot(d_lat, w_lat, NT) + dot(dr_qa, a_qd)
    g_qa_up = jnp.concatenate([g_qu[:RANK], dot(r_qa, d_lat, TN)], 1)
    g_qa_down = dot(dr_qa, hb, TN)
    hidden_grad = d_after + rms_back(inputs, in_scale, attn_gain, dhb)

    t_attn = Totals(
        [g_qa_down, g_qa_up, g_kvb_down, g_kvb_up, g_out_down, g_out_up]
        + [g_gu_down, g_gu_up, g_dn_down, g_dn_up],
        shards,
    )
    t_attn.deal()
    t_attn.gather(ids)
    return (block_out, hidden_grad, *t_attn.home())


def solution(mesh):
    rows = P(("replica", "shard"), None)
    cut2 = P("shard", None)
    cut3 = P("shard", None, None)
    in_specs = (
        (rows, rows, rows, P("replica"), P(), P(), P())
        + (cut2, cut2, cut2, P(), cut2, cut2, cut3, cut3)
        + (cut3,) * 10
    )
    out_specs = (rows, rows) + (cut3,) * 10
    return jax.shard_map(body, mesh=mesh, in_specs=in_specs, out_specs=out_specs, check_vma=False)
```

```python
import functools
import math

import jax
import jax.numpy as jnp
from jax import lax
from jax.experimental import pallas as pl
from jax.experimental.pallas import tpu as pltpu
from jax.sharding import PartitionSpec as P

D = 2048
HEADS = 16
NOPE = 128
ROPE = 64
VDIM = 128
LATENT = 512
TOPK = 6
RANK = 16
ADAPTERS = 8
BLOCK = 256
QW = HEADS * (NOPE + ROPE)
LW = LATENT + 2 * ROPE
LANES = 128
VMEM_LIMIT = 60 * 1024 * 1024
SCALE = (NOPE + ROPE) ** (-0.5)
EPS = 1e-06
f32 = jnp.float32
bf16 = jnp.bfloat16

NN = (((1,), (0,)), ((), ()))
NT = (((1,), (1,)), ((), ()))
TN = (((0,), (0,)), ((), ()))


def dot(a, b, dims=NN):
    return lax.dot_general(a, b, dims, preferred_element_type=f32)


def params(n):
    return pltpu.CompilerParams(
        dimension_semantics=("arbitrary",) * n, vmem_limit_bytes=VMEM_LIMIT
    )


def cost(flops, nbytes):
    return pl.CostEstimate(flops=int(flops), bytes_accessed=int(nbytes), transcendentals=0)


def gate_kernel(*refs):
    del refs


def gate(values, marks):
    anywhere = pl.BlockSpec(memory_space=pl.ANY)
    values, marks = tuple(values), tuple(marks)
    return pl.pallas_call(
        gate_kernel,
        in_specs=[anywhere] * len(values + marks),
        out_specs=[anywhere] * len(values),
        out_shape=[jax.ShapeDtypeStruct(v.shape, v.dtype) for v in values],
        input_output_aliases={i: i for i in range(len(values))},
        cost_estimate=cost(0, 0),
        name="gate",
    )(*values, *marks)


def zero_kernel(*refs):
    refs[-1][0] = 0


def zero_after(*marks):
    anywhere = pl.BlockSpec(memory_space=pl.ANY)
    return pl.pallas_call(
        zero_kernel,
        in_specs=[anywhere] * len(marks),
        out_specs=pl.BlockSpec(memory_space=pltpu.SMEM),
        out_shape=jax.ShapeDtypeStruct((1,), jnp.int32),
        cost_estimate=cost(0, 0),
        name="zero_after",
    )(*marks)[0]


def ring_of(count):
    return list(range(0, count, 2)) + list(range(count - 1, 0, -2))


class Ring:
    def __init__(self, count):
        order = ring_of(count)
        place_of = [order.index(i) for i in range(count)]
        self.count = count
        pos = jnp.asarray(place_of, jnp.int32)[lax.axis_index("shard")]
        self.owners = jnp.asarray(order, jnp.int32)[(pos + jnp.arange(count)) % count]
        self.right = [(order[i], order[(i + 1) % count]) for i in range(count)]
        self.left = [(order[i], order[(i - 1) % count]) for i in range(count)]

    def owner(self, off):
        return self.owners[off % self.count]

    def send_right(self, v):
        return lax.ppermute(v, "shard", self.right)

    def send_left(self, v):
        return lax.ppermute(v, "shard", self.left)

    def scatter_sum(self, piece, holds):
        half = self.count // 2
        far = piece(half)
        n = far.shape[0] // 2
        r, l = far[:n], far[n:]
        if half in holds:
            r, l = gate((r, l), holds[half]())
        r, l = self.send_right(r), self.send_left(l)
        for h in range(half - 1, 0, -1):
            up, down = piece(h), piece(-h)
            if h in holds:
                r, l = gate((r, l), holds[h](r, l))
            if r.shape[0] == n:
                up = jnp.concatenate([up[:n].astype(f32) + r.astype(f32), up[n:].astype(f32)], 0)
                down = jnp.concatenate([down[:n].astype(f32), down[n:].astype(f32) + l.astype(f32)], 0)
            else:
                up = up.astype(f32) + r.astype(f32)
                down = down.astype(f32) + l.astype(f32)
            r, l = self.send_right(up.astype(bf16)), self.send_left(down.astype(bf16))
        return piece(0).astype(f32) + r.astype(f32) + l.astype(f32)


class Walk:
    def __init__(self, ring, *arrays):
        self.ring, self.own, self.pairs, self.halves = ring, list(arrays), [], None

    def hop(self, *marks):
        half, k = self.ring.count // 2, len(self.own)
        if self.pairs:
            held = gate(self.pairs[-1], marks)
            self.pairs[-1] = held
            r, l = held[:k], held[k:]
        else:
            if marks:
                self.own = gate(self.own, marks)
            r = l = self.own
        if len(self.pairs) < half - 1:
            right = [self.ring.send_right(v) for v in r]
            left = [self.ring.send_left(v) for v in l]
            self.pairs.append(right + left)
            return self.pairs[-1]
        right = [self.ring.send_right(v[: v.shape[0] // 2]) for v in r]
        left = [self.ring.send_left(v[v.shape[0] // 2 :]) for v in l]
        self.halves = right + left
        return self.halves

    def blocks(self, i=0):
        k = len(self.own)
        out = [(0, 0, self.own[i])]
        for h, pair in enumerate(self.pairs):
            out += [(-h - 1, 0, pair[i]), (h + 1, 0, pair[k + i])]
        far = self.ring.count // 2
        n = self.own[i].shape[0] // 2
        return out + [(far, 0, self.halves[i]), (far, n, self.halves[k + i])]


def pair_swap(v, replicas):
    return lax.ppermute(v, "replica", [(i, i ^ 1) for i in range(replicas)])


def fill_rows(info, places, blocks, out):
    count = info.shape[0] - 1
    for (off, n, row, half, other), block in zip(places, blocks):
        core = info[count]
        at = info[off % count] * n + row + half * (1 - core if other else core)
        out[pl.ds(pl.multiple_of(at, 16), block.shape[0]), :] = block[...]


def place_kernel(info, *refs, places):
    fill_rows(info, places, refs[:-1], refs[-1])


def place_rows(info, places, blocks, height, first=0, width=None, cut=None):
    width = width or blocks[0].shape[1]
    cut = cut or next((c for c in (2048, 1024) if width % c == 0 and height * c <= 1 << 21), width)
    at = first // cut
    spec = pltpu.PrefetchScalarGridSpec(
        num_scalar_prefetch=1,
        grid=(width // cut,),
        in_specs=[pl.BlockSpec((b.shape[0], cut), lambda i, s: (0, at + i)) for b in blocks],
        out_specs=pl.BlockSpec((height, cut), lambda i, s: (0, i)),
    )
    return pl.pallas_call(
        functools.partial(place_kernel, places=places),
        grid_spec=spec,
        out_shape=jax.ShapeDtypeStruct((height, width), blocks[0].dtype),
        compiler_params=params(1),
        cost_estimate=cost(0, height * width * 4),
        name="place_rows",
    )(info, *blocks)


def latents_kernel(info, *refs, places):
    blocks, out = refs[:-1], refs[-1]
    count = info.shape[0] - 1
    for (off, n, row, _, _), block in zip(places, blocks):
        rows = block.shape[0]
        at = pl.ds(pl.multiple_of(info[off % count] * n + row, 16), rows)
        hide = jnp.where(info[off % count] > info[0], -1e30, 0.0)
        lane = lax.broadcasted_iota(jnp.int32, (rows, LANES), 1)
        tail = jnp.where(lane == LANES - 1, hide, block[:, LATENT:].astype(f32))
        out[at, :LATENT] = block[:, :LATENT]
        out[at, LATENT:] = tail.astype(bf16)


def all_latents(info, blocks, n):
    places = [(off, n, row, 0, False) for off, row, _ in blocks]
    blocks = [v for _, _, v in blocks]
    height = (info.shape[0] - 1) * n
    spec = pltpu.PrefetchScalarGridSpec(
        num_scalar_prefetch=1,
        grid=(1,),
        in_specs=[pl.BlockSpec(b.shape, lambda i, s: (0, 0)) for b in blocks],
        out_specs=pl.BlockSpec((height, LW), lambda i, s: (0, 0)),
    )
    return pl.pallas_call(
        functools.partial(latents_kernel, places=places),
        grid_spec=spec,
        out_shape=jax.ShapeDtypeStruct((height, LW), bf16),
        compiler_params=params(1),
        cost_estimate=cost(0, height * LW * 4),
        name="all_latents",
    )(info, *blocks)


def whole_rows(info, blocks, n):
    places = [(off, n, row, 0, False) for off, row, _ in blocks]
    return place_rows(info, places, [v for _, _, v in blocks], (info.shape[0] - 1) * n)


def pack_kernel(core, qa_ref, kvb_ref, out_ref, all_ref, *, fold):
    del core
    rows, wide = kvb_ref.shape[0], kvb_ref.shape[1] // fold
    all_ref[:, :QW] = qa_ref[:, :QW]
    for i in range(fold):
        all_ref[i * rows : (i + 1) * rows, QW : QW + wide] = kvb_ref[:, i * wide : (i + 1) * wide]
    all_ref[:, QW + wide : QW + wide + D] = out_ref[...]
    rest = jnp.zeros((all_ref.shape[0], LW - LATENT - ROPE), all_ref.dtype)
    all_ref[:, QW + wide + D :] = jnp.concatenate([qa_ref[:, QW:], rest], 1)


def pack_weights(core, w_qa, w_kvb, w_out, replicas):
    parts = 2 if replicas % 2 == 0 else 1
    height, kvb_rows = w_out.shape[0] // parts, w_kvb.shape[0] // parts
    fold = height // kvb_rows
    wide = w_kvb.shape[1] // fold
    width = QW + wide + D + LW
    mine = (core % parts).reshape(1)
    share = lambda n, w: pl.BlockSpec((n, w.shape[1]), lambda i, s: (s[0], 0))
    spec = pltpu.PrefetchScalarGridSpec(
        num_scalar_prefetch=1,
        grid=(1,),
        in_specs=[share(height, w_qa), share(kvb_rows, w_kvb), share(height, w_out)],
        out_specs=pl.BlockSpec((height, width), lambda i, s: (0, 0)),
    )
    packed = pl.pallas_call(
        functools.partial(pack_kernel, fold=fold),
        grid_spec=spec,
        out_shape=jax.ShapeDtypeStruct((height, width), bf16),
        compiler_params=params(1),
        cost_estimate=cost(0, height * width * 4),
        name="pack_weights",
    )(mine, w_qa, w_kvb, w_out)
    return kvb_rows, fold, wide, packed


def own_share(w, replicas, zero=0):
    if replicas % 2:
        return w
    half = w.shape[0] // 2
    return lax.dynamic_slice_in_dim(w, lax.axis_index("replica") % 2 * half + zero, half, 0)


class Swaps:
    def __init__(self, ring, walk, replicas):
        self.ring, self.walk, self.replicas = ring, walk, replicas
        self.pairs = []

    def swap(self, blocks):
        got = [pair_swap(v, self.replicas) for v in blocks] if self.replicas % 2 == 0 else []
        self.pairs.append(got)
        return got

    def rows(self, i, n):
        walk, k = self.walk, len(self.walk.own)
        paired = self.replicas % 2 == 0
        far = self.ring.count // 2
        half = walk.own[i].shape[0] // 2
        got = [(0, 0, walk.own, i)]
        for h, pair in enumerate(walk.pairs):
            got += [(-h - 1, 0, pair, i), (h + 1, 0, pair, k + i)]
        got += [(far, 0, walk.halves, i), (far, half, walk.halves, k + i)]
        sets = [walk.own] + list(walk.pairs) + [walk.halves]
        places, out = [], []
        for off, row, blocks, j in got:
            where = next(m for m, v in enumerate(sets) if v is blocks)
            step = n // 2 if paired else 0
            places.append((off, n, row, step, False))
            out.append(blocks[j])
            if paired:
                places.append((off, n, row, step, True))
                out.append(self.pairs[where][j])
        return places, out


def rotate_pair(lane, v):
    half = ROPE // 2
    return jnp.where(lane < half, -pltpu.roll(v, LANES - half, 1), pltpu.roll(v, half, 1))


def unrotate_pair(lane, v):
    half = ROPE // 2
    return jnp.where(lane < half, pltpu.roll(v, LANES - half, 1), -pltpu.roll(v, half, 1))


def query_kernel(info, hb_ref, r_ref, up_ref, cos_ref, sin_ref, *rest, places):
    blocks, q_ref, w_ref = rest[:-2], rest[-2], rest[-1]
    fill_rows(info, places, blocks, w_ref)
    acc = dot(hb_ref[...], w_ref[...]) + dot(r_ref[...], up_ref[...])
    lane = lax.broadcasted_iota(jnp.int32, (acc.shape[0], LANES), 1)
    for i in range(2):
        own = acc if i == 0 else pltpu.roll(acc, NOPE + ROPE, 1)
        rope = own[:, LANES : 2 * LANES]
        turned = rope * cos_ref[...] + rotate_pair(lane, rope) * sin_ref[...]
        turned = jnp.where(lane == LANES - 1, 1.0, turned)
        q_ref[i] = jnp.concatenate([own[:, :LANES], turned], 1).astype(bf16)


def query_heads(info, hb, r, places, blocks, up, cos, sin):
    tokens = hb.shape[0]
    width = 2 * (NOPE + ROPE)
    whole = lambda a: pl.BlockSpec(a.shape, lambda i, s: (0,) * a.ndim)
    column = lambda a: pl.BlockSpec((a.shape[0], width), lambda i, s: (0, i))
    spec = pltpu.PrefetchScalarGridSpec(
        num_scalar_prefetch=1,
        grid=(HEADS // 2,),
        in_specs=[whole(hb), whole(r), column(up), whole(cos), whole(sin)]
        + [column(block) for block in blocks],
        out_specs=pl.BlockSpec((2, tokens, 2 * LANES), lambda i, s: (i, 0, 0)),
        scratch_shapes=[pltpu.VMEM((D, width), bf16)],
    )
    return pl.pallas_call(
        functools.partial(query_kernel, places=places),
        grid_spec=spec,
        out_shape=jax.ShapeDtypeStruct((HEADS, tokens, 2 * LANES), bf16),
        compiler_params=params(1),
        cost_estimate=cost(2 * tokens * D * QW, D * QW * 2),
        name="query_heads",
    )(info, hb, r, up, cos, sin, *blocks)


def query_back_kernel(info, dq_ref, up_ref, rt_ref, *rest, places):
    blocks = rest[:-6]
    dhb_ref, dr_ref, dup_ref, acc, racc, w_ref = rest[-6:]
    i = pl.program_id(0)
    tokens = dq_ref.shape[1]

    @pl.when(i == 0)
    def _():
        acc[...] = jnp.zeros_like(acc)
        racc[...] = jnp.zeros_like(racc)

    fill_rows(info, places, blocks, w_ref)
    pad = jnp.zeros((tokens, LANES), f32)
    first = jnp.concatenate([dq_ref[0].astype(f32), pad], 1)
    second = jnp.concatenate([dq_ref[1].astype(f32), pad], 1)
    both = (first + pltpu.roll(second, NOPE + ROPE, 1)).astype(bf16)
    acc[...] += dot(both, w_ref[...], NT)
    racc[...] += dot(both, up_ref[...], NT)
    dup_ref[...] = dot(rt_ref[...], both)

    @pl.when(i == pl.num_programs(0) - 1)
    def _():
        dhb_ref[...] = acc[...]
        dr_ref[...] = racc[...]


def query_back(info, dq, places, blocks, up, rt):
    tokens = dq.shape[1]
    width = 2 * (NOPE + ROPE)
    column = lambda a: pl.BlockSpec((a.shape[0], width), lambda i, s: (0, i))
    still = lambda *shape: pl.BlockSpec(shape, lambda i, s: (0, 0))
    spec = pltpu.PrefetchScalarGridSpec(
        num_scalar_prefetch=1,
        grid=(HEADS // 2,),
        in_specs=[
            pl.BlockSpec((2, tokens, 2 * LANES), lambda i, s: (i, 0, 0)),
            column(up),
            still(*rt.shape),
        ]
        + [column(block) for block in blocks],
        out_specs=[
            still(tokens, D),
            still(tokens, LANES),
            pl.BlockSpec((rt.shape[0], width), lambda i, s: (0, i)),
        ],
        scratch_shapes=[
            pltpu.VMEM((tokens, D), f32),
            pltpu.VMEM((tokens, LANES), f32),
            pltpu.VMEM((D, width), bf16),
        ],
    )
    return pl.pallas_call(
        functools.partial(query_back_kernel, places=places),
        grid_spec=spec,
        out_shape=[
            jax.ShapeDtypeStruct((tokens, D), f32),
            jax.ShapeDtypeStruct((tokens, LANES), f32),
            jax.ShapeDtypeStruct((rt.shape[0], QW), f32),
        ],
        compiler_params=params(1),
        cost_estimate=cost(2 * tokens * D * QW, D * QW * 2),
        name="query_back",
    )(info, dq, up, rt, *blocks)


LOG2E = math.log2(math.e)


PER_STEP = 2
SMALL = 2 * RANK


def attend_kernel(l_ref, w_ref, u_ref, q_ref, mix_ref, lse_ref, kv_ref):
    wide = NOPE + VDIM
    w = w_ref[...].reshape(LATENT, PER_STEP * wide)
    both_kv = dot(l_ref[:, :LATENT], w) + dot(l_ref[:, LATENT:], u_ref[...])
    both_kv = both_kv.astype(bf16)
    kv_ref[...] = both_kv
    ones = jnp.ones((both_kv.shape[0], LANES), bf16)
    for i in range(PER_STEP):
        kv = both_kv[:, i * wide : (i + 1) * wide]
        keys = jnp.concatenate([kv[:, :NOPE], l_ref[:, LATENT:]], 1)
        values = jnp.concatenate([kv[:, NOPE:], ones], 1)
        scores = dot(q_ref[i], keys, NT)
        top = jnp.max(scores, axis=1, keepdims=True)
        weights = jnp.exp2((scores - top) * (SCALE * LOG2E)).astype(bf16)
        both = dot(weights, values)
        total = both[:, VDIM:]
        mix_ref[:, i * VDIM : (i + 1) * VDIM] = (both[:, :VDIM] / total).astype(bf16)
        lse = top * (SCALE * LOG2E) + jnp.log2(total)
        lse_ref[i] = lse.T[:8]


def folded(w_kvb, at):
    pieces, _, rows, width = w_kvb.shape
    wide = PER_STEP * (NOPE + VDIM)
    per = width // wide
    return pl.BlockSpec(
        (pieces, 1, rows, wide), lambda h, *s: (0, (at + h) // per, 0, (at + h) % per)
    )


def attend(l_all, w_kvb, u_kvb, q):
    length = l_all.shape[0]
    tokens = q.shape[1]
    wide = NOPE + VDIM
    column = lambda n, w: pl.BlockSpec((n, PER_STEP * w), lambda h: (0, h))
    head = lambda *shape: pl.BlockSpec((PER_STEP,) + shape, lambda h: (h, 0, 0))
    return pl.pallas_call(
        attend_kernel,
        grid=(HEADS // PER_STEP,),
        in_specs=[
            pl.BlockSpec((length, LW), lambda h: (0, 0)),
            folded(w_kvb, 0),
            column(LANES, wide),
            head(tokens, 2 * LANES),
        ],
        out_specs=[column(tokens, VDIM), head(8, tokens), column(length, wide)],
        out_shape=[
            jax.ShapeDtypeStruct((tokens, HEADS * VDIM), bf16),
            jax.ShapeDtypeStruct((HEADS, 8, tokens), f32),
            jax.ShapeDtypeStruct((length, HEADS * wide), bf16),
        ],
        compiler_params=params(1),
        cost_estimate=cost(HEADS * 2 * length * (LW * 256 + tokens * 512), 8e6),
        name="attend",
    )(l_all, w_kvb, u_kvb, q)


def attend_back_kernel(
    info,
    l_ref,
    lt_ref,
    w_ref,
    u_ref,
    kv_ref,
    q_ref,
    lse_ref,
    delta_ref,
    dm_ref,
    cos_ref,
    sin_ref,
    was_ref,
    dq_ref,
    dl_ref,
    du_ref,
    acc,
):
    h = pl.program_id(0)
    wide = NOPE + VDIM
    count = info.shape[0] - 1
    rows = acc.shape[0] // count
    at = lambda k: pl.ds(pl.multiple_of(info[k] * rows, rows), rows)

    @pl.when(h == 0)
    def _():
        if len(was_ref.shape) == 3:
            for k in range(count):
                acc[at(k), :] = was_ref[k].astype(f32)
        else:
            acc[...] = jnp.zeros_like(acc)

    dkvs, drope = [], 0.0
    for i in range(PER_STEP):
        kv = kv_ref[:, i * wide : (i + 1) * wide]
        keys = jnp.concatenate([kv[:, :NOPE], l_ref[:, LATENT:]], 1)
        values = kv[:, NOPE:]
        dm = dm_ref[:, i * VDIM : (i + 1) * VDIM]
        scores = dot(keys, q_ref[i], NT)
        probs = jnp.exp2(scores * (SCALE * LOG2E) - lse_ref[i, :1])
        dvalues = dot(probs.astype(bf16), dm)
        dprobs = dot(values, dm, NT)
        dscores = (probs * (dprobs - delta_ref[i, :1])).astype(bf16)
        dq = dot(dscores, keys, TN) * SCALE
        lane = lax.broadcasted_iota(jnp.int32, (dq.shape[0], LANES), 1)
        rope = dq[:, LANES:]
        rope = rope * cos_ref[...] + unrotate_pair(lane, rope) * sin_ref[...]
        dq_ref[i] = jnp.concatenate([dq[:, :LANES], rope], 1).astype(bf16)
        dkeys = dot(dscores, q_ref[i]) * SCALE
        dkvs += [dkeys[:, :NOPE].astype(bf16), dvalues.astype(bf16)]
        drope += dkeys[:, NOPE:]
    dkv = jnp.concatenate(dkvs, 1)
    w = w_ref[...].reshape(LATENT, PER_STEP * wide)
    acc[:, :LATENT] += dot(dkv, w, NT)
    acc[:, LATENT:] += dot(dkv, u_ref[...], NT) + drope
    du_ref[...] = dot(lt_ref[...], dkv)

    @pl.when(h == pl.num_programs(0) - 1)
    def _():
        for k in range(count):
            dl_ref[k] = acc[at(k), :].astype(bf16)


def attend_back(info, part, l_all, lt, w_kvb, u_kvb, kv, q, lse, delta, dmix, cos, sin, was):
    length = l_all.shape[0]
    tokens = q.shape[1]
    wide = NOPE + VDIM
    heads = HEADS // 2
    count = info.shape[0] - 1
    at = part * heads // PER_STEP
    still = lambda a: pl.BlockSpec(a.shape, lambda h, s: (0,) * a.ndim)
    column = lambda n, w: pl.BlockSpec((n, PER_STEP * w), lambda h, s: (0, at + h))
    head = lambda *shape: pl.BlockSpec((PER_STEP,) + shape, lambda h, s: (at + h, 0, 0))
    spec = pltpu.PrefetchScalarGridSpec(
        num_scalar_prefetch=1,
        grid=(heads // PER_STEP,),
        in_specs=[
            still(l_all),
            still(lt),
            folded(w_kvb, at),
            column(LANES, wide),
            column(length, wide),
            head(tokens, 2 * LANES),
            head(8, tokens),
            head(8, tokens),
            column(tokens, VDIM),
            still(cos),
            still(sin),
            still(was),
        ],
        out_specs=[
            pl.BlockSpec((PER_STEP, tokens, 2 * LANES), lambda h, s: (h, 0, 0)),
            pl.BlockSpec((count, length // count, LW), lambda h, s: (0, 0, 0)),
            pl.BlockSpec((lt.shape[0], PER_STEP * wide), lambda h, s: (0, h)),
        ],
        scratch_shapes=[pltpu.VMEM((length, LW), f32)],
    )
    return pl.pallas_call(
        attend_back_kernel,
        grid_spec=spec,
        out_shape=[
            jax.ShapeDtypeStruct((heads, tokens, 2 * LANES), bf16),
            jax.ShapeDtypeStruct((count, length // count, LW), bf16),
            jax.ShapeDtypeStruct((lt.shape[0], heads * wide), f32),
        ],
        compiler_params=params(1),
        cost_estimate=cost(heads * 2 * length * (LW * 256 + tokens * 1024), 30e6),
        name="attend_back",
    )(info, l_all, lt, w_kvb, u_kvb, kv, q, lse, delta, dmix, cos, sin, was)


def picks(slot_row, slots):
    row = lax.broadcasted_iota(jnp.int32, (slots, slot_row.shape[1]), 0)
    return jnp.where(row == slot_row, 1.0, 0.0).astype(bf16)


def silu_parts(gate):
    sig = 1.0 / (1.0 + jnp.exp(-gate))
    return gate * sig, sig * (1.0 + gate * (1.0 - sig))


def router_probs(logits, experts):
    lane = lax.broadcasted_iota(jnp.int32, logits.shape, 1)
    logits = jnp.where(lane < experts, logits, -1e30)
    odds = jnp.exp(logits - jnp.max(logits, axis=1, keepdims=True))
    return odds / jnp.sum(odds, axis=1, keepdims=True)


def routed_kernel(info, slot_ref, wr_ref, w_in, w_out, *rest, offs, slots, wide, experts):
    chunks, count = len(offs), info.shape[0] - 1
    x_refs, g_refs = rest[:chunks], rest[chunks : 2 * chunks]
    y_ref, dx_ref, pull_ref, rows, grads, hidden, dacts = rest[2 * chunks :]
    e = pl.program_id(0)
    ff = w_out.shape[1]
    weights = []
    for c in range(chunks):
        pick = picks(slot_ref[info[1 + offs[c] % count], pl.ds(e, 1), :], slots)
        at = pl.ds(c * slots, slots)
        x = dot(pick, x_refs[c][...]).astype(bf16)
        rows[at, :] = x
        weight = router_probs(dot(x, wr_ref[...]), experts)
        lane = lax.broadcasted_iota(jnp.int32, weight.shape, 1)
        weight = jnp.sum(jnp.where(lane == info[0] + e, weight, 0.0), axis=1, keepdims=True)
        weights.append(weight)
        grads[at, :] = (dot(pick, g_refs[c][...]) * weight).astype(bf16)
    weight = jnp.concatenate(weights, 0)
    for a in range(0, ff, wide):
        b = min(a + wide, ff)
        gate = dot(rows[...], w_in[0, :, a:b])
        up = dot(rows[...], w_in[0, :, ff + a : ff + b])
        dhid = dot(grads[...], w_out[0, a:b, :], NT)
        silu, slope = silu_parts(gate)
        hidden[:, a:b] = (silu * up).astype(bf16)
        dacts[:, a:b] = (dhid * up * slope).astype(bf16)
        dacts[:, ff + a : ff + b] = (dhid * silu).astype(bf16)
    pull = jnp.zeros((rows.shape[0], 1), f32)
    step = 2 * wide
    for a in range(0, D, step):
        y = dot(hidden[...], w_out[0, :, a : a + step])
        pull += jnp.sum(y * grads[:, a : a + step].astype(f32), axis=1, keepdims=True)
        y_ref[0, :, a : a + step] = (y * weight).astype(bf16)
        dx_ref[0, :, a : a + step] = dot(dacts[...], w_in[0, a : a + step, :], NT).astype(bf16)
    lane = lax.broadcasted_iota(jnp.int32, (rows.shape[0], LANES), 1)
    pull_ref[0] = jnp.where(lane == info[0] + e, pull, 0.0).astype(bf16)


def routed(info, offs, xs, gs, slot_all, w_router, experts, w_in, w_out):
    chunks, tokens = len(xs), xs[0].shape[0]
    local = w_in.shape[0]
    ff = w_out.shape[1]
    slots = tokens // 2
    rows = chunks * slots
    once = pl.Buffered(1)
    whole = lambda a: pl.BlockSpec(a.shape, lambda e, s: (0,) * a.ndim, pipeline_mode=once)
    out = pl.BlockSpec((1, rows, D), lambda e, s: (e, 0, 0))
    spec = pltpu.PrefetchScalarGridSpec(
        num_scalar_prefetch=1,
        grid=(local,),
        in_specs=[
            whole(slot_all),
            whole(w_router),
            pl.BlockSpec((1, D, 2 * ff), lambda e, s: (e, 0, 0)),
            pl.BlockSpec((1, ff, D), lambda e, s: (e, 0, 0)),
        ]
        + [whole(v) for v in (*xs, *gs)],
        out_specs=[out, out, pl.BlockSpec((1, rows, LANES), lambda e, s: (e, 0, 0))],
        scratch_shapes=[
            pltpu.VMEM((rows, D), bf16),
            pltpu.VMEM((rows, D), bf16),
            pltpu.VMEM((rows, ff), bf16),
            pltpu.VMEM((rows, 2 * ff), bf16),
        ],
    )
    shape = jax.ShapeDtypeStruct((local, rows, D), bf16)
    return pl.pallas_call(
        functools.partial(
            routed_kernel, offs=offs, slots=slots, wide=2 * LANES, experts=experts
        ),
        grid_spec=spec,
        out_shape=[shape, shape, jax.ShapeDtypeStruct((local, rows, LANES), bf16)],
        compiler_params=params(1),
        cost_estimate=cost(local * rows * D * ff * 12, local * D * ff * 6),
        name="routed",
    )(info, slot_all, w_router, w_in, w_out, *xs, *gs)


def shared_kernel(
    info,
    slot_ref,
    y_ref,
    dx_ref,
    pull_ref,
    wi_ref,
    wo_ref,
    u_ref,
    dn_ref,
    *rest,
    offs,
    slots,
    experts,
):
    chunks, count = len(offs), info.shape[0] - 1
    blocks = rest[: 2 * chunks]
    out_ref, dout_ref, gu_up_ref, gu_down_ref, dn_up_ref, dn_down_ref = rest[2 * chunks :]
    local = y_ref.shape[0]
    half = dn_ref.shape[0]
    tokens = blocks[0].shape[0]
    x = jnp.concatenate([ref[...] for ref in blocks[:chunks]], 0)
    g = jnp.concatenate([ref[...] for ref in blocks[chunks:]], 0)
    proj = dot(x, wi_ref[...])
    r = proj[:, 2 * half :].astype(bf16)
    prob = router_probs(proj[:, 2 * half :], experts)
    acts = proj[:, : 2 * half] + dot(r, u_ref[...])
    gate, up = acts[:, :half], acts[:, half:]
    silu, slope = silu_parts(gate)
    inner = (silu * up).astype(bf16)
    rdn = dot(inner, dn_ref[...]).astype(bf16)
    back = dot(g, wo_ref[...], NT)
    drdn = back[:, half:].astype(bf16)
    dinner = back[:, :half] + dot(drdn, dn_ref[...], NT)
    dboth = jnp.concatenate([dinner * up * slope, dinner * silu], 1).astype(bf16)
    dr = dot(dboth, u_ref[...], NT)

    def rows(ref, c, a, b):
        return jnp.concatenate([ref[e, c * slots : (c + 1) * slots, a:b] for e in range(local)], 0)

    chosen, pulls = [], []
    for c in range(chunks):
        owner = info[1 + offs[c] % count]
        pick = [picks(slot_ref[owner, e : e + 1, :], slots) for e in range(local)]
        chosen.append(jnp.concatenate(pick, 0))
        pulls.append(dot(chosen[c], rows(pull_ref, c, 0, LANES), TN))
    pulls = jnp.concatenate(pulls, 0)
    dlogit = pulls - prob * jnp.sum(pulls, axis=1, keepdims=True)
    both = jnp.concatenate([inner, rdn], 1)
    dall = jnp.concatenate([dboth, (dr + dlogit).astype(bf16)], 1)
    step = 4 * LANES
    for a in range(0, D, step):
        out = dot(both, wo_ref[:, a : a + step])
        dx = dot(dall, wi_ref[a : a + step, :], NT)
        for c in range(chunks):
            at = slice(c * tokens, (c + 1) * tokens)
            put = lambda ref: dot(chosen[c], rows(ref, c, a, a + step), TN)
            out_ref[c, :, a : a + step] = (out[at] + put(y_ref)).astype(bf16)
            dout_ref[c, :, a : a + step] = (dx[at] + put(dx_ref)).astype(bf16)
    few = gu_up_ref.shape[0]
    gu_up_ref[...] = dot(r, dboth, TN)[:few]
    gu_down_ref[...] = dot(dr.astype(bf16), x, TN)[:few]
    dn_up_ref[...] = dot(rdn, g, TN)[:few]
    dn_down_ref[...] = dot(drdn, inner, TN)[:few]


def shared(info, offs, xs, gs, slot_all, experts, y, dx, pull, wi, wo, u, dn):
    chunks, tokens = len(xs), xs[0].shape[0]
    slots = tokens // 2
    half = dn.shape[0]
    once = pl.Buffered(1)
    whole = lambda a: pl.BlockSpec(a.shape, lambda c, s: (0,) * a.ndim, pipeline_mode=once)
    still = lambda *shape: pl.BlockSpec(shape, lambda c, s: (0,) * len(shape))
    operands = [slot_all, y, dx, pull, wi, wo, u, dn, *xs, *gs]
    shapes = [(chunks, tokens, D)] * 2
    few = round_up(experts + RANK, RANK)
    shapes += [(few, 2 * half), (few, D), (few, D), (few, half)]
    spec = pltpu.PrefetchScalarGridSpec(
        num_scalar_prefetch=1,
        grid=(1,),
        in_specs=[whole(a) for a in operands],
        out_specs=[still(*shape) for shape in shapes],
    )
    return pl.pallas_call(
        functools.partial(shared_kernel, offs=offs, slots=slots, experts=experts),
        grid_spec=spec,
        out_shape=[
            jax.ShapeDtypeStruct(shape, bf16 if i < 2 else f32) for i, shape in enumerate(shapes)
        ],
        compiler_params=params(1),
        cost_estimate=cost(chunks * 4e9, chunks * 8e6),
        name="shared",
    )(info, *operands)


def rms_scale(v):
    return lax.rsqrt(jnp.mean(v * v, axis=-1, keepdims=True) + EPS)


def rms_back(v, scale, gain, dy):
    unit = v * scale
    gdy = gain * dy
    return (gdy - unit * jnp.mean(unit * gdy, axis=-1, keepdims=True)) * scale


def angles(positions):
    half = ROPE // 2
    ladder = jnp.arange(half).astype(f32)
    frequency = jnp.exp(ladder * (-2.0 * math.log(10000.0) / ROPE))
    turn = positions.astype(f32)[:, None] * frequency[None, :]
    return jnp.cos(turn), jnp.sin(turn)


def pad_lanes(v, width, before=0):
    return jnp.pad(v, ((0, 0), (before, width - before - v.shape[1])))


def pad_rows(v, height, before=0):
    return jnp.pad(v, ((before, height - before - v.shape[0]), (0, 0)))


def round_up(n, m):
    return -(-n // m) * m


def pack(parts, unit=LANES):
    return jnp.concatenate([pad_lanes(v, round_up(v.shape[1], unit)) for v in parts], 1)


def unpack(v, widths, unit=LANES):
    out, at = [], 0
    for w in widths:
        out.append(v[:, at : at + w])
        at += round_up(w, unit)
    return out


class Totals:
    def __init__(self, parts, shards):
        self.shards = shards
        self.widths = [v.shape[1] for v in parts]
        packed = pack(parts)
        self.columns = round_up(packed.shape[1], shards * LANES)
        packed = pad_lanes(packed, self.columns).astype(bf16)
        self.cut = self.columns // shards
        self.packed = packed.reshape(RANK, shards, self.cut).transpose(1, 0, 2)

    def deal(self):
        mine = lax.all_to_all(self.packed, "shard", split_axis=0, concat_axis=0, tiled=True)
        self.mine = jnp.sum(mine.astype(f32), axis=0).astype(bf16)
        return self.mine

    def gather(self, ids):
        seqs = lax.all_gather(self.mine, "replica", axis=0)
        chosen = (ids[None, :] == jnp.arange(ADAPTERS)[:, None]).astype(f32)
        sums = jnp.sum(chosen[:, :, None, None] * seqs.astype(f32)[None], axis=1).astype(bf16)
        self.sums = sums.reshape(self.shards, ADAPTERS // self.shards, RANK, self.cut)
        return self.sums

    def home(self):
        full = lax.all_to_all(self.sums, "shard", split_axis=0, concat_axis=0, tiled=True)
        full = full.transpose(1, 2, 0, 3).reshape(ADAPTERS // self.shards, RANK, self.columns)
        out, at = [], 0
        for w in self.widths:
            out.append(full[:, :, at : at + w].astype(f32))
            at += round_up(w, LANES)
        return out


def body(
    hidden_in,
    out_grad,
    routes,
    seq_adapter,
    attn_gain,
    latent_gain,
    ffn_gain,
    w_qa,
    w_kvb,
    w_out,
    w_router,
    w_shared_in,
    w_shared_out,
    w_expert_in,
    w_expert_out,
    qa_down,
    qa_up,
    kvb_down,
    kvb_up,
    out_down,
    out_up,
    gu_down,
    gu_up,
    dn_down,
    dn_up,
):
    shards = lax.axis_size("shard")
    replicas = lax.axis_size("replica")
    place = lax.axis_index("shard")
    tokens = hidden_in.shape[0]
    local = w_expert_in.shape[0]
    experts = local * shards
    ring = Ring(shards)
    adapter_id = seq_adapter[0]
    core = (lax.axis_index("replica") % 2).astype(jnp.int32)
    spots = jnp.concatenate([ring.owners, core.reshape(1)])
    ids = lax.all_gather(seq_adapter, "replica", axis=0, tiled=True)
    first = (place * local).astype(jnp.int32).reshape(1)

    tables = [qa_down, qa_up[:, :, :QW], qa_up[:, :, QW:], kvb_down, kvb_up, out_down, out_up]
    tables = [t[0] for t in tables + [gu_down, gu_up, dn_down, dn_up]]
    dealt = pack(tables)
    cut = round_up(dealt.shape[1], shards * LANES) // shards
    dealt = pad_lanes(dealt, cut * shards).reshape(RANK, shards, cut).transpose(1, 0, 2)
    dealt = lax.all_to_all(dealt, "shard", split_axis=0, concat_axis=0, tiled=True)
    dealt = lax.dynamic_index_in_dim(dealt, adapter_id, 0, keepdims=True)
    dealt = jnp.broadcast_to(dealt, (shards, RANK, cut))
    dealt = lax.all_to_all(dealt, "shard", split_axis=0, concat_axis=0, tiled=True)
    dealt = dealt.transpose(1, 0, 2).reshape(RANK, shards * cut)
    a_qd, a_quq, a_qul, a_kd, a_ku, a_od, a_ou, a_gd, a_gu, a_nd, a_nu = unpack(
        dealt, [t.shape[1] for t in tables]
    )

    kvb_rows, fold, kvb_wide, own_weights = pack_weights(core, w_qa, w_kvb, w_out, replicas)
    w_walk = Walk(ring, own_weights)
    w_swaps = Swaps(ring, w_walk, replicas)
    w1 = w_walk.hop()
    own_swap = w_swaps.swap(w_walk.own)
    w2 = w_walk.hop(*own_swap)
    width = w_shared_out.shape[0]
    half = round_up(width, LANES)
    rows_in = w_shared_in.shape[0]
    if replicas % 2 == 0:
        core = lax.axis_index("replica") % 2
    mine = own_share(w_shared_in, replicas, zero_after(*w1))
    mine = mine.reshape(mine.shape[0], 2, shards, width).transpose(2, 0, 1, 3)
    mine = jnp.pad(mine, ((0, 0), (0, 0), (0, 0), (0, half - width)))
    mine = mine.reshape(shards, mine.shape[1], 2 * half)
    ready = mine
    inputs = hidden_in.astype(f32)
    in_scale = rms_scale(inputs)
    hb = (inputs * in_scale * attn_gain).astype(bf16)
    swap1 = w_swaps.swap(w_walk.pairs[0])
    w3 = w_walk.hop(*swap1, ready[0, :16], hb[:16])
    swap2 = w_swaps.swap(w_walk.pairs[1])
    w4 = w_walk.hop(*swap2, ids)
    u_q = pad_rows(a_quq, LANES)
    u_kvb = pad_rows(a_ku, LANES, ROPE)
    wr = pad_lanes(w_router, LANES)
    r_qa = dot(hb, a_qd, NT).astype(bf16)
    w_swaps.swap(w_walk.pairs[2])
    w_swaps.swap(w_walk.halves)
    w_at, w_blocks = w_swaps.rows(0, w_out.shape[0])
    kvb_at, out_at, lat_at = QW, QW + kvb_wide, QW + kvb_wide + D
    w_lat = place_rows(spots, w_at, w_blocks, D, lat_at, LW, LANES)[:, : LATENT + ROPE]
    full_kvb = place_rows(spots, w_at, w_blocks, D, kvb_at, kvb_wide, kvb_wide)
    full_kvb = full_kvb.reshape(LATENT // kvb_rows, fold, kvb_rows, kvb_wide)
    full_out = place_rows(spots, w_at, w_blocks, D, out_at, D, D // 2)

    lat_raw = dot(hb, w_lat) + dot(r_qa, a_qul)
    latent_raw, rope_raw = lat_raw[:, :LATENT], lat_raw[:, LATENT:]
    lat_scale = rms_scale(latent_raw)
    latent = (latent_raw * lat_scale * latent_gain).astype(bf16)
    positions = place * tokens + jnp.arange(tokens)
    cos_half, sin_half = angles(positions)
    rh = ROPE // 2
    rope_a, rope_b = rope_raw[:, :rh], rope_raw[:, rh:]
    rope = jnp.concatenate(
        [rope_a * cos_half - rope_b * sin_half, rope_b * cos_half + rope_a * sin_half], 1
    ).astype(bf16)
    r_kv = dot(latent, a_kd, NT).astype(bf16)
    l_own = jnp.concatenate([latent, rope, r_kv, routes.astype(bf16)], 1)
    l_own = pad_lanes(l_own, LW)
    l_walk = Walk(ring, l_own)
    l_walk.hop()
    l_walk.hop(full_out)
    l3 = l_walk.hop(full_kvb)
    l4 = l_walk.hop(u_q, u_kvb)
    (hb_late,) = gate((hb,), l3)
    g_walk = Walk(ring, out_grad)
    g1 = g_walk.hop(*l4)
    (mine,) = gate((ready,), l4)
    mine = lax.all_to_all(mine, "shard", split_axis=0, concat_axis=0, tiled=True)
    if replicas % 2 == 0:
        other = pair_swap(mine, replicas)
        w_si = jnp.concatenate(
            [jnp.where(core == 0, mine, other), jnp.where(core == 0, other, mine)], 1
        )
    else:
        w_si = mine
    w_si = w_si.reshape(shards * rows_in, 2 * half)

    w_i = jnp.concatenate([w_si, pad_lanes(jnp.concatenate([w_router, a_gd.T], 1), LANES)], 1)
    w_o = jnp.concatenate([pad_rows(w_shared_out, half), pad_rows(a_nu, LANES)], 0)
    gu_g = lax.dynamic_slice_in_dim(a_gu, place * width, width, 1)
    gu_u = lax.dynamic_slice_in_dim(a_gu, shards * width + place * width, width, 1)
    u_gu = jnp.concatenate([pad_lanes(gu_g, half), pad_lanes(gu_u, half)], 1)
    u_gu = pad_rows(u_gu, LANES, experts)
    nd_own = lax.dynamic_slice_in_dim(a_nd, place * width, width, 1)
    dn_own = pad_rows(pad_lanes(nd_own.T, LANES), half)

    l_all = all_latents(spots, l_walk.blocks(), tokens)
    cos = pad_lanes(jnp.concatenate([cos_half, cos_half], 1), LANES)
    sin = pad_lanes(jnp.concatenate([sin_half, sin_half], 1), LANES)
    q = query_heads(
        spots, hb_late, pad_lanes(r_qa, LANES), w_at, w_blocks, u_q, cos, sin
    )

    mixture, lse, kv = attend(l_all, full_kvb, u_kvb, q)
    (mixture,) = gate((mixture,), g1)
    r_out = dot(mixture, a_od, NT).astype(bf16)
    after_attn = inputs + dot(mixture, full_out) + dot(r_out, a_ou)
    ffn_scale = rms_scale(after_attn)
    ffn_low = (after_attn * ffn_scale * ffn_gain).astype(bf16)

    at = LATENT + ROPE + RANK
    routes_all = l_all[:, at : at + TOPK].astype(jnp.int32).reshape(shards, tokens, TOPK)
    wanted = first[0] + jnp.arange(local)
    mask = jnp.any(routes_all[:, None, :, :] == wanted[None, :, None, None], axis=-1)
    before = jnp.triu(jnp.ones((tokens, tokens), bf16), 1)
    rank = lax.dot_general(
        mask.astype(bf16), before, (((2,), (0,)), ((), ())), preferred_element_type=f32
    )
    slot_all = jnp.where(mask, rank.astype(jnp.int32), -1)

    out_piece, dx_piece, small = {}, {}, []


    info = jnp.concatenate([first, ring.owners])

    def run_routed(members, *after):
        offs, xs, gs = ([m[i] for m in members] for i in range(3))
        if after:
            xs = gate(xs, after)
        return offs, xs, gs, *routed(
            info, offs, xs, gs, slot_all, wr, experts, w_expert_in, w_expert_out
        )

    def run_shared(offs, xs, gs, y, dxr, pull):
        out, dx, *grads = shared(
            info, offs, xs, gs, slot_all, experts, y, dxr, pull, w_i, w_o, u_gu, dn_own
        )
        small.append(grads)
        for i, off in enumerate(offs):
            out_piece[off], dx_piece[off] = out[i], dx[i]
        return grads[-1]

    far = shards // 2
    walk = Walk(ring, ffn_low)
    members = lambda h: [
        (off, x, g) for off, x, g in zip((-h, h), walk.pairs[h - 1], g_walk.pairs[h - 1])
    ]
    x1 = walk.hop()
    done = run_routed([(0, ffn_low, out_grad)])
    walk.hop(done[3])
    g_walk.hop(*x1)
    mark = run_shared(*done)
    done = run_routed(members(1), mark)
    x3 = walk.hop(done[3])
    g_walk.hop(*walk.pairs[1])
    mark = run_shared(*done)
    done = run_routed(members(2), mark)
    walk.hop(done[3])
    g_walk.hop(*walk.pairs[2])
    mark = run_shared(*done)
    opposite = (far, jnp.concatenate(walk.halves, 0), jnp.concatenate(g_walk.halves, 0))
    run_shared(*run_routed(members(3) + [opposite], mark))
    out_piece[-far], dx_piece[-far] = out_piece[far], dx_piece[far]
    small = [sum(parts[1:], parts[0]) for parts in zip(*small)]

    def spread(v, cols):
        return jnp.concatenate(
            [
                lax.dynamic_update_slice_in_dim(
                    jnp.zeros((RANK, cols), f32), part, place * width, 1
                )
                for part in v
            ],
            1,
        )

    g_gu_up = small[0][experts : experts + RANK]
    g_gu_up = spread([g_gu_up[:, :width], g_gu_up[:, half : half + width]], shards * width)
    g_gu_down = small[1][experts : experts + RANK]
    g_dn_up = small[2][:RANK]
    g_dn_down = spread([small[3][:RANK, :width]], shards * width)

    seen = {}
    ffn_grad = ring.scatter_sum(lambda off: dx_piece[off], {})

    d_after = out_grad.astype(f32) + rms_back(after_attn, ffn_scale, ffn_gain, ffn_grad)
    d_after_low = d_after.astype(bf16)
    dr_out = dot(d_after_low, a_ou, NT).astype(bf16)
    dmix = (dot(d_after_low, full_out, NT) + dot(dr_out, a_od)).astype(bf16)
    g_out_up = dot(r_out, d_after_low, TN)
    g_out_down = dot(dr_out, mixture, TN)
    delta = (dmix.astype(f32) * mixture.astype(f32)).reshape(tokens, HEADS, VDIM).sum(-1).T
    delta = jnp.broadcast_to(delta[:, None, :], (HEADS, 8, tokens))
    lt = l_all[:, LATENT + ROPE : LATENT + ROPE + SMALL].T
    parts = []

    def back(*marks):
        was = parts[-1][1] if parts else jnp.zeros((8, LANES), bf16)
        (marked,) = gate((lse,), marks) if not parts else gate((lse + 0.0,), marks)
        parts.append(
            attend_back(
                spots, len(parts), l_all, lt, full_kvb, u_kvb, kv, q, marked, delta, dmix, cos, sin, was
            )
        )
        return (parts[-1][2],)

    def first_arrived(r, l):
        seen["far"] = (r[:16], l[:16])
        return ()

    def next_arrived(r, l):
        seen["next"] = (r[:16], l[:16])
        return back(*seen["far"])

    def last_arrived(r, l):
        back(*seen["next"])
        dl = parts[-1][1]
        seen["dl"] = ring.scatter_sum(
            lambda off: dl[off % shards],
            {far - 2: query_grads, far - 3: dl_arrived},
        )
        return seen["dl near"]

    def query_grads(r, l):
        dq = jnp.concatenate([part[0] for part in parts], 0)
        seen["q"] = query_back(spots, dq, w_at, w_blocks, u_q, pad_lanes(r_qa, SMALL).T)
        return (seen["q"][1],)

    def dl_arrived(r, l):
        seen["dl near"] = (r[:16], l[:16])
        return ()

    out_sum = ring.scatter_sum(
        lambda off: out_piece[off],
        {
            far: lambda: (ffn_grad,),
            far - 1: first_arrived,
            far - 2: next_arrived,
            far - 3: last_arrived,
        },
    )
    block_out = (after_attn + out_sum).astype(bf16)
    g_ku = jnp.concatenate([part[2] for part in parts], 1)
    g_kvb_up = g_ku[:RANK]
    dhb_q, dr_q, g_qu = seen["q"]
    dl_own = seen["dl"]
    dr_kv = dl_own[:, LATENT + ROPE : LATENT + ROPE + RANK].astype(bf16)
    d_latent = dl_own[:, :LATENT] + dot(dr_kv, a_kd)
    g_kvb_down = dot(dr_kv, latent, TN)
    d_latent = rms_back(latent_raw, lat_scale, latent_gain, d_latent)
    drope = dl_own[:, LATENT : LATENT + ROPE]
    drope_a, drope_b = drope[:, :rh], drope[:, rh:]
    drope = jnp.concatenate(
        [drope_a * cos_half + drope_b * sin_half, drope_b * cos_half - drope_a * sin_half], 1
    )
    d_lat = jnp.concatenate([d_latent, drope], 1).astype(bf16)
    dr_qa = (dr_q[:, :RANK] + dot(d_lat, a_qul, NT)).astype(bf16)
    dhb = dhb_q + dot(d_lat, w_lat, NT) + dot(dr_qa, a_qd)
    g_qa_up = jnp.concatenate([g_qu[:RANK], dot(r_qa, d_lat, TN)], 1)
    g_qa_down = dot(dr_qa, hb, TN)
    hidden_grad = d_after + rms_back(inputs, in_scale, attn_gain, dhb)

    t_attn = Totals(
        [g_qa_down, g_qa_up, g_kvb_down, g_kvb_up, g_out_down, g_out_up]
        + [g_gu_down, g_gu_up, g_dn_down, g_dn_up],
        shards,
    )
    t_attn.deal()
    t_attn.gather(ids)
    return (block_out, hidden_grad, *t_attn.home())


def solution(mesh):
    rows = P(("replica", "shard"), None)
    cut2 = P("shard", None)
    cut3 = P("shard", None, None)
    in_specs = (
        (rows, rows, rows, P("replica"), P(), P(), P())
        + (cut2, cut2, cut2, P(), cut2, cut2, cut3, cut3)
        + (cut3,) * 10
    )
    out_specs = (rows, rows) + (cut3,) * 10
    return jax.shard_map(body, mesh=mesh, in_specs=in_specs, out_specs=out_specs, check_vma=False)
```
